32 devices in a mesh: dp: 8 (over y, x, core), tensor: 4 (over z).
Axes of the slice: x: 2, y: 2, z: 4, core: 2. Of those that a mesh axis runs over, the one named last changes fastest.
Arguments:
- inputs: bfloat16 [8192, 2048], P(('dp', 'tensor')), may hold values from -6 to 6
- cotangent: bfloat16 [8192, 2048], P(('dp', 'tensor')), may hold values from -6 to 6
- doc_lengths: int32 [8, 3], P('dp'), may hold values from 1 to 896, 1024 in all within a row
- norm_gains: float32 [2, 2048], replicated, may hold values from 0.5 to 1.5
- attn_weight: float32 [4, 2048, 2048], P(None, 'dp', 'tensor'), may hold values from -0.26516504 to 0.26516504
- mlp_weight: float32 [3, 2048, 8192], P(None, 'dp', 'tensor'), may hold values from -0.125 to 0.125
- gain_first: float32 [2, 2048], replicated, may hold values from -80 to 80
- attn_first: float32 [4, 2048, 2048], P(None, 'dp', 'tensor'), may hold values from -28 to 28
- mlp_first: float32 [3, 2048, 8192], P(None, 'dp', 'tensor'), may hold values from -32 to 32
- gain_second: float32 [2, 2048], replicated, may hold values from 737.28 to 2949.12
- attn_second: float32 [4, 2048, 2048], P(None, 'dp', 'tensor'), may hold values from 90.112 to 360.448
- mlp_second: float32 [3, 2048, 8192], P(None, 'dp', 'tensor'), may hold values from 131.072 to 524.288
Outputs:
- layer_out: bfloat16 [8192, 2048], P(('dp', 'tensor'))
- grad_in: float32 [8192, 2048], P(('dp', 'tensor'))
- gain_grad: float32 [2, 2048], replicated
- attn_grad: float32 [4, 2048, 2048], P(None, 'dp', 'tensor')
- mlp_grad: float32 [3, 2048, 8192], P(None, 'dp', 'tensor')
- gain_first_new: float32 [2, 2048], replicated
- attn_first_new: float32 [4, 2048, 2048], P(None, 'dp', 'tensor')
- mlp_first_new: float32 [3, 2048, 8192], P(None, 'dp', 'tensor')
- gain_second_new: float32 [2, 2048], replicated
- attn_second_new: float32 [4, 2048, 2048], P(None, 'dp', 'tensor')
- mlp_second_new: float32 [3, 2048, 8192], P(None, 'dp', 'tensor')
- gain_new: float32 [2, 2048], replicated
- attn_new: float32 [4, 2048, 2048], P(None, 'dp', 'tensor')
- mlp_new: float32 [3, 2048, 8192], P(None, 'dp', 'tensor')
The draws below stay inside these ranges and needn't reach their ends.
Inputs may be any that keep to these rules, and one draw needn't show every extreme that they name: `doc_lengths`: each row sums to 1024, and its longest document has exactly 896 tokens.
All inputs are finite; a program needn't handle non-finite values.
Results may differ from the reference program's by a relative error of at most 0.015.
Values may be sent and summed in bfloat16 or wider, within the bound.
A program may use at most 320 MiB of HBM per device.

```python
import math
import jax
import jax.numpy as jnp
import numpy as np
from jax import lax

D = 2048
FF = 8192
HEAD_DIM = 64
DOCS = 3
STEP = 10
SEQS = 8
SEQ_LEN = 1024
TOKENS = 8192
LONGEST = 896


def draw_attn_weight(key, part):
    key = jax.random.fold_in(key, 5)
    factor = jnp.array([1.0, 1.0, 1.0, 8.0 ** 0.5], jnp.float32).reshape(4, 1, 1) * D ** (-0.5)
    base = jax.random.truncated_normal(key, -4.0, 4.0, (4, D, D), jnp.float32)
    return base * factor


def shard_levels(rng, dims, shards, smallest, top_value):
    factor_of, own = 1.0, jax.random.fold_in(rng, 6)
    for dim, parts in shards:
        steps = jnp.exp(jax.random.uniform(jax.random.fold_in(own, dim), (parts,), jnp.float32, smallest / len(shards), top_value / len(shards)))
        factor_of = factor_of * jnp.repeat(steps, dims[dim] // parts).reshape([-1 if axis == dim else 1 for axis in range(len(dims))])
    return factor_of


def length_profile(count, total, limit, lean):
    portions = [(1 << 20) // math.isqrt(standing ** lean) + 1 for standing in range(2, count + 1)]
    surplus, given = total - limit - (count - 1), [1] * (count - 1)
    while surplus > 0:
        candidates = [i for i in range(count - 1) if given[i] < limit]
        whole, budget = sum([portions[i] for i in candidates]), surplus
        for i in candidates:
            more = min(limit - given[i], max(1, budget * portions[i] // whole), surplus)
            given[i] = given[i] + more
            surplus = surplus - more
    return np.array([limit] + given)


def uneven(rng, amount, total, reach, skew):
    if amount == 2:
        one = jax.random.randint(rng, (), max(1, total - reach), min(reach, total - 1) + 1)
        return jnp.stack([one, total - one])
    sizes = jnp.asarray(length_profile(amount, total, reach, skew), jnp.int32)
    couples = (amount - 1) // 2
    donor, taker = sizes[1:1 + 2 * couples:2], sizes[2:2 + 2 * couples:2]
    margin = jnp.minimum(donor - 1, reach - taker)
    passed = jax.random.randint(jax.random.fold_in(rng, 1), (couples,), 0, 1 << 20) % (margin + 1)
    sizes = sizes.at[1:1 + 2 * couples:2].set(donor - passed).at[2:2 + 2 * couples:2].set(taker + passed)
    return sizes[jax.random.permutation(jax.random.fold_in(rng, 2), amount)]


def bell_draw(stream_key, extent, deviation, most, shards=(), kind=jnp.bfloat16):
    gain = shard_levels(stream_key, extent, shards, -0.22, 0.18) if shards else 1.0
    values = jax.random.normal(stream_key, extent, jnp.float32) * deviation * gain
    return jnp.minimum(jnp.maximum(values, -most), most).astype(kind)


def setup_inputs(seed: int = 0) -> dict:
    seeds = jax.random.split(jax.random.key(seed), 13)
    inputs = bell_draw(seeds[0], (TOKENS, D), 1.0, 6.0, ((0, 32),))
    cotangent = bell_draw(seeds[1], (TOKENS, D), 1.0, 6.0, ((0, 32),))
    doc_lengths = jax.vmap(lambda own: uneven(own, DOCS, SEQ_LEN, LONGEST, 0))(jax.random.split(seeds[2], SEQS)).reshape((SEQS, DOCS)).astype(jnp.int32)
    norm_gains = jnp.clip(1.0 + 0.1 * jax.random.normal(seeds[3], (2, D), jnp.float32), 0.5, 1.5)
    attn_weight = draw_attn_weight(jax.random.fold_in(seeds[12], 71), 0)
    mlp_weight = bell_draw(seeds[5], (3, D, FF), D ** -0.5, 0.125, ((1, 8), (2, 4)), jnp.float32)
    gain_first = bell_draw(seeds[6], (2, D), (0.14 * TOKENS ** 0.5), 80.0, (), jnp.float32)
    attn_first = bell_draw(seeds[7], (4, D, D), (0.05 * TOKENS ** 0.5), 28.0, ((1, 8), (2, 4)), jnp.float32)
    mlp_first = bell_draw(seeds[8], (3, D, FF), (0.06 * TOKENS ** 0.5), 32.0, ((1, 8), (2, 4)), jnp.float32)
    gain_second = jnp.clip(jnp.exp(jax.random.uniform(seeds[9], (2, D), jnp.float32, math.log(737.28), math.log(2949.12))), 737.28, 2949.12)
    attn_second = jnp.clip(jnp.exp(math.log(360.448) - 1.3862944 * jax.random.uniform(seeds[10], (4, D, D), jnp.float32) ** shard_levels(seeds[10], (4, D, D), ((1, 8), (2, 4)), -0.2, 0.2)), 90.112, 360.448)
    mlp_second = jnp.clip(jnp.exp(math.log(524.288) - 1.3862944 * jax.random.uniform(seeds[11], (3, D, FF), jnp.float32) ** shard_levels(seeds[11], (3, D, FF), ((1, 8), (2, 4)), -0.2, 0.2)), 131.072, 524.288)
    return dict(inputs=inputs, cotangent=cotangent, doc_lengths=doc_lengths, norm_gains=norm_gains, attn_weight=attn_weight, mlp_weight=mlp_weight, gain_first=gain_first, attn_first=attn_first, mlp_first=mlp_first, gain_second=gain_second, attn_second=attn_second, mlp_second=mlp_second)


PRECISE = lax.Precision.HIGHEST
EPS_NORM = 1e-05
ROPE_BASE = 130000.0
BETA_ONE = 0.9
BETA_TWO = 0.95
EPS_ADAM = 1e-08
WEIGHT_DECAY = 0.1
GAIN_RATE = 0.3
MASKED = -1e+30

@jax.custom_vjp
def low(v):
    return lax.optimization_barrier(v.astype(jnp.bfloat16)).astype(jnp.float32)

@jax.custom_vjp
def low_back(v):
    return v

def low_keep(v):
    return (low(v), None)

def low_pass(kept, grad):
    return (grad,)

def back_keep(v):
    return (v, None)

def back_low(kept, grad):
    return (low(grad),)
low.defvjp(low_keep, low_pass)
low_back.defvjp(back_keep, back_low)

def norm_apply(field, gain_row):
    return field * lax.rsqrt(lax.optimization_barrier(jnp.mean(field * field, axis=-1, keepdims=True)) + EPS_NORM) * gain_row

def doc_layout(lengths, seq_length):
    doc_ends = jnp.cumsum(lengths).astype(jnp.int32)
    starts = (doc_ends - lengths).astype(jnp.int32)
    places = jnp.arange(seq_length, dtype=jnp.int32)
    segment = lax.optimization_barrier(jnp.sum((places[:, None] >= doc_ends[None, :]).astype(jnp.int32), axis=1)).astype(jnp.int32)
    owners = segment[:, None] == jnp.arange(lengths.shape[0], dtype=jnp.int32)[None, :]
    position = places - lax.optimization_barrier(jnp.sum(jnp.where(owners, starts[None, :], 0), axis=1)).astype(jnp.int32)
    return (segment, position)

def rope_tables(position):
    half_dim = HEAD_DIM // 2
    frequencies = jnp.power(jnp.float32(ROPE_BASE), -2.0 * jnp.arange(half_dim, dtype=jnp.float32) / HEAD_DIM)
    angles = position.astype(jnp.float32)[:, None] * frequencies[None, :]
    return (jnp.cos(angles)[:, None, :], jnp.sin(angles)[:, None, :])

def rotate(field, cos_table, sine_table):
    half_dim = field.shape[-1] // 2
    first_half = field[..., :half_dim]
    second_half = field[..., half_dim:]
    return jnp.concatenate([first_half * cos_table - second_half * sine_table, second_half * cos_table + first_half * sine_table], axis=-1)

def attend_block(query_block, seg_rows, pos_rows, key_rows, values, segment, position):
    raw_score = low_back(jnp.einsum('bhd,khd->hbk', query_block, key_rows, precision=PRECISE) * HEAD_DIM ** (-0.5))
    allowed = (seg_rows[:, None] == segment[None, :]) & (position[None, :] <= pos_rows[:, None])
    masked_score = jnp.where(allowed[None], raw_score, MASKED)
    row_peak = lax.optimization_barrier(jnp.max(masked_score, axis=-1, keepdims=True))
    exp_score = jnp.exp(masked_score - row_peak)
    prob_low = low(exp_score / lax.optimization_barrier(jnp.sum(exp_score, axis=-1, keepdims=True)))
    return jnp.einsum('hbk,khd->bhd', prob_low, values, precision=PRECISE)

def attention(queries, key_rows, values, segment, position):
    seq_length = queries.shape[0]
    block_rows = min(512, seq_length)
    block_count = seq_length // block_rows
    head_count = queries.shape[1]
    query_blocks = queries.reshape(block_count, block_rows, head_count, HEAD_DIM)
    seg_blocks = segment.reshape(block_count, block_rows)
    pos_blocks = position.reshape(block_count, block_rows)

    def one_block(pieces):
        return attend_block(pieces[0], pieces[1], pieces[2], key_rows, values, segment, position)
    result = lax.map(jax.checkpoint(one_block), (query_blocks, seg_blocks, pos_blocks))
    return result.reshape(seq_length, head_count, HEAD_DIM)

def block_forward(layer_in, attn_mats, mlp_mats, gain_vals, segment, position, cos_table, sine_table):
    seq_length = layer_in.shape[0]
    head_count = D // HEAD_DIM
    attn_low = low(attn_mats)
    mlp_low = low(mlp_mats)
    first_in = low(norm_apply(layer_in, gain_vals[0]))

    def project(matrix):
        return low_back(jnp.dot(first_in, matrix, precision=PRECISE)).reshape(seq_length, head_count, HEAD_DIM)
    queries = low(rotate(project(attn_low[0]), cos_table, sine_table))
    key_rows = low(rotate(project(attn_low[1]), cos_table, sine_table))
    values = low(project(attn_low[2]))
    attended = low_back(low(attention(queries, key_rows, values, segment, position))).reshape(seq_length, D)
    middle = layer_in + low_back(jnp.dot(attended, attn_low[3].T, precision=PRECISE))
    second_in = low(norm_apply(middle, gain_vals[1]))
    gate_proj = low_back(jnp.dot(second_in, mlp_low[0], precision=PRECISE))
    up_proj = low_back(jnp.dot(second_in, mlp_low[1], precision=PRECISE))
    hidden = low(jax.nn.silu(gate_proj) * up_proj)
    return middle + low_back(jnp.dot(hidden, mlp_low[2].T, precision=PRECISE))

def attn_rates():
    return jnp.array([1.0, 1.0, 1.0, 8.0 ** 0.5], jnp.float32).reshape(4, 1, 1) * (0.5 * D ** (-0.5))

def adam_update(weight, gradient, moment_one, moment_two, step_rate):
    first_new = BETA_ONE * moment_one + (1.0 - BETA_ONE) * gradient
    second_new = BETA_TWO * moment_two + (1.0 - BETA_TWO) * gradient * gradient
    fix_one = 1.0 - BETA_ONE ** STEP
    fix_two = 1.0 - BETA_TWO ** STEP
    weight_new = weight - step_rate * (first_new / fix_one / (jnp.sqrt(second_new / fix_two) + EPS_ADAM) + WEIGHT_DECAY * weight)
    return (first_new, second_new, weight_new)

def reference(inputs, cotangent, doc_lengths, norm_gains, attn_weight, mlp_weight, gain_first, attn_first, mlp_first, gain_second, attn_second, mlp_second):
    seq_inputs = inputs.astype(jnp.float32).reshape(SEQS, SEQ_LEN, D)
    seq_cotangent = cotangent.astype(jnp.float32).reshape(SEQS, SEQ_LEN, D)

    def one_sequence(totals, pieces):
        seq_rows, seq_grads, lengths = pieces
        segment, position = doc_layout(lengths, SEQ_LEN)
        cos_table, sine_table = rope_tables(position)

        def forward(layer_in, attn_mats, mlp_mats, gain_vals):
            return block_forward(layer_in, attn_mats, mlp_mats, gain_vals, segment, position, cos_table, sine_table)
        seq_out, pullback = jax.vjp(forward, seq_rows, attn_weight, mlp_weight, norm_gains)
        seq_in_grad, grad_attn, grad_mlp, grad_gain = pullback(seq_grads)
        totals = (totals[0] + grad_attn, totals[1] + grad_mlp, totals[2] + grad_gain)
        return (totals, (seq_out, seq_in_grad))
    zeros_init = (jnp.zeros(attn_weight.shape, jnp.float32), jnp.zeros(mlp_weight.shape, jnp.float32), jnp.zeros(norm_gains.shape, jnp.float32))
    sums, stacked = lax.scan(one_sequence, zeros_init, (seq_inputs, seq_cotangent, doc_lengths))
    attn_grad, mlp_grad, gain_grad = sums
    layer_out, grad_in = stacked
    gain_first_new, gain_second_new, gain_new = adam_update(norm_gains, gain_grad, gain_first, gain_second, GAIN_RATE)
    attn_first_new, attn_second_new, attn_new = adam_update(attn_weight, attn_grad, attn_first, attn_second, attn_rates())
    mlp_first_new, mlp_second_new, mlp_new = adam_update(mlp_weight, mlp_grad, mlp_first, mlp_second, 0.5 * D ** (-0.5))
    return (layer_out.reshape(TOKENS, D).astype(jnp.bfloat16), grad_in.reshape(TOKENS, D), gain_grad, attn_grad, mlp_grad, gain_first_new, attn_first_new, mlp_first_new, gain_second_new, attn_second_new, mlp_second_new, gain_new, attn_new, mlp_new)
```

```python
import jax
import jax.numpy as jnp
from jax import lax
from jax.sharding import PartitionSpec as P

D = 2048
HEAD_DIM = 64
STEP = 10


EPS_NORM = 1e-05
ROPE_BASE = 130000.0
BETA_ONE = 0.9
BETA_TWO = 0.95
EPS_ADAM = 1e-08
WEIGHT_DECAY = 0.1
GAIN_RATE = 0.3
MASKED = -1e30


def doc_layout(lengths, seq_length):
    doc_ends = jnp.cumsum(lengths)
    starts = doc_ends - lengths
    places = jnp.arange(seq_length, dtype=jnp.int32)
    segment = jnp.sum((places[:, None] >= doc_ends[None, :]).astype(jnp.int32), axis=1)
    owners = segment[:, None] == jnp.arange(lengths.shape[0], dtype=jnp.int32)[None, :]
    position = places - jnp.sum(jnp.where(owners, starts[None, :], 0), axis=1)
    return (segment, position)


def rope_tables(position):
    half_dim = HEAD_DIM // 2
    frequencies = jnp.power(
        jnp.float32(ROPE_BASE), -2.0 * jnp.arange(half_dim, dtype=jnp.float32) / HEAD_DIM
    )
    angles = position.astype(jnp.float32)[:, None] * frequencies[None, :]
    return (jnp.cos(angles)[:, None, :], jnp.sin(angles)[:, None, :])


def rotate(field, cos_table, sine_table):
    half_dim = field.shape[-1] // 2
    first_half = field[..., :half_dim]
    second_half = field[..., half_dim:]
    return jnp.concatenate(
        [
            first_half * cos_table - second_half * sine_table,
            second_half * cos_table + first_half * sine_table,
        ],
        axis=-1,
    )


def rotate_back(gradient, cos_table, sine_table):
    half_dim = gradient.shape[-1] // 2
    first_half = gradient[..., :half_dim]
    second_half = gradient[..., half_dim:]
    return jnp.concatenate(
        [
            first_half * cos_table + second_half * sine_table,
            second_half * cos_table - first_half * sine_table,
        ],
        axis=-1,
    )


def norm_forward(field):
    inv_scale = lax.rsqrt(jnp.mean(field * field, axis=-1, keepdims=True) + EPS_NORM)
    return (field * inv_scale, inv_scale)


def norm_backward(gradient, normed, inv_scale, gain_row):
    scaled = gradient * gain_row
    field_grad = inv_scale * (scaled - normed * jnp.mean(scaled * normed, axis=-1, keepdims=True))
    return (field_grad, jnp.sum(gradient * normed, axis=0))


def dot_transposed(left, right):
    return lax.dot_general(
        left, right, (((1,), (1,)), ((), ())), preferred_element_type=jnp.float32
    )


def dot_over_rows(left, right):
    return lax.dot_general(
        left, right, (((0,), (0,)), ((), ())), preferred_element_type=jnp.float32
    )


def allowed_keys(seg_rows, pos_rows, segment, position):
    return (seg_rows[:, None] == segment[None, :]) & (position[None, :] <= pos_rows[:, None])


def attend_forward(
    query_block, seg_rows, pos_rows, key_rows, values, segment, position, score_scale
):
    raw_score = (
        jnp.einsum("bhd,khd->hbk", query_block, key_rows, preferred_element_type=jnp.float32)
        * score_scale
    )
    allowed = allowed_keys(seg_rows, pos_rows, segment, position)
    masked_score = jnp.where(allowed[None], raw_score, MASKED)
    row_peak = jnp.max(masked_score, axis=-1, keepdims=True)
    exp_score = jnp.exp(masked_score - row_peak)
    exp_total = jnp.sum(exp_score, axis=-1, keepdims=True)
    prob_low = (exp_score / exp_total).astype(jnp.bfloat16)
    result = jnp.einsum(
        "hbk,khd->bhd", prob_low, values, preferred_element_type=jnp.float32
    ).astype(jnp.bfloat16)
    return (result, (row_peak + jnp.log(exp_total))[..., 0])


def attend_backward(carry_sums, pieces, key_rows, values, segment, position, score_scale):
    key_sum, value_sum = carry_sums
    query_block, grad_block, log_total, seg_rows, pos_rows = pieces
    raw_score = (
        jnp.einsum("bhd,khd->hbk", query_block, key_rows, preferred_element_type=jnp.float32)
        * score_scale
    )
    allowed = allowed_keys(seg_rows, pos_rows, segment, position)
    probs = jnp.where(allowed[None], jnp.exp(raw_score - log_total[:, :, None]), 0.0)
    value_sum = value_sum + jnp.einsum(
        "hbk,bhd->khd", probs.astype(jnp.bfloat16), grad_block, preferred_element_type=jnp.float32
    )
    prob_grad = jnp.einsum("bhd,khd->hbk", grad_block, values, preferred_element_type=jnp.float32)
    score_grad = (probs * (prob_grad - jnp.sum(prob_grad * probs, axis=-1, keepdims=True))).astype(
        jnp.bfloat16
    )
    query_grad = (
        jnp.einsum("hbk,khd->bhd", score_grad, key_rows, preferred_element_type=jnp.float32)
        * score_scale
    )
    key_sum = (
        key_sum
        + jnp.einsum("hbk,bhd->khd", score_grad, query_block, preferred_element_type=jnp.float32)
        * score_scale
    )
    return ((key_sum, value_sum), query_grad)


def attn_rates():
    return jnp.array([1.0, 1.0, 1.0, 8.0**0.5], jnp.float32).reshape(4, 1, 1) * (0.5 * D ** (-0.5))


def adam_update(weight, gradient, moment_one, moment_two, step_rate):
    first_new = BETA_ONE * moment_one + (1.0 - BETA_ONE) * gradient
    second_new = BETA_TWO * moment_two + (1.0 - BETA_TWO) * gradient * gradient
    fix_one = 1.0 - BETA_ONE**STEP
    fix_two = 1.0 - BETA_TWO**STEP
    weight_new = weight - step_rate * (
        first_new / fix_one / (jnp.sqrt(second_new / fix_two) + EPS_ADAM) + WEIGHT_DECAY * weight
    )
    return (first_new, second_new, weight_new)


def local(
    inputs,
    cotangent,
    doc_lengths,
    norm_gains,
    attn_weight,
    mlp_weight,
    gain_first,
    attn_first,
    mlp_first,
    gain_second,
    attn_second,
    mlp_second,
):
    row_count = inputs.shape[0]
    seq_length = row_count * lax.axis_size("tensor")
    head_width = attn_weight.shape[2]
    head_count = head_width // HEAD_DIM
    segment, position = doc_layout(doc_lengths[0], seq_length)
    cos_table, sine_table = rope_tables(position)
    block_rows = min(512, seq_length)
    block_count = seq_length // block_rows
    seg_blocks = segment.reshape(block_count, block_rows)
    pos_blocks = position.reshape(block_count, block_rows)
    score_scale = HEAD_DIM ** (-0.5)
    layer_in = inputs.astype(jnp.float32)
    normed_one, inv_one = norm_forward(layer_in)
    first_in = lax.all_gather(
        (normed_one * norm_gains[0]).astype(jnp.bfloat16), "tensor", axis=0, tiled=True
    )
    attn_low = lax.all_gather(attn_weight.astype(jnp.bfloat16), "dp", axis=1, tiled=True)

    def project(matrix):
        return jnp.dot(first_in, matrix, preferred_element_type=jnp.float32).reshape(
            seq_length, head_count, HEAD_DIM
        )

    queries = rotate(project(attn_low[0]), cos_table, sine_table).astype(jnp.bfloat16)
    key_rows = rotate(project(attn_low[1]), cos_table, sine_table).astype(jnp.bfloat16)
    values = project(attn_low[2]).astype(jnp.bfloat16)
    query_blocks = queries.reshape(block_count, block_rows, head_count, HEAD_DIM)

    def forward_block(pieces):
        return attend_forward(
            pieces[0], pieces[1], pieces[2], key_rows, values, segment, position, score_scale
        )

    attended, log_totals = lax.map(forward_block, (query_blocks, seg_blocks, pos_blocks))
    attended = attended.reshape(seq_length, head_width)
    middle = layer_in + lax.psum_scatter(
        dot_transposed(attended, attn_low[3]).astype(jnp.bfloat16),
        "tensor",
        scatter_dimension=0,
        tiled=True,
    ).astype(jnp.float32)
    normed_two, inv_two = norm_forward(middle)
    second_in = lax.all_gather(
        (normed_two * norm_gains[1]).astype(jnp.bfloat16), "tensor", axis=0, tiled=True
    )
    mlp_low = lax.all_gather(mlp_weight.astype(jnp.bfloat16), "dp", axis=1, tiled=True)
    gate_proj = jnp.dot(second_in, mlp_low[0], preferred_element_type=jnp.float32)
    up_proj = jnp.dot(second_in, mlp_low[1], preferred_element_type=jnp.float32)
    sigmoid_gate = jax.nn.sigmoid(gate_proj)
    hidden = (gate_proj * sigmoid_gate * up_proj).astype(jnp.bfloat16)
    layer_out = middle + lax.psum_scatter(
        dot_transposed(hidden, mlp_low[2]).astype(jnp.bfloat16),
        "tensor",
        scatter_dimension=0,
        tiled=True,
    ).astype(jnp.float32)
    attn_back, mlp_back = (
        lax.all_gather(attn_weight.astype(jnp.bfloat16), "dp", axis=1, tiled=True),
        lax.all_gather(mlp_weight.astype(jnp.bfloat16), "dp", axis=1, tiled=True),
    )
    grad_out = lax.all_gather(cotangent, "tensor", axis=0, tiled=True)
    d_hidden = jnp.dot(grad_out, mlp_back[2], preferred_element_type=jnp.float32)
    down_grad = dot_over_rows(grad_out, hidden)
    d_gate = (
        d_hidden * up_proj * (sigmoid_gate * (1.0 + gate_proj * (1.0 - sigmoid_gate)))
    ).astype(jnp.bfloat16)
    d_up = (d_hidden * (gate_proj * sigmoid_gate)).astype(jnp.bfloat16)

    def to_owner(partial):
        return lax.psum_scatter(
            partial.astype(jnp.bfloat16), "dp", scatter_dimension=0, tiled=True
        ).astype(jnp.float32)

    mlp_grad = jnp.stack(
        [
            to_owner(dot_over_rows(second_in, d_gate)),
            to_owner(dot_over_rows(second_in, d_up)),
            to_owner(down_grad),
        ]
    )
    d_second = lax.psum_scatter(
        (dot_transposed(d_gate, mlp_back[0]) + dot_transposed(d_up, mlp_back[1])).astype(
            jnp.bfloat16
        ),
        "tensor",
        scatter_dimension=0,
        tiled=True,
    ).astype(jnp.float32)
    d_middle, gain_two = norm_backward(d_second, normed_two, inv_two, norm_gains[1])
    d_middle = d_middle + cotangent.astype(jnp.float32)
    d_attn = lax.all_gather(d_middle.astype(jnp.bfloat16), "tensor", axis=0, tiled=True)
    out_proj_grad = dot_over_rows(d_attn, attended)
    d_attended = jnp.dot(d_attn, attn_back[3], preferred_element_type=jnp.float32).astype(
        jnp.bfloat16
    )
    grad_blocks = d_attended.reshape(block_count, block_rows, head_count, HEAD_DIM)

    def back_block(carry_sums, pieces):
        return attend_backward(carry_sums, pieces, key_rows, values, segment, position, score_scale)

    empty_sum = jnp.zeros((seq_length, head_count, HEAD_DIM), jnp.float32)
    block_sums, query_grad = lax.scan(
        back_block,
        (empty_sum, empty_sum),
        (query_blocks, grad_blocks, log_totals, seg_blocks, pos_blocks),
    )
    key_grad, value_grad = block_sums
    query_raw = (
        rotate_back(query_grad.reshape(seq_length, head_count, HEAD_DIM), cos_table, sine_table)
        .reshape(seq_length, head_width)
        .astype(jnp.bfloat16)
    )
    key_raw = (
        rotate_back(key_grad, cos_table, sine_table)
        .reshape(seq_length, head_width)
        .astype(jnp.bfloat16)
    )
    value_raw = value_grad.reshape(seq_length, head_width).astype(jnp.bfloat16)
    attn_grad = jnp.stack(
        [
            to_owner(dot_over_rows(first_in, query_raw)),
            to_owner(dot_over_rows(first_in, key_raw)),
            to_owner(dot_over_rows(first_in, value_raw)),
            to_owner(out_proj_grad),
        ]
    )
    d_first = lax.psum_scatter(
        (
            dot_transposed(query_raw, attn_back[0])
            + dot_transposed(key_raw, attn_back[1])
            + dot_transposed(value_raw, attn_back[2])
        ).astype(jnp.bfloat16),
        "tensor",
        scatter_dimension=0,
        tiled=True,
    ).astype(jnp.float32)
    d_input, gain_one = norm_backward(d_first, normed_one, inv_one, norm_gains[0])
    grad_in = d_input + d_middle
    gain_grad = lax.psum(jnp.stack([gain_one, gain_two]), ("dp", "tensor"))
    gain_first_new, gain_second_new, gain_new = adam_update(
        norm_gains, gain_grad, gain_first, gain_second, GAIN_RATE
    )
    attn_first_new, attn_second_new, attn_new = adam_update(
        attn_weight, attn_grad, attn_first, attn_second, attn_rates()
    )
    mlp_first_new, mlp_second_new, mlp_new = adam_update(
        mlp_weight, mlp_grad, mlp_first, mlp_second, 0.5 * D ** (-0.5)
    )
    return (
        layer_out.astype(jnp.bfloat16),
        grad_in,
        gain_grad,
        attn_grad,
        mlp_grad,
        gain_first_new,
        attn_first_new,
        mlp_first_new,
        gain_second_new,
        attn_second_new,
        mlp_second_new,
        gain_new,
        attn_new,
        mlp_new,
    )


def solution(mesh):
    placed = (
        P(("dp", "tensor"), None),
        P(("dp", "tensor"), None),
        P("dp", None),
        P(),
        P(None, "dp", "tensor"),
        P(None, "dp", "tensor"),
        P(),
        P(None, "dp", "tensor"),
        P(None, "dp", "tensor"),
        P(),
        P(None, "dp", "tensor"),
        P(None, "dp", "tensor"),
    )
    return jax.shard_map(
        local,
        mesh=mesh,
        in_specs=placed,
        out_specs=(
            P(("dp", "tensor"), None),
            P(("dp", "tensor"), None),
            P(),
            P(None, "dp", "tensor"),
            P(None, "dp", "tensor"),
            P(),
            P(None, "dp", "tensor"),
            P(None, "dp", "tensor"),
            P(),
            P(None, "dp", "tensor"),
            P(None, "dp", "tensor"),
            P(),
            P(None, "dp", "tensor"),
            P(None, "dp", "tensor"),
        ),
        check_vma=False,
    )
```

```python
import functools

import jax
import jax.numpy as jnp
from jax import lax
from jax.experimental import pallas as pl
from jax.experimental.pallas import tpu as pltpu
from jax.sharding import PartitionSpec as P

D = 2048
HEAD_DIM = 64
STEP = 10


EPS_NORM = 1e-05
ROPE_BASE = 130000.0
BETA_ONE = 0.9
BETA_TWO = 0.95
EPS_ADAM = 1e-08
WEIGHT_DECAY = 0.1
GAIN_RATE = 0.3
MASKED = -1e30


def doc_layout(lengths, seq_length):
    doc_ends = jnp.cumsum(lengths)
    starts = doc_ends - lengths
    places = jnp.arange(seq_length, dtype=jnp.int32)
    segment = jnp.sum((places[:, None] >= doc_ends[None, :]).astype(jnp.int32), axis=1)
    owners = segment[:, None] == jnp.arange(lengths.shape[0], dtype=jnp.int32)[None, :]
    position = places - jnp.sum(jnp.where(owners, starts[None, :], 0), axis=1)
    return (segment, position)


def rope_tables(position):
    half_dim = HEAD_DIM // 2
    frequencies = jnp.power(
        jnp.float32(ROPE_BASE), -2.0 * jnp.arange(half_dim, dtype=jnp.float32) / HEAD_DIM
    )
    angles = position.astype(jnp.float32)[:, None] * frequencies[None, :]
    return (jnp.cos(angles)[:, None, :], jnp.sin(angles)[:, None, :])


def rotate(field, cos_table, sine_table):
    half_dim = field.shape[-1] // 2
    first_half = field[..., :half_dim]
    second_half = field[..., half_dim:]
    return jnp.concatenate(
        [
            first_half * cos_table - second_half * sine_table,
            second_half * cos_table + first_half * sine_table,
        ],
        axis=-1,
    )


def rotate_back(gradient, cos_table, sine_table):
    half_dim = gradient.shape[-1] // 2
    first_half = gradient[..., :half_dim]
    second_half = gradient[..., half_dim:]
    return jnp.concatenate(
        [
            first_half * cos_table + second_half * sine_table,
            second_half * cos_table - first_half * sine_table,
        ],
        axis=-1,
    )


def dot_transposed(left, right):
    return lax.dot_general(
        left, right, (((1,), (1,)), ((), ())), preferred_element_type=jnp.float32
    )


def dot_over_rows(left, right):
    return lax.dot_general(
        left, right, (((0,), (0,)), ((), ())), preferred_element_type=jnp.float32
    )


def allowed_keys(seg_rows, pos_rows, segment, position):
    return (seg_rows[:, None] == segment[None, :]) & (position[None, :] <= pos_rows[:, None])


def attend_forward(
    query_block, seg_rows, pos_rows, key_rows, values, segment, position, score_scale
):
    raw_score = (
        jnp.einsum("bhd,khd->hbk", query_block, key_rows, preferred_element_type=jnp.float32)
        * score_scale
    )
    allowed = allowed_keys(seg_rows, pos_rows, segment, position)
    masked_score = jnp.where(allowed[None], raw_score, MASKED)
    row_peak = jnp.max(masked_score, axis=-1, keepdims=True)
    exp_score = jnp.exp(masked_score - row_peak)
    exp_total = jnp.sum(exp_score, axis=-1, keepdims=True)
    prob_low = (exp_score / exp_total).astype(jnp.bfloat16)
    result = jnp.einsum(
        "hbk,khd->bhd", prob_low, values, preferred_element_type=jnp.float32
    ).astype(jnp.bfloat16)
    return (result, (row_peak + jnp.log(exp_total))[..., 0])


def attend_backward(carry_sums, pieces, key_rows, values, segment, position, score_scale):
    key_sum, value_sum = carry_sums
    query_block, grad_block, log_total, seg_rows, pos_rows = pieces
    raw_score = (
        jnp.einsum("bhd,khd->hbk", query_block, key_rows, preferred_element_type=jnp.float32)
        * score_scale
    )
    allowed = allowed_keys(seg_rows, pos_rows, segment, position)
    probs = jnp.where(allowed[None], jnp.exp(raw_score - log_total[:, :, None]), 0.0)
    value_sum = value_sum + jnp.einsum(
        "hbk,bhd->khd", probs.astype(jnp.bfloat16), grad_block, preferred_element_type=jnp.float32
    )
    prob_grad = jnp.einsum("bhd,khd->hbk", grad_block, values, preferred_element_type=jnp.float32)
    score_grad = (probs * (prob_grad - jnp.sum(prob_grad * probs, axis=-1, keepdims=True))).astype(
        jnp.bfloat16
    )
    query_grad = (
        jnp.einsum("hbk,khd->bhd", score_grad, key_rows, preferred_element_type=jnp.float32)
        * score_scale
    )
    key_sum = (
        key_sum
        + jnp.einsum("hbk,bhd->khd", score_grad, query_block, preferred_element_type=jnp.float32)
        * score_scale
    )
    return ((key_sum, value_sum), query_grad)


MESH = pl.DeviceIdType.MESH
BLOCK = 32
TILE = 256


def line_kernel(n, parts, products, extras, outs, gathers, finish, *refs):
    refs = list(refs)
    take = lambda count: [refs.pop(0) for _ in range(count)]
    lefts, rights, more, results = take(products), take(products), take(extras), take(outs)
    gathered = take(1)[0] if gathers else None
    if products:
        totals, run_right, run_left, sums_sent, sums_got = take(5)
    if gathers:
        rows_sent, rows_got = take(2)
    me = lax.axis_index("tensor")
    has_left, has_right = me > 0, me < n - 1
    rows = totals.shape[1] if products else gathered.shape[0] // n
    part_rows = rows // parts
    hops = n - 1

    def sum_copy(way, part, hop):
        slot = part * hops + hop
        run = (run_right, run_left)[way]
        return pltpu.make_async_remote_copy(
            src_ref=run.at[slot],
            dst_ref=run.at[slot],
            send_sem=sums_sent.at[way, slot],
            recv_sem=sums_got.at[way, slot],
            device_id={"tensor": me + 1 - 2 * way},
            device_id_type=MESH,
        )

    def product(dest):
        first = pl.multiple_of(dest * rows, rows)

        @pl.loop(0, totals.shape[2] // TILE)
        def _(tile):
            columns = pl.ds(pl.multiple_of(tile * TILE, TILE), TILE)
            value = None
            for left, right in zip(lefts, rights):
                term = lax.dot_general(
                    left[pl.ds(first, rows), :],
                    right[columns, :],
                    (((1,), (1,)), ((), ())),
                    preferred_element_type=jnp.float32,
                )
                value = term if value is None else value + term
            totals[dest, :, columns] = value

    def pass_on(way, part, hop, dest):
        run, slot = (run_right, run_left)[way], part * hops + hop
        fed = (has_left, has_right)[way]
        copy = sum_copy(way, part, hop)

        @pl.when(fed)
        def _():
            copy.wait_recv()

            @pl.loop(0, part_rows // BLOCK)
            def _(block):
                at = pl.multiple_of(block * BLOCK, BLOCK)
                own = totals[dest, pl.ds(part * part_rows + at, BLOCK), :]
                came = run[slot, pl.ds(at, BLOCK), :].astype(jnp.float32)
                run[slot, pl.ds(at, BLOCK), :] = (own + came).astype(jnp.bfloat16)

        @pl.when(jnp.logical_not(fed))
        def _():
            @pl.loop(0, part_rows // BLOCK)
            def _(block):
                at = pl.multiple_of(block * BLOCK, BLOCK)
                own = totals[dest, pl.ds(part * part_rows + at, BLOCK), :]
                run[slot, pl.ds(at, BLOCK), :] = own.astype(jnp.bfloat16)

        copy.start()

    def sum_step(part, hop):
        far, near = n - 1 - hop, hop
        if part == 0:
            pl.when(far > me)(lambda: product(far))
            pl.when(near < me)(lambda: product(near))
            if hop == 0:
                product(me)
        pl.when(far > me)(lambda: pass_on(0, part, hop, far))
        pl.when(near < me)(lambda: pass_on(1, part, hop, near))

    def last_sum(part):
        for way, fed, hop in ((0, has_left, n - 1 - me), (1, has_right, me)):
            run = (run_right, run_left)[way]

            @pl.when(fed)
            def _():
                sum_copy(way, part, hop).wait_recv()
                slot = part * hops + hop

                @pl.loop(0, part_rows // BLOCK)
                def _(block):
                    at = pl.multiple_of(block * BLOCK, BLOCK)
                    own = pl.ds(part * part_rows + at, BLOCK)
                    came = run[slot, pl.ds(at, BLOCK), :].astype(jnp.float32)
                    totals[me, own, :] = totals[me, own, :] + came

    def finish_part(part):
        @pl.loop(0, part_rows // BLOCK)
        def _(block):
            at = pl.multiple_of(part * part_rows + block * BLOCK, BLOCK)
            total = totals[me, pl.ds(at, BLOCK), :] if products else None
            sent = finish(at, total, more, results)
            if gathers:
                gathered[pl.ds(pl.multiple_of(me * rows + at, BLOCK), BLOCK), :] = sent

    def row_copy(way, part, hop, owner):
        place = gathered.at[pl.ds(pl.multiple_of(owner * rows + part * part_rows, part_rows), part_rows), :]
        slot = part * hops + hop
        return pltpu.make_async_remote_copy(
            src_ref=place,
            dst_ref=place,
            send_sem=rows_sent.at[way, slot],
            recv_sem=rows_got.at[way, slot],
            device_id={"tensor": me + 1 - 2 * way},
            device_id_type=MESH,
        )

    def rows_start(part):
        pl.when(has_right)(lambda: row_copy(0, part, 0, me).start())
        pl.when(has_left)(lambda: row_copy(1, part, 0, me).start())

    def rows_step(part, hop):
        @pl.when(hop < me)
        def _():
            owner = me - 1 - hop
            row_copy(0, part, hop, owner).wait_recv()
            if hop + 1 < hops:
                pl.when(has_right)(lambda: row_copy(0, part, hop + 1, owner).start())

        @pl.when(hop < n - 1 - me)
        def _():
            owner = me + 1 + hop
            row_copy(1, part, hop, owner).wait_recv()
            if hop + 1 < hops:
                pl.when(has_left)(lambda: row_copy(1, part, hop + 1, owner).start())

    barrier = pltpu.get_barrier_semaphore()
    for there, step in ((has_left, -1), (has_right, 1)):

        @pl.when(there)
        def _():
            pl.semaphore_signal(barrier, inc=1, device_id={"tensor": me + step}, device_id_type=MESH)

    pl.semaphore_wait(barrier, has_left.astype(jnp.int32) + has_right.astype(jnp.int32))

    for result in results:
        if result.shape[0] == 8:
            result[...] = jnp.zeros_like(result)
    for part in range(parts):
        for hop in range(hops):
            if products:
                sum_step(part, hop)
            if gathers and part > 0:
                rows_step(part - 1, hop)
        if products:
            last_sum(part)
        finish_part(part)
        if gathers:
            rows_start(part)
    if gathers:
        for hop in range(hops):
            rows_step(parts - 1, hop)
    for part in range(parts):
        for hop in range(hops):
            if products:
                pl.when(n - 1 - hop > me)(lambda: sum_copy(0, part, hop).wait_send())
                pl.when(hop < me)(lambda: sum_copy(1, part, hop).wait_send())
            if gathers:
                pl.when(has_right & (hop <= me))(lambda: row_copy(0, part, hop, me - hop).wait_send())
                pl.when(has_left & (hop <= n - 1 - me))(
                    lambda: row_copy(1, part, hop, me + hop).wait_send()
                )


def line_exchange(name, collective_id, pairs, extras, outs, rows, width, finish, gathers, parts):
    n = lax.axis_size("tensor")
    hops = n - 1
    scratch = []
    if pairs:
        scratch = scratch + [
            pltpu.VMEM((n, rows, width), jnp.float32),
            pltpu.VMEM((parts * hops, rows // parts, width), jnp.bfloat16),
            pltpu.VMEM((parts * hops, rows // parts, width), jnp.bfloat16),
            pltpu.SemaphoreType.DMA((2, parts * hops)),
            pltpu.SemaphoreType.DMA((2, parts * hops)),
        ]
    if gathers:
        scratch = scratch + [
            pltpu.SemaphoreType.DMA((2, parts * hops)),
            pltpu.SemaphoreType.DMA((2, parts * hops)),
        ]
        outs = outs + [jax.ShapeDtypeStruct((n * rows, width), jnp.bfloat16)]
    operands = [pair[0] for pair in pairs] + [pair[1] for pair in pairs] + list(extras)
    depth = sum(pair[0].shape[1] for pair in pairs)
    whole = pl.BlockSpec(memory_space=pltpu.VMEM)
    return pl.pallas_call(
        functools.partial(
            line_kernel, n, parts, len(pairs), len(extras), len(outs) - gathers, gathers, finish
        ),
        out_shape=outs,
        in_specs=[whole] * len(operands),
        out_specs=[whole] * len(outs),
        scratch_shapes=scratch,
        compiler_params=pltpu.CompilerParams(
            collective_id=collective_id, has_side_effects=True, vmem_limit_bytes=60 * 2**20
        ),
        cost_estimate=pl.CostEstimate(
            flops=2 * n * rows * width * max(depth, 1),
            bytes_accessed=200 * 2**20,
            transcendentals=0,
        ),
        name=name,
    )(*operands)


def inverse_scale(field):
    return lax.rsqrt(jnp.mean(field * field, axis=-1, keepdims=True) + EPS_NORM)


def first_norm(at, total, more, results):
    layer_in, gains = more
    field = layer_in[pl.ds(at, BLOCK), :].astype(jnp.float32)
    return (field * inverse_scale(field) * gains[0:1, :]).astype(jnp.bfloat16)


def second_norm(at, total, more, results):
    layer_in, gains = more
    field = layer_in[pl.ds(at, BLOCK), :].astype(jnp.float32) + total
    results[0][pl.ds(at, BLOCK), :] = field
    return (field * inverse_scale(field) * gains[1:2, :]).astype(jnp.bfloat16)


def norm_back(field, gradient, gain_row, gain_out):
    inv_scale = inverse_scale(field)
    normed = field * inv_scale
    scaled = gradient * gain_row
    back = inv_scale * (scaled - normed * jnp.mean(scaled * normed, axis=-1, keepdims=True))
    product = gradient * normed
    folded = product[0:8]
    for k in range(8, BLOCK, 8):
        folded = folded + product[k : k + 8]
    gain_out[...] = gain_out[...] + folded
    return back


def second_back(at, total, more, results):
    middle, cotangent, gains = more
    rows = pl.ds(at, BLOCK)
    back = norm_back(middle[rows, :], total, gains[1:2, :], results[1])
    back = back + cotangent[rows, :].astype(jnp.float32)
    results[0][rows, :] = back
    return back.astype(jnp.bfloat16)


def first_back(at, total, more, results):
    layer_in, d_middle, gains = more
    rows = pl.ds(at, BLOCK)
    back = norm_back(layer_in[rows, :].astype(jnp.float32), total, gains[0:1, :], results[1])
    results[0][rows, :] = back + d_middle[rows, :]


def attn_rates():
    return jnp.array([1.0, 1.0, 1.0, 8.0**0.5], jnp.float32).reshape(4, 1, 1) * (0.5 * D ** (-0.5))


def adam_update(weight, gradient, moment_one, moment_two, step_rate):
    first_new = BETA_ONE * moment_one + (1.0 - BETA_ONE) * gradient
    second_new = BETA_TWO * moment_two + (1.0 - BETA_TWO) * gradient * gradient
    fix_one = 1.0 - BETA_ONE**STEP
    fix_two = 1.0 - BETA_TWO**STEP
    weight_new = weight - step_rate * (
        first_new / fix_one / (jnp.sqrt(second_new / fix_two) + EPS_ADAM) + WEIGHT_DECAY * weight
    )
    return (first_new, second_new, weight_new)


def local(
    inputs,
    cotangent,
    doc_lengths,
    norm_gains,
    attn_weight,
    mlp_weight,
    gain_first,
    attn_first,
    mlp_first,
    gain_second,
    attn_second,
    mlp_second,
):
    row_count = inputs.shape[0]
    seq_length = row_count * lax.axis_size("tensor")
    head_width = attn_weight.shape[2]
    head_count = head_width // HEAD_DIM
    segment, position = doc_layout(doc_lengths[0], seq_length)
    cos_table, sine_table = rope_tables(position)
    block_rows = min(512, seq_length)
    block_count = seq_length // block_rows
    seg_blocks = segment.reshape(block_count, block_rows)
    pos_blocks = position.reshape(block_count, block_rows)
    score_scale = HEAD_DIM ** (-0.5)
    width = inputs.shape[1]
    rows_f32 = jax.ShapeDtypeStruct((row_count, width), jnp.float32)
    gain_f32 = jax.ShapeDtypeStruct((8, width), jnp.float32)
    exchange = functools.partial(line_exchange, rows=row_count, width=width)
    (first_in,) = exchange(
        "first_norm", 1, [], [inputs, norm_gains], [], finish=first_norm, gathers=True, parts=1
    )
    attn_low = lax.all_gather(attn_weight.astype(jnp.bfloat16), "dp", axis=1, tiled=True)

    def project(matrix):
        return jnp.dot(first_in, matrix, preferred_element_type=jnp.float32).reshape(
            seq_length, head_count, HEAD_DIM
        )

    queries = rotate(project(attn_low[0]), cos_table, sine_table).astype(jnp.bfloat16)
    key_rows = rotate(project(attn_low[1]), cos_table, sine_table).astype(jnp.bfloat16)
    values = project(attn_low[2]).astype(jnp.bfloat16)
    query_blocks = queries.reshape(block_count, block_rows, head_count, HEAD_DIM)

    def forward_block(pieces):
        return attend_forward(
            pieces[0], pieces[1], pieces[2], key_rows, values, segment, position, score_scale
        )

    attended, log_totals = lax.map(forward_block, (query_blocks, seg_blocks, pos_blocks))
    attended = attended.reshape(seq_length, head_width)
    middle, second_in = exchange(
        "attention_out",
        2,
        [(attended, attn_low[3])],
        [inputs, norm_gains],
        [rows_f32],
        finish=second_norm,
        gathers=True,
        parts=2,
    )
    mlp_low = lax.all_gather(mlp_weight.astype(jnp.bfloat16), "dp", axis=1, tiled=True)
    gate_proj = jnp.dot(second_in, mlp_low[0], preferred_element_type=jnp.float32)
    up_proj = jnp.dot(second_in, mlp_low[1], preferred_element_type=jnp.float32)
    sigmoid_gate = jax.nn.sigmoid(gate_proj)
    hidden = (gate_proj * sigmoid_gate * up_proj).astype(jnp.bfloat16)
    layer_out = middle + lax.psum_scatter(
        dot_transposed(hidden, mlp_low[2]).astype(jnp.bfloat16),
        "tensor",
        scatter_dimension=0,
        tiled=True,
    ).astype(jnp.float32)
    attn_back, mlp_back = (
        lax.all_gather(attn_weight.astype(jnp.bfloat16), "dp", axis=1, tiled=True),
        lax.all_gather(mlp_weight.astype(jnp.bfloat16), "dp", axis=1, tiled=True),
    )
    grad_out = lax.all_gather(cotangent, "tensor", axis=0, tiled=True)
    d_hidden = jnp.dot(grad_out, mlp_back[2], preferred_element_type=jnp.float32)
    down_grad = dot_over_rows(grad_out, hidden)
    d_gate = (
        d_hidden * up_proj * (sigmoid_gate * (1.0 + gate_proj * (1.0 - sigmoid_gate)))
    ).astype(jnp.bfloat16)
    d_up = (d_hidden * (gate_proj * sigmoid_gate)).astype(jnp.bfloat16)

    def to_owner(partial):
        return lax.psum_scatter(
            partial.astype(jnp.bfloat16), "dp", scatter_dimension=0, tiled=True
        ).astype(jnp.float32)

    mlp_grad = jnp.stack(
        [
            to_owner(dot_over_rows(second_in, d_gate)),
            to_owner(dot_over_rows(second_in, d_up)),
            to_owner(down_grad),
        ]
    )
    d_middle, gain_two, d_attn = exchange(
        "mlp_back",
        3,
        [(d_gate, mlp_back[0]), (d_up, mlp_back[1])],
        [middle, cotangent, norm_gains],
        [rows_f32, gain_f32],
        finish=second_back,
        gathers=True,
        parts=2,
    )
    out_proj_grad = dot_over_rows(d_attn, attended)
    d_attended = jnp.dot(d_attn, attn_back[3], preferred_element_type=jnp.float32).astype(
        jnp.bfloat16
    )
    grad_blocks = d_attended.reshape(block_count, block_rows, head_count, HEAD_DIM)

    def back_block(carry_sums, pieces):
        return attend_backward(carry_sums, pieces, key_rows, values, segment, position, score_scale)

    empty_sum = jnp.zeros((seq_length, head_count, HEAD_DIM), jnp.float32)
    block_sums, query_grad = lax.scan(
        back_block,
        (empty_sum, empty_sum),
        (query_blocks, grad_blocks, log_totals, seg_blocks, pos_blocks),
    )
    key_grad, value_grad = block_sums
    query_raw = (
        rotate_back(query_grad.reshape(seq_length, head_count, HEAD_DIM), cos_table, sine_table)
        .reshape(seq_length, head_width)
        .astype(jnp.bfloat16)
    )
    key_raw = (
        rotate_back(key_grad, cos_table, sine_table)
        .reshape(seq_length, head_width)
        .astype(jnp.bfloat16)
    )
    value_raw = value_grad.reshape(seq_length, head_width).astype(jnp.bfloat16)
    attn_grad = jnp.stack(
        [
            to_owner(dot_over_rows(first_in, query_raw)),
            to_owner(dot_over_rows(first_in, key_raw)),
            to_owner(dot_over_rows(first_in, value_raw)),
            to_owner(out_proj_grad),
        ]
    )
    grad_in, gain_one = exchange(
        "attention_back",
        4,
        [(query_raw, attn_back[0]), (key_raw, attn_back[1]), (value_raw, attn_back[2])],
        [inputs, d_middle, norm_gains],
        [rows_f32, gain_f32],
        finish=first_back,
        gathers=False,
        parts=1,
    )
    gain_grad = lax.psum(jnp.stack([jnp.sum(gain_one, axis=0), jnp.sum(gain_two, axis=0)]), ("dp", "tensor"))
    gain_first_new, gain_second_new, gain_new = adam_update(
        norm_gains, gain_grad, gain_first, gain_second, GAIN_RATE
    )
    attn_first_new, attn_second_new, attn_new = adam_update(
        attn_weight, attn_grad, attn_first, attn_second, attn_rates()
    )
    mlp_first_new, mlp_second_new, mlp_new = adam_update(
        mlp_weight, mlp_grad, mlp_first, mlp_second, 0.5 * D ** (-0.5)
    )
    return (
        layer_out.astype(jnp.bfloat16),
        grad_in,
        gain_grad,
        attn_grad,
        mlp_grad,
        gain_first_new,
        attn_first_new,
        mlp_first_new,
        gain_second_new,
        attn_second_new,
        mlp_second_new,
        gain_new,
        attn_new,
        mlp_new,
    )


def solution(mesh):
    placed = (
        P(("dp", "tensor"), None),
        P(("dp", "tensor"), None),
        P("dp", None),
        P(),
        P(None, "dp", "tensor"),
        P(None, "dp", "tensor"),
        P(),
        P(None, "dp", "tensor"),
        P(None, "dp", "tensor"),
        P(),
        P(None, "dp", "tensor"),
        P(None, "dp", "tensor"),
    )
    return jax.shard_map(
        local,
        mesh=mesh,
        in_specs=placed,
        out_specs=(
            P(("dp", "tensor"), None),
            P(("dp", "tensor"), None),
            P(),
            P(None, "dp", "tensor"),
            P(None, "dp", "tensor"),
            P(),
            P(None, "dp", "tensor"),
            P(None, "dp", "tensor"),
            P(),
            P(None, "dp", "tensor"),
            P(None, "dp", "tensor"),
            P(),
            P(None, "dp", "tensor"),
            P(None, "dp", "tensor"),
        ),
        check_vma=False,
    )
```

```python
import functools

import jax
import jax.numpy as jnp
from jax import lax
from jax.experimental import pallas as pl
from jax.experimental.pallas import tpu as pltpu
from jax.sharding import PartitionSpec as P

D = 2048
HEAD_DIM = 64
STEP = 10


EPS_NORM = 1e-05
ROPE_BASE = 130000.0
BETA_ONE = 0.9
BETA_TWO = 0.95
EPS_ADAM = 1e-08
WEIGHT_DECAY = 0.1
GAIN_RATE = 0.3
MASKED = -1e30


def doc_layout(lengths, seq_length):
    doc_ends = jnp.cumsum(lengths)
    starts = doc_ends - lengths
    places = jnp.arange(seq_length, dtype=jnp.int32)
    segment = jnp.sum((places[:, None] >= doc_ends[None, :]).astype(jnp.int32), axis=1)
    owners = segment[:, None] == jnp.arange(lengths.shape[0], dtype=jnp.int32)[None, :]
    position = places - jnp.sum(jnp.where(owners, starts[None, :], 0), axis=1)
    return (segment, position)


def rope_tables(position):
    half_dim = HEAD_DIM // 2
    frequencies = jnp.power(
        jnp.float32(ROPE_BASE), -2.0 * jnp.arange(half_dim, dtype=jnp.float32) / HEAD_DIM
    )
    angles = position.astype(jnp.float32)[:, None] * frequencies[None, :]
    cosine, sine = jnp.cos(angles), jnp.sin(angles)
    return (
        jnp.concatenate([cosine, cosine] * 2, axis=1),
        jnp.concatenate([-sine, sine] * 2, axis=1),
    )


MESH = pl.DeviceIdType.MESH
BLOCK = 32
TILE = 256


def whole_part(count):
    return [pl.BlockSpec(memory_space=pltpu.VMEM)] * count


def greet(n, me):
    barrier = pltpu.get_barrier_semaphore()
    for there, step in ((me > 0, -1), (me < n - 1, 1)):

        @pl.when(there)
        def _():
            pl.semaphore_signal(barrier, inc=1, device_id={"tensor": me + step}, device_id_type=MESH)

    pl.semaphore_wait(barrier, (me > 0).astype(jnp.int32) + (me < n - 1).astype(jnp.int32))


def blocks_of(count, body):
    @pl.loop(0, count // BLOCK)
    def _(block):
        body(pl.multiple_of(block * BLOCK, BLOCK))


class RowGather:
    def __init__(self, n, me, parts, place, sent, got):
        self.n, self.me, self.parts, self.place = n, me, parts, place
        self.sent, self.got = sent, got
        self.rows = place.shape[0] // n
        self.has_left, self.has_right = me > 0, me < n - 1

    def copy(self, way, part, hop, owner):
        count = self.rows // self.parts
        first = pl.multiple_of(owner * self.rows + part * count, count)
        block = self.place.at[pl.ds(first, count), :]
        slot = part * (self.n - 1) + hop
        return pltpu.make_async_remote_copy(
            src_ref=block,
            dst_ref=block,
            send_sem=self.sent.at[way, slot],
            recv_sem=self.got.at[way, slot],
            device_id={"tensor": self.me + 1 - 2 * way},
            device_id_type=MESH,
        )

    def start(self, part):
        pl.when(self.has_right)(lambda: self.copy(0, part, 0, self.me).start())
        pl.when(self.has_left)(lambda: self.copy(1, part, 0, self.me).start())

    def step(self, part, hop):
        last = hop + 1 == self.n - 1

        @pl.when(hop < self.me)
        def _():
            owner = self.me - 1 - hop
            self.copy(0, part, hop, owner).wait_recv()
            if not last:
                pl.when(self.has_right)(lambda: self.copy(0, part, hop + 1, owner).start())

        @pl.when(hop < self.n - 1 - self.me)
        def _():
            owner = self.me + 1 + hop
            self.copy(1, part, hop, owner).wait_recv()
            if not last:
                pl.when(self.has_left)(lambda: self.copy(1, part, hop + 1, owner).start())

    def drain(self):
        for part in range(self.parts):
            for hop in range(self.n - 1):
                pl.when(self.has_right & (hop <= self.me))(
                    lambda: self.copy(0, part, hop, self.me - hop).wait_send()
                )
                pl.when(self.has_left & (hop <= self.n - 1 - self.me))(
                    lambda: self.copy(1, part, hop, self.me + hop).wait_send()
                )


class SumScatter:
    def __init__(self, n, me, parts, lefts, rights, totals, runs, sent, got):
        self.n, self.me, self.parts = n, me, parts
        self.lefts, self.rights, self.totals, self.runs = lefts, rights, totals, runs
        self.sent, self.got = sent, got
        self.rows = totals.shape[1]
        self.fed = (me > 0, me < n - 1)

    def copy(self, way, part, hop):
        slot = part * (self.n - 1) + hop
        run = self.runs[way].at[slot]
        return pltpu.make_async_remote_copy(
            src_ref=run,
            dst_ref=run,
            send_sem=self.sent.at[way, slot],
            recv_sem=self.got.at[way, slot],
            device_id={"tensor": self.me + 1 - 2 * way},
            device_id_type=MESH,
        )

    def product(self, dest):
        first = pl.multiple_of(dest * self.rows, self.rows)

        @pl.loop(0, self.totals.shape[2] // TILE)
        def _(tile):
            columns = pl.ds(pl.multiple_of(tile * TILE, TILE), TILE)
            value = None
            for left, right in zip(self.lefts, self.rights):
                term = lax.dot_general(
                    left[pl.ds(first, self.rows), :],
                    right[columns, :],
                    (((1,), (1,)), ((), ())),
                    preferred_element_type=jnp.float32,
                )
                value = term if value is None else value + term
            self.totals[dest, :, columns] = value.astype(self.totals.dtype)

    def dests(self, hop):
        far, near = self.n - 1 - hop, hop
        return ((0, far, far > self.me), (1, near, near < self.me))

    def products(self, hop):
        for way, dest, needed in self.dests(hop):
            pl.when(needed)(lambda: self.product(dest))

    def open(self, part, hop):
        for way, dest, needed in self.dests(hop):
            run, slot = self.runs[way], part * (self.n - 1) + hop
            first = part * (self.rows // self.parts)

            @pl.when(needed & jnp.logical_not(self.fed[way]))
            def _():
                def body(at):
                    own = self.totals[dest, pl.ds(first + at, BLOCK), :]
                    run[slot, pl.ds(at, BLOCK), :] = own.astype(jnp.bfloat16)

                blocks_of(self.rows // self.parts, body)
                self.copy(way, part, hop).start()

    def pass_on(self, part, hop):
        for way, dest, needed in self.dests(hop):
            run, slot = self.runs[way], part * (self.n - 1) + hop
            first = part * (self.rows // self.parts)

            @pl.when(needed & self.fed[way])
            def _():
                self.copy(way, part, hop).wait_recv()

                def body(at):
                    own = self.totals[dest, pl.ds(first + at, BLOCK), :].astype(jnp.float32)
                    came = run[slot, pl.ds(at, BLOCK), :].astype(jnp.float32)
                    run[slot, pl.ds(at, BLOCK), :] = (own + came).astype(jnp.bfloat16)

                blocks_of(self.rows // self.parts, body)
                self.copy(way, part, hop).start()

    def last(self, part):
        first = part * (self.rows // self.parts)
        for way, hop in ((0, self.n - 1 - self.me), (1, self.me)):
            run = self.runs[way]

            @pl.when(self.fed[way])
            def _():
                self.copy(way, part, hop).wait_recv()
                slot = part * (self.n - 1) + hop

                def body(at):
                    own = pl.ds(first + at, BLOCK)
                    came = run[slot, pl.ds(at, BLOCK), :].astype(jnp.float32)
                    total = self.totals[self.me, own, :].astype(jnp.float32) + came
                    self.totals[self.me, own, :] = total.astype(self.totals.dtype)

                blocks_of(self.rows // self.parts, body)

    def drain(self):
        for part in range(self.parts):
            for hop in range(self.n - 1):
                for way, dest, needed in self.dests(hop):
                    pl.when(needed)(lambda: self.copy(way, part, hop).wait_send())


def scatter_scratch(n, parts, rows, width, kept=jnp.float32):
    slots = parts * (n - 1)
    return [
        pltpu.VMEM((n, rows, width), kept),
        pltpu.VMEM((slots, rows // parts, width), jnp.bfloat16),
        pltpu.VMEM((slots, rows // parts, width), jnp.bfloat16),
        pltpu.SemaphoreType.DMA((2, slots)),
        pltpu.SemaphoreType.DMA((2, slots)),
    ]


def gather_scratch(n, parts):
    return [pltpu.SemaphoreType.DMA((2, parts * (n - 1)))] * 2


def line_kernel(n, parts, products, extras, outs, gathers, finish, *refs):
    refs = list(refs)
    take = lambda count: [refs.pop(0) for _ in range(count)]
    lefts, rights, more, results = take(products), take(products), take(extras), take(outs)
    gathered = take(1)[0] if gathers else None
    me = lax.axis_index("tensor")
    if products:
        totals, run_right, run_left, sent, got = take(5)
        sums = SumScatter(n, me, parts, lefts, rights, totals, (run_right, run_left), sent, got)
    if gathers:
        gather = RowGather(n, me, parts, gathered, *take(2))
    rows = totals.shape[1] if products else gathered.shape[0] // n
    part_rows = rows // parts

    def finish_part(part):
        def body(block):
            at = pl.multiple_of(part * part_rows + block, BLOCK)
            total = totals[me, pl.ds(at, BLOCK), :] if products else None
            sent_rows = finish(at, total, more, results)
            if gathers:
                gathered[pl.ds(pl.multiple_of(me * rows + at, BLOCK), BLOCK), :] = sent_rows

        blocks_of(part_rows, body)

    greet(n, me)
    for result in results:
        if result.shape[0] == 8:
            result[...] = jnp.zeros_like(result)
    if products:
        for hop in range(n - 1):
            sums.products(hop)
            sums.open(0, hop)
        for part in range(1, parts):
            for hop in range(n - 1):
                sums.open(part, hop)
        sums.product(me)
    for part in range(parts):
        for hop in range(n - 1):
            if products:
                sums.pass_on(part, hop)
            if gathers and part > 0:
                gather.step(part - 1, hop)
        if products:
            sums.last(part)
        finish_part(part)
        if gathers:
            gather.start(part)
    if gathers:
        for hop in range(n - 1):
            gather.step(parts - 1, hop)
        gather.drain()
    if products:
        sums.drain()


def line_exchange(name, collective_id, pairs, extras, outs, rows, width, finish, gathers, parts):
    n = lax.axis_size("tensor")
    scratch = scatter_scratch(n, parts, rows, width) if pairs else []
    if gathers:
        scratch = scratch + gather_scratch(n, parts)
        outs = outs + [jax.ShapeDtypeStruct((n * rows, width), jnp.bfloat16)]
    operands = [pair[0] for pair in pairs] + [pair[1] for pair in pairs] + list(extras)
    specs = whole_part(len(operands))
    for k, (left, right, which) in enumerate(pairs):
        specs[len(pairs) + k] = pl.BlockSpec(
            (None, *right.shape[1:]), lambda i, which=which: (which, 0, 0), pipeline_mode=pl.Buffered(1)
        )
    depth = sum(pair[0].shape[1] for pair in pairs)
    return pl.pallas_call(
        functools.partial(
            line_kernel, n, parts, len(pairs), len(extras), len(outs) - gathers, gathers, finish
        ),
        grid=(1,),
        out_shape=outs,
        in_specs=specs,
        out_specs=whole_part(len(outs)),
        scratch_shapes=scratch,
        compiler_params=pltpu.CompilerParams(
            collective_id=collective_id, has_side_effects=True, vmem_limit_bytes=60 * 2**20
        ),
        cost_estimate=pl.CostEstimate(
            flops=2 * n * rows * width * max(depth, 1),
            bytes_accessed=200 * 2**20,
            transcendentals=0,
        ),
        name=name,
    )(*operands)


def everywhere_kernel(sizes, field, result, came, sent, got):
    places = [lax.axis_index(name) for name in sizes]
    partners = []
    for name, place in zip(sizes, places):
        stride = 1
        while stride < sizes[name]:
            other = place + stride - 2 * stride * (place // stride % 2)
            partners.append({name: other})
            stride = 2 * stride
    barrier = pltpu.get_barrier_semaphore()
    for partner in partners:
        pl.semaphore_signal(barrier, inc=1, device_id=partner, device_id_type=MESH)
    pl.semaphore_wait(barrier, len(partners))
    result[...] = field[...]
    for k, partner in enumerate(partners):
        came[2 * k] = result[...]
        copy = pltpu.make_async_remote_copy(
            src_ref=came.at[2 * k],
            dst_ref=came.at[2 * k + 1],
            send_sem=sent.at[k],
            recv_sem=got.at[k],
            device_id=partner,
            device_id_type=MESH,
        )
        copy.start()
        copy.wait()
        result[...] = result[...] + came[2 * k + 1]


def sum_everywhere(field):
    sizes = {name: lax.axis_size(name) for name in ("dp", "tensor")}
    steps = sum(size.bit_length() - 1 for size in sizes.values())
    return pl.pallas_call(
        functools.partial(everywhere_kernel, sizes),
        out_shape=jax.ShapeDtypeStruct(field.shape, jnp.float32),
        in_specs=whole_part(1),
        out_specs=pl.BlockSpec(memory_space=pltpu.VMEM),
        scratch_shapes=[
            pltpu.VMEM((2 * steps, *field.shape), jnp.float32),
            pltpu.SemaphoreType.DMA((steps,)),
            pltpu.SemaphoreType.DMA((steps,)),
        ],
        compiler_params=pltpu.CompilerParams(collective_id=7, has_side_effects=True),
        name="gain_sum",
    )(field)


def inverse_scale(field):
    return lax.rsqrt(jnp.mean(field * field, axis=-1, keepdims=True) + EPS_NORM)


def first_norm(at, total, more, results):
    layer_in, gains = more
    field = layer_in[pl.ds(at, BLOCK), :].astype(jnp.float32)
    return (field * inverse_scale(field) * gains[0:1, :]).astype(jnp.bfloat16)


def second_norm(at, total, more, results):
    layer_in, gains = more
    field = layer_in[pl.ds(at, BLOCK), :].astype(jnp.float32) + total
    results[0][pl.ds(at, BLOCK), :] = field
    return (field * inverse_scale(field) * gains[1:2, :]).astype(jnp.bfloat16)


def norm_back(field, gradient, gain_row, gain_out):
    inv_scale = inverse_scale(field)
    normed = field * inv_scale
    scaled = gradient * gain_row
    back = inv_scale * (scaled - normed * jnp.mean(scaled * normed, axis=-1, keepdims=True))
    product = gradient * normed
    folded = product[0:8]
    for k in range(8, BLOCK, 8):
        folded = folded + product[k : k + 8]
    gain_out[...] = gain_out[...] + folded
    return back


def second_back(at, total, more, results):
    middle, cotangent, gains = more
    rows = pl.ds(at, BLOCK)
    back = norm_back(middle[rows, :], total, gains[1:2, :], results[1])
    back = back + cotangent[rows, :].astype(jnp.float32)
    results[0][rows, :] = back
    return back.astype(jnp.bfloat16)


def first_back(at, total, more, results):
    layer_in, d_middle, gains = more
    rows = pl.ds(at, BLOCK)
    back = norm_back(layer_in[rows, :].astype(jnp.float32), total, gains[0:1, :], results[1])
    results[0][rows, :] = back + d_middle[rows, :]


PAIR = 2 * HEAD_DIM
QUERIES = 256


def turned(field, cos_tile, sine_tile):
    lanes = lax.broadcasted_iota(jnp.int32, field.shape, 1)
    ahead = pltpu.roll(field, PAIR - HEAD_DIM // 2, 1)
    behind = pltpu.roll(field, HEAD_DIM // 2, 1)
    partner = jnp.where(lanes % HEAD_DIM < HEAD_DIM // 2, ahead, behind)
    return field * cos_tile + partner * sine_tile


def one_head(tile, head):
    lanes = lax.broadcasted_iota(jnp.int32, tile.shape, 1)
    return jnp.where(lanes // HEAD_DIM == head, tile, jnp.zeros_like(tile))


def over_lanes(left, right):
    return lax.dot_general(
        left, right, (((1,), (1,)), ((), ())), preferred_element_type=jnp.float32
    )


def masked(scores, starts, first_query):
    keys = lax.broadcasted_iota(jnp.int32, scores.shape, 0)
    queries = first_query + lax.broadcasted_iota(jnp.int32, scores.shape, 1)
    return jnp.where((keys >= starts) & (keys <= queries), scores, MASKED)


def attention_forward_kernel(
    n, first_in, weights, cos_ref, sine_ref, starts_ref, own_rows,
    queries, key_rows, values, attended, log_totals, gathered, turned_values, sent, got
):
    me = lax.axis_index("tensor")
    rows = own_rows.shape[0]
    length, width = queries.shape
    greet(n, me)
    gather = RowGather(n, me, 1, gathered, sent, got)
    blocks_of(
        rows,
        lambda at: gathered.__setitem__(
            (pl.ds(pl.multiple_of(me * rows + at, BLOCK), BLOCK), slice(None)),
            own_rows[pl.ds(at, BLOCK), :],
        ),
    )
    gather.start(0)

    @pl.loop(0, length // QUERIES)
    def _(block):
        at = pl.ds(pl.multiple_of(block * QUERIES, QUERIES), QUERIES)
        source = first_in[at, :]
        cos_tile, sine_tile = cos_ref[at, :], sine_ref[at, :]
        for which, target in enumerate((queries, key_rows, values)):
            field = jnp.dot(source, weights[which], preferred_element_type=jnp.float32)
            for pair in range(width // PAIR):
                tile = field[:, pair * PAIR : (pair + 1) * PAIR]
                if which < 2:
                    tile = turned(tile, cos_tile, sine_tile)
                if which == 0:
                    tile = tile.astype(jnp.bfloat16) * HEAD_DIM ** (-0.5)
                target[at, pair * PAIR : (pair + 1) * PAIR] = tile.astype(jnp.bfloat16)

    @pl.loop(0, width // PAIR)
    def _(pair):
        lanes = pl.ds(pl.multiple_of(pair * PAIR, PAIR), PAIR)
        turned_values[...] = values[:, lanes].astype(jnp.float32).T.astype(jnp.bfloat16)
        for block in range(length // QUERIES):
            at = pl.ds(block * QUERIES, QUERIES)
            reach = (block + 1) * QUERIES
            starts = starts_ref[:, at]
            both = []
            for head in range(2):
                query = one_head(queries[at, lanes], head)
                scores = masked(
                    over_lanes(key_rows[0:reach, lanes], query), starts, block * QUERIES
                )
                peak = jnp.max(scores, axis=0, keepdims=True)
                raised = jnp.exp(scores - peak)
                total = jnp.sum(raised, axis=0, keepdims=True)
                result = jnp.dot(
                    turned_values[head * HEAD_DIM : (head + 1) * HEAD_DIM, 0:reach],
                    raised.astype(jnp.bfloat16),
                    preferred_element_type=jnp.float32,
                )
                both.append(result / total)
                log_totals[2 * pair + head, :, at] = peak + jnp.log(total)
            attended[at, lanes] = jnp.concatenate(both, axis=0).T.astype(jnp.bfloat16)

    for hop in range(n - 1):
        gather.step(0, hop)
    gather.drain()


def attention_forward(first_in, weights, cos_tile, sine_tile, starts, own_rows):
    n = lax.axis_size("tensor")
    length, depth = first_in.shape
    width = weights.shape[2]
    narrow = jax.ShapeDtypeStruct((length, width), jnp.bfloat16)
    outs = [
        narrow,
        narrow,
        narrow,
        narrow,
        jax.ShapeDtypeStruct((width // HEAD_DIM, 1, length), jnp.float32),
        jax.ShapeDtypeStruct((length, depth), jnp.bfloat16),
    ]
    specs = whole_part(6)
    specs[1] = pl.BlockSpec((3, depth, width), lambda i: (0, 0, 0), pipeline_mode=pl.Buffered(1))
    return pl.pallas_call(
        functools.partial(attention_forward_kernel, n),
        grid=(1,),
        out_shape=outs,
        in_specs=specs,
        out_specs=whole_part(len(outs)),
        scratch_shapes=[pltpu.VMEM((PAIR, length), jnp.bfloat16)] + gather_scratch(n, 1),
        compiler_params=pltpu.CompilerParams(
            collective_id=5, has_side_effects=True, vmem_limit_bytes=60 * 2**20
        ),
        cost_estimate=pl.CostEstimate(
            flops=6 * length * depth * width, bytes_accessed=200 * 2**20, transcendentals=0
        ),
        name="attention_forward",
    )(first_in, weights, cos_tile, sine_tile, starts, own_rows)


def attention_back_kernel(
    n, d_attn, out_weight, queries, key_rows, values, attended, log_totals, cos_ref, sine_ref,
    starts_ref, middle, hidden, down_weight, query_raw, key_raw, value_raw, layer_out,
    d_attended, turned_keys, key_sum, value_sum, held, held_sems,
    totals, run_right, run_left, sent, got
):
    me = lax.axis_index("tensor")
    length, width = queries.shape

    def fetch(block):
        return pltpu.make_async_copy(
            d_attn.at[pl.ds(block * QUERIES, QUERIES), :], held.at[block % 2], held_sems.at[block % 2]
        )

    fetch(0).start()
    greet(n, me)
    sums = SumScatter(n, me, 1, [hidden], [down_weight], totals, (run_right, run_left), sent, got)
    for hop in range(n - 1):
        sums.products(hop)
        sums.open(0, hop)
    sums.product(me)

    for block in range(length // QUERIES):
        fetch(block).wait()
        if (block + 1) * QUERIES < length:
            fetch(block + 1).start()
        d_attended[block * QUERIES : (block + 1) * QUERIES, :] = jnp.dot(
            held[block % 2], out_weight[0], preferred_element_type=jnp.float32
        ).astype(jnp.bfloat16)

    def back_pair(pair):
        lanes = pl.ds(pl.multiple_of(pair * PAIR, PAIR), PAIR)
        turned_keys[...] = key_rows[:, lanes].astype(jnp.float32).T.astype(jnp.bfloat16)
        key_sum[...] = jnp.zeros_like(key_sum)
        value_sum[...] = jnp.zeros_like(value_sum)
        for block in range(length // QUERIES):
            at = pl.ds(block * QUERIES, QUERIES)
            reach = (block + 1) * QUERIES
            starts = starts_ref[:, at]
            grads = d_attended[at, lanes]
            shares = (grads.astype(jnp.float32) * attended[at, lanes].astype(jnp.float32)).T
            both = []
            for head in range(2):
                heads = slice(head * HEAD_DIM, (head + 1) * HEAD_DIM)
                query = one_head(queries[at, lanes], head)
                grad = one_head(grads, head)
                share = jnp.sum(shares[heads], axis=0, keepdims=True)
                scores = masked(
                    over_lanes(key_rows[0:reach, lanes], query), starts, block * QUERIES
                )
                probs = jnp.exp(scores - log_totals[2 * pair + head, :, at])
                prob_grad = over_lanes(values[0:reach, lanes], grad)
                score_grad = (probs * (prob_grad - share)).astype(jnp.bfloat16)
                value_sum[0:reach, :] = value_sum[0:reach, :] + jnp.dot(
                    probs.astype(jnp.bfloat16), grad, preferred_element_type=jnp.float32
                )
                key_sum[0:reach, :] = key_sum[0:reach, :] + jnp.dot(
                    score_grad, query, preferred_element_type=jnp.float32
                )
                both.append(
                    jnp.dot(
                        turned_keys[heads, 0:reach], score_grad, preferred_element_type=jnp.float32
                    )
                )
            query_grad = jnp.concatenate(both, axis=0).T * HEAD_DIM ** (-0.5)
            query_raw[at, lanes] = turned(query_grad, cos_ref[at, :], -sine_ref[at, :]).astype(
                jnp.bfloat16
            )
        key_raw[:, lanes] = turned(key_sum[...], cos_ref[...], -sine_ref[...]).astype(jnp.bfloat16)
        value_raw[:, lanes] = value_sum[...].astype(jnp.bfloat16)

    pairs = width // PAIR
    pl.loop(0, pairs // 2)(back_pair)
    sums.pass_on(0, 0)
    pl.loop(pairs // 2, pairs)(back_pair)
    for hop in range(1, n - 1):
        sums.pass_on(0, hop)
    sums.last(0)

    def body(at):
        rows = pl.ds(at, BLOCK)
        layer_out[rows, :] = (middle[rows, :] + totals[me, rows, :]).astype(jnp.bfloat16)

    blocks_of(middle.shape[0], body)
    sums.drain()


def attention_back(
    d_attn, attn_low, queries, key_rows, values, attended, log_totals, cos_tile, sine_tile, starts,
    middle, hidden, mlp_low
):
    n = lax.axis_size("tensor")
    length, depth = d_attn.shape
    width, units = queries.shape[1], hidden.shape[1]
    rows = middle.shape[0]
    narrow = jax.ShapeDtypeStruct((length, width), jnp.bfloat16)
    specs = whole_part(13)
    once = pl.Buffered(1)
    specs[0] = pl.BlockSpec(memory_space=pl.ANY)
    specs[1] = pl.BlockSpec((1, depth, width), lambda i: (3, 0, 0), pipeline_mode=once)
    specs[12] = pl.BlockSpec((None, depth, units), lambda i: (2, 0, 0), pipeline_mode=once)
    return pl.pallas_call(
        functools.partial(attention_back_kernel, n),
        grid=(1,),
        out_shape=[narrow, narrow, narrow, jax.ShapeDtypeStruct((rows, depth), jnp.bfloat16)],
        in_specs=specs,
        out_specs=whole_part(4),
        scratch_shapes=[
            pltpu.VMEM((length, width), jnp.bfloat16),
            pltpu.VMEM((PAIR, length), jnp.bfloat16),
            pltpu.VMEM((length, PAIR), jnp.float32),
            pltpu.VMEM((length, PAIR), jnp.float32),
            pltpu.VMEM((2, QUERIES, depth), jnp.bfloat16),
            pltpu.SemaphoreType.DMA((2,)),
        ]
        + scatter_scratch(n, 1, rows, depth, jnp.bfloat16),
        compiler_params=pltpu.CompilerParams(
            collective_id=6, has_side_effects=True, vmem_limit_bytes=60 * 2**20
        ),
        cost_estimate=pl.CostEstimate(
            flops=2 * length * depth * (width + units),
            bytes_accessed=200 * 2**20,
            transcendentals=0,
        ),
        name="attention_back",
    )(
        d_attn, attn_low, queries, key_rows, values, attended, log_totals, cos_tile, sine_tile,
        starts, middle, hidden, mlp_low
    )


def turn_into(target, source):
    @pl.loop(0, source.shape[0] // TILE)
    def _(block):
        at = pl.ds(pl.multiple_of(block * TILE, TILE), TILE)
        for k in range(source.shape[1] // TILE):
            columns = slice(k * TILE, (k + 1) * TILE)
            target[columns, at] = source[at, columns].astype(jnp.float32).T.astype(jnp.bfloat16)


def mlp_kernel(second_in, cotangent, weights, hidden, d_gate, d_up, grads, second_turned, cot_turned):
    @pl.when(pl.program_id(0) == 0)
    def _():
        turn_into(second_turned, second_in)
        turn_into(cot_turned, cotangent)

    for block in range(second_in.shape[0] // QUERIES):
        at = slice(block * QUERIES, (block + 1) * QUERIES)
        source = second_in[at, :]
        gate_proj = jnp.dot(source, weights[0], preferred_element_type=jnp.float32)
        up_proj = jnp.dot(source, weights[1], preferred_element_type=jnp.float32)
        d_hidden = jnp.dot(cotangent[at, :], weights[2], preferred_element_type=jnp.float32)
        sigmoid_gate = jax.nn.sigmoid(gate_proj)
        silu = gate_proj * sigmoid_gate
        hidden[at, :] = (silu * up_proj).astype(jnp.bfloat16)
        slope = sigmoid_gate * (1.0 + gate_proj * (1.0 - sigmoid_gate))
        d_gate[at, :] = (d_hidden * up_proj * slope).astype(jnp.bfloat16)
        d_up[at, :] = (d_hidden * silu).astype(jnp.bfloat16)
    for which, (left, right) in enumerate(
        ((second_turned, d_gate), (second_turned, d_up), (cot_turned, hidden))
    ):

        @pl.loop(0, left.shape[0] // 512)
        def _(block):
            at = pl.ds(pl.multiple_of(block * 512, 512), 512)
            grads[which, at, :] = jnp.dot(
                left[at, :], right[...], preferred_element_type=jnp.float32
            ).astype(jnp.bfloat16)


def mlp_middle(second_in, cotangent, weights):
    length, depth = second_in.shape
    units = weights.shape[2]
    tile = 256
    wide = jax.ShapeDtypeStruct((length, units), jnp.bfloat16)
    column = pl.BlockSpec((length, tile), lambda j: (0, j))
    stacked = pl.BlockSpec((3, depth, tile), lambda j: (0, 0, j))
    return pl.pallas_call(
        mlp_kernel,
        grid=(units // tile,),
        out_shape=[wide, wide, wide, jax.ShapeDtypeStruct((3, depth, units), jnp.bfloat16)],
        in_specs=whole_part(2) + [stacked],
        out_specs=[column, column, column, stacked],
        scratch_shapes=[pltpu.VMEM((depth, length), jnp.bfloat16)] * 2,
        compiler_params=pltpu.CompilerParams(vmem_limit_bytes=60 * 2**20),
        cost_estimate=pl.CostEstimate(
            flops=12 * length * depth * units, bytes_accessed=60 * 2**20, transcendentals=0
        ),
        name="mlp_middle",
    )(second_in, cotangent, weights)


def grads_kernel(first_in, query_raw, key_raw, value_raw, d_attn, attended, grads, turned_rows):
    which = pl.program_id(0)
    pl.when(which == 0)(lambda: turn_into(turned_rows, first_in))
    pl.when(which == 3)(lambda: turn_into(turned_rows, d_attn))
    for k, right in enumerate((query_raw, key_raw, value_raw, attended)):

        @pl.when(which == k)
        def _():
            @pl.loop(0, turned_rows.shape[0] // 512)
            def _(block):
                at = pl.ds(pl.multiple_of(block * 512, 512), 512)
                grads[at, :] = jnp.dot(
                    turned_rows[at, :], right[...], preferred_element_type=jnp.float32
                ).astype(jnp.bfloat16)


def attention_grads(first_in, query_raw, key_raw, value_raw, d_attn, attended):
    length, depth = first_in.shape
    width = attended.shape[1]
    return pl.pallas_call(
        grads_kernel,
        grid=(4,),
        out_shape=jax.ShapeDtypeStruct((4, depth, width), jnp.bfloat16),
        in_specs=whole_part(6),
        out_specs=pl.BlockSpec((None, depth, width), lambda j: (j, 0, 0)),
        scratch_shapes=[pltpu.VMEM((depth, length), jnp.bfloat16)],
        compiler_params=pltpu.CompilerParams(vmem_limit_bytes=60 * 2**20),
        cost_estimate=pl.CostEstimate(
            flops=8 * length * depth * width, bytes_accessed=20 * 2**20, transcendentals=0
        ),
        name="attention_grads",
    )(first_in, query_raw, key_raw, value_raw, d_attn, attended)


def attn_rates():
    return jnp.array([1.0, 1.0, 1.0, 8.0**0.5], jnp.float32).reshape(4, 1, 1) * (0.5 * D ** (-0.5))


def adam_update(weight, gradient, moment_one, moment_two, step_rate):
    first_new = BETA_ONE * moment_one + (1.0 - BETA_ONE) * gradient
    second_new = BETA_TWO * moment_two + (1.0 - BETA_TWO) * gradient * gradient
    fix_one = 1.0 - BETA_ONE**STEP
    fix_two = 1.0 - BETA_TWO**STEP
    weight_new = weight - step_rate * (
        first_new / fix_one / (jnp.sqrt(second_new / fix_two) + EPS_ADAM) + WEIGHT_DECAY * weight
    )
    return (first_new, second_new, weight_new)


def local(
    inputs,
    cotangent,
    doc_lengths,
    norm_gains,
    attn_weight,
    mlp_weight,
    gain_first,
    attn_first,
    mlp_first,
    gain_second,
    attn_second,
    mlp_second,
):
    row_count = inputs.shape[0]
    seq_length = row_count * lax.axis_size("tensor")
    segment, position = doc_layout(doc_lengths[0], seq_length)
    cos_tile, sine_tile = rope_tables(position)
    starts = (jnp.arange(seq_length, dtype=jnp.int32) - position)[None, :]
    width = inputs.shape[1]
    rows_f32 = jax.ShapeDtypeStruct((row_count, width), jnp.float32)
    gain_f32 = jax.ShapeDtypeStruct((8, width), jnp.float32)
    exchange = functools.partial(line_exchange, rows=row_count, width=width)
    (first_in,) = exchange(
        "first_norm", 1, [], [inputs, norm_gains], [], finish=first_norm, gathers=True, parts=1
    )
    attn_low = lax.all_gather(attn_weight.astype(jnp.bfloat16), "dp", axis=1, tiled=True)

    queries, key_rows, values, attended, log_totals, grad_out = attention_forward(
        first_in, attn_low, cos_tile, sine_tile, starts, cotangent
    )
    middle, second_in = exchange(
        "attention_out",
        2,
        [(attended, attn_low, 3)],
        [inputs, norm_gains],
        [rows_f32],
        finish=second_norm,
        gathers=True,
        parts=2,
    )
    mlp_low = lax.all_gather(mlp_weight.astype(jnp.bfloat16), "dp", axis=1, tiled=True)
    hidden, d_gate, d_up, mlp_sums = mlp_middle(second_in, grad_out, mlp_low)

    def to_owner(partial):
        return lax.psum_scatter(partial, "dp", scatter_dimension=1, tiled=True).astype(jnp.float32)

    mlp_grad = to_owner(mlp_sums)
    d_middle, gain_two, d_attn = exchange(
        "mlp_back",
        3,
        [(d_gate, mlp_low, 0), (d_up, mlp_low, 1)],
        [middle, cotangent, norm_gains],
        [rows_f32, gain_f32],
        finish=second_back,
        gathers=True,
        parts=2,
    )
    query_raw, key_raw, value_raw, layer_out = attention_back(
        d_attn,
        attn_low,
        queries,
        key_rows,
        values,
        attended,
        log_totals,
        cos_tile,
        sine_tile,
        starts,
        middle,
        hidden,
        mlp_low,
    )
    attn_sums, mlp_grad = lax.optimization_barrier(
        (attention_grads(first_in, query_raw, key_raw, value_raw, d_attn, attended), mlp_grad)
    )
    attn_grad = to_owner(attn_sums)
    grad_in, gain_one = exchange(
        "input_back",
        4,
        [(query_raw, attn_low, 0), (key_raw, attn_low, 1), (value_raw, attn_low, 2)],
        [inputs, d_middle, norm_gains],
        [rows_f32, gain_f32],
        finish=first_back,
        gathers=False,
        parts=1,
    )
    gain_parts = jnp.stack([jnp.sum(gain_one, axis=0), jnp.sum(gain_two, axis=0)])
    gain_grad = sum_everywhere(gain_parts.reshape(8, -1)).reshape(norm_gains.shape)
    gain_first_new, gain_second_new, gain_new = adam_update(
        norm_gains, gain_grad, gain_first, gain_second, GAIN_RATE
    )
    attn_first_new, attn_second_new, attn_new = adam_update(
        attn_weight, attn_grad, attn_first, attn_second, attn_rates()
    )
    mlp_first_new, mlp_second_new, mlp_new = adam_update(
        mlp_weight, mlp_grad, mlp_first, mlp_second, 0.5 * D ** (-0.5)
    )
    return (
        layer_out,
        grad_in,
        gain_grad,
        attn_grad,
        mlp_grad,
        gain_first_new,
        attn_first_new,
        mlp_first_new,
        gain_second_new,
        attn_second_new,
        mlp_second_new,
        gain_new,
        attn_new,
        mlp_new,
    )


def solution(mesh):
    placed = (
        P(("dp", "tensor"), None),
        P(("dp", "tensor"), None),
        P("dp", None),
        P(),
        P(None, "dp", "tensor"),
        P(None, "dp", "tensor"),
        P(),
        P(None, "dp", "tensor"),
        P(None, "dp", "tensor"),
        P(),
        P(None, "dp", "tensor"),
        P(None, "dp", "tensor"),
    )
    return jax.shard_map(
        local,
        mesh=mesh,
        in_specs=placed,
        out_specs=(
            P(("dp", "tensor"), None),
            P(("dp", "tensor"), None),
            P(),
            P(None, "dp", "tensor"),
            P(None, "dp", "tensor"),
            P(),
            P(None, "dp", "tensor"),
            P(None, "dp", "tensor"),
            P(),
            P(None, "dp", "tensor"),
            P(None, "dp", "tensor"),
            P(),
            P(None, "dp", "tensor"),
            P(None, "dp", "tensor"),
        ),
        check_vma=False,
    )
```

```python
import functools

import jax
import jax.numpy as jnp
from jax import lax
from jax.experimental import pallas as pl
from jax.experimental.pallas import tpu as pltpu
from jax.sharding import PartitionSpec as P

D = 2048
HEAD_DIM = 64
STEP = 10


EPS_NORM = 1e-05
ROPE_BASE = 130000.0
BETA_ONE = 0.9
BETA_TWO = 0.95
EPS_ADAM = 1e-08
WEIGHT_DECAY = 0.1
GAIN_RATE = 0.3
MASKED = -1e30


def doc_layout(lengths, seq_length):
    doc_ends = jnp.cumsum(lengths)
    starts = doc_ends - lengths
    places = jnp.arange(seq_length, dtype=jnp.int32)
    segment = jnp.sum((places[:, None] >= doc_ends[None, :]).astype(jnp.int32), axis=1)
    owners = segment[:, None] == jnp.arange(lengths.shape[0], dtype=jnp.int32)[None, :]
    position = places - jnp.sum(jnp.where(owners, starts[None, :], 0), axis=1)
    return (segment, position)


def rope_tables(position):
    half_dim = HEAD_DIM // 2
    frequencies = jnp.power(
        jnp.float32(ROPE_BASE), -2.0 * jnp.arange(half_dim, dtype=jnp.float32) / HEAD_DIM
    )
    angles = position.astype(jnp.float32)[:, None] * frequencies[None, :]
    cosine, sine = jnp.cos(angles), jnp.sin(angles)
    return (
        jnp.concatenate([cosine, cosine] * 2, axis=1),
        jnp.concatenate([-sine, sine] * 2, axis=1),
    )


MESH = pl.DeviceIdType.MESH
BLOCK = 32
TILE = 256


def whole_part(count):
    return [pl.BlockSpec(memory_space=pltpu.VMEM)] * count


def greet(n, me):
    barrier = pltpu.get_barrier_semaphore()
    for there, step in ((me > 0, -1), (me < n - 1, 1)):

        @pl.when(there)
        def _():
            pl.semaphore_signal(barrier, inc=1, device_id={"tensor": me + step}, device_id_type=MESH)

    pl.semaphore_wait(barrier, (me > 0).astype(jnp.int32) + (me < n - 1).astype(jnp.int32))


def blocks_of(count, body):
    @pl.loop(0, count // BLOCK)
    def _(block):
        body(pl.multiple_of(block * BLOCK, BLOCK))


class RowGather:
    def __init__(self, n, me, parts, place, sent, got):
        self.n, self.me, self.parts, self.place = n, me, parts, place
        self.sent, self.got = sent, got
        self.rows = place.shape[0] // n
        self.has_left, self.has_right = me > 0, me < n - 1

    def copy(self, way, part, hop, owner):
        count = self.rows // self.parts
        first = pl.multiple_of(owner * self.rows + part * count, count)
        block = self.place.at[pl.ds(first, count), :]
        slot = part * (self.n - 1) + hop
        return pltpu.make_async_remote_copy(
            src_ref=block,
            dst_ref=block,
            send_sem=self.sent.at[way, slot],
            recv_sem=self.got.at[way, slot],
            device_id={"tensor": self.me + 1 - 2 * way},
            device_id_type=MESH,
        )

    def start(self, part):
        pl.when(self.has_right)(lambda: self.copy(0, part, 0, self.me).start())
        pl.when(self.has_left)(lambda: self.copy(1, part, 0, self.me).start())

    def step(self, part, hop):
        last = hop + 1 == self.n - 1

        @pl.when(hop < self.me)
        def _():
            owner = self.me - 1 - hop
            self.copy(0, part, hop, owner).wait_recv()
            if not last:
                pl.when(self.has_right)(lambda: self.copy(0, part, hop + 1, owner).start())

        @pl.when(hop < self.n - 1 - self.me)
        def _():
            owner = self.me + 1 + hop
            self.copy(1, part, hop, owner).wait_recv()
            if not last:
                pl.when(self.has_left)(lambda: self.copy(1, part, hop + 1, owner).start())

    def drain(self):
        for part in range(self.parts):
            for hop in range(self.n - 1):
                pl.when(self.has_right & (hop <= self.me))(
                    lambda: self.copy(0, part, hop, self.me - hop).wait_send()
                )
                pl.when(self.has_left & (hop <= self.n - 1 - self.me))(
                    lambda: self.copy(1, part, hop, self.me + hop).wait_send()
                )


class SumScatter:
    def __init__(self, n, me, parts, lefts, rights, totals, run, sent, got):
        self.n, self.me, self.parts = n, me, parts
        self.lefts, self.rights, self.totals, self.run = lefts, rights, totals, run
        self.sent, self.got = sent, got
        self.rows = totals.shape[1]
        self.fed = (me > 0, me < n - 1)

    def copy(self, way, part, hop):
        slot = part * (self.n - 1) + hop
        run = self.run.at[self.place(way, part, hop)]
        return pltpu.make_async_remote_copy(
            src_ref=run,
            dst_ref=run,
            send_sem=self.sent.at[way, slot],
            recv_sem=self.got.at[way, slot],
            device_id={"tensor": self.me + 1 - 2 * way},
            device_id_type=MESH,
        )

    def product(self, dest):
        first = pl.multiple_of(dest * self.rows, self.rows)

        @pl.loop(0, self.totals.shape[2] // TILE)
        def _(tile):
            columns = pl.ds(pl.multiple_of(tile * TILE, TILE), TILE)
            value = None
            for left, right in zip(self.lefts, self.rights):
                term = lax.dot_general(
                    left[pl.ds(first, self.rows), :],
                    right[columns, :],
                    (((1,), (1,)), ((), ())),
                    preferred_element_type=jnp.float32,
                )
                value = term if value is None else value + term
            self.totals[dest, :, columns] = value.astype(self.totals.dtype)

    def place(self, way, part, hop):
        return part * (self.n + 1) + (hop, self.n - hop)[way]

    def begin(self):
        for hop in range(self.n - 1):
            for way, dest in ((0, self.n - 1 - hop), (1, hop)):
                needed = (dest > self.me, dest < self.me)[way]
                run = self.run
                pl.when(needed)(lambda: self.product(dest))

                @pl.when(needed & jnp.logical_not(self.fed[way]))
                def _():
                    for part in range(self.parts):
                        first = part * (self.rows // self.parts)
                        slot = self.place(way, part, hop)

                        def body(at):
                            own = self.totals[dest, pl.ds(first + at, BLOCK), :]
                            run[slot, pl.ds(at, BLOCK), :] = own.astype(jnp.bfloat16)

                        blocks_of(self.rows // self.parts, body)
                        self.copy(way, part, hop).start()

        self.product(self.me)

    def arrivals(self, count):
        for way, behind in ((0, self.me), (1, self.n - 1 - self.me)):
            hop = count - behind
            yield way, hop, (self.n - 1 - hop, hop)[way], self.fed[way] & (hop >= 0)

    def pass_on(self, part, count):
        for way, hop, dest, there in self.arrivals(count):
            run, slot = self.run, self.place(way, part, hop)
            first = part * (self.rows // self.parts)

            @pl.when(there)
            def _():
                self.copy(way, part, hop).wait_recv()

                def body(at):
                    own = self.totals[dest, pl.ds(first + at, BLOCK), :].astype(jnp.float32)
                    came = run[slot, pl.ds(at, BLOCK), :].astype(jnp.float32)
                    run[slot, pl.ds(at, BLOCK), :] = (own + came).astype(jnp.bfloat16)

                blocks_of(self.rows // self.parts, body)
                self.copy(way, part, hop).start()

    def last(self, part):
        first = part * (self.rows // self.parts)
        for way, hop, dest, there in self.arrivals(self.n - 1):
            run, slot = self.run, self.place(way, part, hop)

            @pl.when(there)
            def _():
                self.copy(way, part, hop).wait_recv()

                def body(at):
                    own = pl.ds(first + at, BLOCK)
                    came = run[slot, pl.ds(at, BLOCK), :].astype(jnp.float32)
                    total = self.totals[self.me, own, :].astype(jnp.float32) + came
                    self.totals[self.me, own, :] = total.astype(self.totals.dtype)

                blocks_of(self.rows // self.parts, body)

    def drain(self):
        for part in range(self.parts):
            for hop in range(self.n - 1):
                pl.when(self.n - 1 - hop > self.me)(lambda: self.copy(0, part, hop).wait_send())
                pl.when(hop < self.me)(lambda: self.copy(1, part, hop).wait_send())


def scatter_scratch(n, parts, rows, width):
    slots = parts * (n - 1)
    kept = jnp.float32 if n * rows * width <= 2**21 else jnp.bfloat16
    return [
        pltpu.VMEM((n, rows, width), kept),
        pltpu.VMEM((parts * (n + 1), rows // parts, width), jnp.bfloat16),
        pltpu.SemaphoreType.DMA((2, slots)),
        pltpu.SemaphoreType.DMA((2, slots)),
    ]


def gather_scratch(n, parts):
    return [pltpu.SemaphoreType.DMA((2, parts * (n - 1)))] * 2


class SideProduct:
    def __init__(self, source, columns, target, held, weight, staged, sems):
        self.source, self.columns, self.target = source, columns, target
        self.held, self.weight, self.staged, self.sems = held, weight, staged, sems
        self.count = source.shape[0] // QUERIES
        self.done = 0

    def fetch(self, block):
        return pltpu.make_async_copy(
            self.source.at[pl.ds(block * QUERIES, QUERIES), :],
            self.held.at[block % 2],
            self.sems.at[block % 2],
        )

    def store(self, block):
        return pltpu.make_async_copy(
            self.staged.at[block % 2],
            self.target.at[pl.ds(block * QUERIES, QUERIES), :],
            self.sems.at[2 + block % 2],
        )

    def fetch_weight(self):
        return pltpu.make_async_copy(self.columns.at[2], self.weight, self.sems.at[4])

    def open(self, lefts):
        self.fetch_weight().start()
        self.fetch(0).start()

    def step(self):
        block = self.done
        if block == self.count:
            return
        if block == 0:
            self.fetch_weight().wait()
        self.fetch(block).wait()
        if block + 1 < self.count:
            self.fetch(block + 1).start()
        if block >= 2:
            self.store(block - 2).wait()

        @pl.loop(0, self.weight.shape[0] // TILE)
        def _(tile):
            columns = pl.ds(pl.multiple_of(tile * TILE, TILE), TILE)
            self.staged[block % 2, :, columns] = over_lanes(
                self.held[block % 2], self.weight[columns, :]
            ).astype(jnp.bfloat16)

        self.store(block).start()
        self.done = block + 1

    def close(self):
        while self.done < self.count:
            self.step()
        for block in range(max(0, self.count - 2), self.count):
            self.store(block).wait()


def side_scratch(depth, units):
    return [
        pltpu.VMEM((2, QUERIES, units), jnp.bfloat16),
        pltpu.VMEM((depth, units), jnp.bfloat16),
        pltpu.VMEM((2, QUERIES, depth), jnp.bfloat16),
        pltpu.SemaphoreType.DMA((5,)),
    ]


def line_kernel(n, parts, products, extras, outs, gathers, side, finish, *refs):
    refs = list(refs)
    take = lambda count: [refs.pop(0) for _ in range(count)]
    lefts, rights, more = take(products), take(products), take(extras)
    side_in = take(2) if side else None
    results = take(outs)
    gathered = take(1)[0] if gathers else None
    filler = SideProduct(*side_in, *take(1), *[refs.pop() for _ in range(4)][::-1]) if side else None
    me = lax.axis_index("tensor")
    if products:
        totals = refs[0]
        sums = SumScatter(n, me, parts, lefts, rights, *take(4))
    if gathers:
        gather = RowGather(n, me, parts, gathered, *take(2))
    rows = totals.shape[1] if products else gathered.shape[0] // n
    part_rows = rows // parts

    def finish_part(part):
        def body(block):
            at = pl.multiple_of(part * part_rows + block, BLOCK)
            total = totals[me, pl.ds(at, BLOCK), :].astype(jnp.float32) if products else None
            sent_rows = finish(at, total, more, results)
            if gathers:
                gathered[pl.ds(pl.multiple_of(me * rows + at, BLOCK), BLOCK), :] = sent_rows

        blocks_of(part_rows, body)

    greet(n, me)
    for result in results:
        if result.shape[0] == 8:
            result[...] = jnp.zeros_like(result)
    if products:
        sums.begin()
    if filler:
        filler.open(lefts)
    for part in range(parts):
        for hop in range(n - 1):
            if filler:
                filler.step()
            if products and hop < n - 2:
                sums.pass_on(part, hop + 1)
            if products and hop == n - 2:
                sums.last(part)
            if gathers and part > 0:
                gather.step(part - 1, hop)
        finish_part(part)
        if gathers:
            gather.start(part)
    if gathers:
        for hop in range(n - 1):
            if filler:
                filler.step()
            gather.step(parts - 1, hop)
        gather.drain()
    if filler:
        filler.close()
    if products:
        sums.drain()


def line_exchange(
    name, collective_id, pairs, extras, outs, rows, width, finish, gathers, parts, side=()
):
    n = lax.axis_size("tensor")
    scratch = scatter_scratch(n, parts, rows, width) if pairs else []
    if gathers:
        scratch = scratch + gather_scratch(n, parts)
        outs = outs + [jax.ShapeDtypeStruct((n * rows, width), jnp.bfloat16)]
    operands = [pair[0] for pair in pairs] + [pair[1] for pair in pairs] + list(extras)
    specs = whole_part(len(operands)) + [pl.BlockSpec(memory_space=pl.ANY)] * len(side)
    own_outs = len(outs) - gathers
    out_specs = whole_part(len(outs))
    operands = operands + list(side)
    if side:
        outs = outs + [jax.ShapeDtypeStruct((side[0].shape[0], width), jnp.bfloat16)]
        out_specs = out_specs + [pl.BlockSpec(memory_space=pl.ANY)]
        scratch = scratch + side_scratch(width, side[0].shape[1])
    for k, (left, right, which) in enumerate(pairs):
        specs[len(pairs) + k] = pl.BlockSpec(
            (None, *right.shape[1:]), lambda i, which=which: (which, 0, 0), pipeline_mode=pl.Buffered(1)
        )
    depth = sum(pair[0].shape[1] for pair in pairs)
    return pl.pallas_call(
        functools.partial(
            line_kernel, n, parts, len(pairs), len(extras), own_outs, gathers, len(side) > 0, finish
        ),
        grid=(1,),
        out_shape=outs,
        in_specs=specs,
        out_specs=out_specs,
        scratch_shapes=scratch,
        compiler_params=pltpu.CompilerParams(
            collective_id=collective_id, has_side_effects=True, vmem_limit_bytes=60 * 2**20
        ),
        cost_estimate=pl.CostEstimate(
            flops=2 * n * rows * width * max(depth, 1),
            bytes_accessed=200 * 2**20,
            transcendentals=0,
        ),
        name=name,
    )(*operands)


def everywhere_kernel(sizes, field, result, came, sent, got):
    places = [lax.axis_index(name) for name in sizes]
    partners = []
    for name, place in zip(sizes, places):
        stride = 1
        while stride < sizes[name]:
            other = place + stride - 2 * stride * (place // stride % 2)
            partners.append({name: other})
            stride = 2 * stride
    barrier = pltpu.get_barrier_semaphore()
    for partner in partners:
        pl.semaphore_signal(barrier, inc=1, device_id=partner, device_id_type=MESH)
    pl.semaphore_wait(barrier, len(partners))
    result[...] = field[...]
    for k, partner in enumerate(partners):
        came[2 * k] = result[...]
        copy = pltpu.make_async_remote_copy(
            src_ref=came.at[2 * k],
            dst_ref=came.at[2 * k + 1],
            send_sem=sent.at[k],
            recv_sem=got.at[k],
            device_id=partner,
            device_id_type=MESH,
        )
        copy.start()
        copy.wait()
        result[...] = result[...] + came[2 * k + 1]


def sum_everywhere(field):
    sizes = {name: lax.axis_size(name) for name in ("dp", "tensor")}
    steps = sum(size.bit_length() - 1 for size in sizes.values())
    return pl.pallas_call(
        functools.partial(everywhere_kernel, sizes),
        out_shape=jax.ShapeDtypeStruct(field.shape, jnp.float32),
        in_specs=whole_part(1),
        out_specs=pl.BlockSpec(memory_space=pltpu.VMEM),
        scratch_shapes=[
            pltpu.VMEM((2 * steps, *field.shape), jnp.float32),
            pltpu.SemaphoreType.DMA((steps,)),
            pltpu.SemaphoreType.DMA((steps,)),
        ],
        compiler_params=pltpu.CompilerParams(collective_id=7, has_side_effects=True),
        name="gain_sum",
    )(field)


def inverse_scale(field):
    return lax.rsqrt(jnp.mean(field * field, axis=-1, keepdims=True) + EPS_NORM)


def first_norm(at, total, more, results):
    layer_in, gains = more
    field = layer_in[pl.ds(at, BLOCK), :].astype(jnp.float32)
    return (field * inverse_scale(field) * gains[0:1, :]).astype(jnp.bfloat16)


def second_norm(at, total, more, results):
    layer_in, gains = more
    field = layer_in[pl.ds(at, BLOCK), :].astype(jnp.float32) + total
    results[0][pl.ds(at, BLOCK), :] = field
    return (field * inverse_scale(field) * gains[1:2, :]).astype(jnp.bfloat16)


def norm_back(field, gradient, gain_row, gain_out):
    inv_scale = inverse_scale(field)
    normed = field * inv_scale
    scaled = gradient * gain_row
    back = inv_scale * (scaled - normed * jnp.mean(scaled * normed, axis=-1, keepdims=True))
    product = gradient * normed
    folded = product[0:8]
    for k in range(8, BLOCK, 8):
        folded = folded + product[k : k + 8]
    gain_out[...] = gain_out[...] + folded
    return back


def second_back(at, total, more, results):
    middle, cotangent, gains = more
    rows = pl.ds(at, BLOCK)
    back = norm_back(middle[rows, :], total, gains[1:2, :], results[1])
    back = back + cotangent[rows, :].astype(jnp.float32)
    results[0][rows, :] = back
    return back.astype(jnp.bfloat16)


def first_back(at, total, more, results):
    layer_in, d_middle, gains = more
    rows = pl.ds(at, BLOCK)
    back = norm_back(layer_in[rows, :].astype(jnp.float32), total, gains[0:1, :], results[1])
    results[0][rows, :] = back + d_middle[rows, :]


PAIR = 2 * HEAD_DIM
QUERIES = 256


def turned(field, cos_tile, sine_tile):
    lanes = lax.broadcasted_iota(jnp.int32, field.shape, 1)
    ahead = pltpu.roll(field, PAIR - HEAD_DIM // 2, 1)
    behind = pltpu.roll(field, HEAD_DIM // 2, 1)
    partner = jnp.where(lanes % HEAD_DIM < HEAD_DIM // 2, ahead, behind)
    return field * cos_tile + partner * sine_tile


def one_head(tile, head):
    lanes = lax.broadcasted_iota(jnp.int32, tile.shape, 1)
    return jnp.where(lanes // HEAD_DIM == head, tile, jnp.zeros_like(tile))


def over_lanes(left, right):
    return lax.dot_general(
        left, right, (((1,), (1,)), ((), ())), preferred_element_type=jnp.float32
    )


def masked(scores, starts, first_query):
    keys = lax.broadcasted_iota(jnp.int32, scores.shape, 0)
    queries = first_query + lax.broadcasted_iota(jnp.int32, scores.shape, 1)
    return jnp.where((keys >= starts) & (keys <= queries), scores, MASKED)


def attention_forward_kernel(
    first_in, weights, cos_ref, sine_ref, starts_ref,
    queries, key_rows, values, attended, log_totals, turned_values
):
    length, width = queries.shape

    @pl.loop(0, length // QUERIES)
    def _(block):
        at = pl.ds(pl.multiple_of(block * QUERIES, QUERIES), QUERIES)
        source = first_in[at, :]
        cos_tile, sine_tile = cos_ref[at, :], sine_ref[at, :]
        for which, target in enumerate((queries, key_rows, values)):
            field = jnp.dot(source, weights[which], preferred_element_type=jnp.float32)
            for pair in range(width // PAIR):
                tile = field[:, pair * PAIR : (pair + 1) * PAIR]
                if which < 2:
                    tile = turned(tile, cos_tile, sine_tile)
                if which == 0:
                    tile = tile.astype(jnp.bfloat16) * HEAD_DIM ** (-0.5)
                target[at, pair * PAIR : (pair + 1) * PAIR] = tile.astype(jnp.bfloat16)

    @pl.loop(0, width // PAIR)
    def _(pair):
        lanes = pl.ds(pl.multiple_of(pair * PAIR, PAIR), PAIR)
        turned_values[...] = values[:, lanes].astype(jnp.float32).T.astype(jnp.bfloat16)
        for block in range(length // QUERIES):
            at = pl.ds(block * QUERIES, QUERIES)
            reach = (block + 1) * QUERIES
            starts = starts_ref[:, at]
            both = []
            for head in range(2):
                query = one_head(queries[at, lanes], head)
                scores = masked(
                    over_lanes(key_rows[0:reach, lanes], query), starts, block * QUERIES
                )
                peak = jnp.max(scores, axis=0, keepdims=True)
                raised = jnp.exp(scores - peak)
                total = jnp.sum(raised, axis=0, keepdims=True)
                result = jnp.dot(
                    turned_values[head * HEAD_DIM : (head + 1) * HEAD_DIM, 0:reach],
                    raised.astype(jnp.bfloat16),
                    preferred_element_type=jnp.float32,
                )
                both.append(result / total)
                log_totals[2 * pair + head, :, at] = peak + jnp.log(total)
            attended[at, lanes] = jnp.concatenate(both, axis=0).T.astype(jnp.bfloat16)


def attention_forward(first_in, weights, cos_tile, sine_tile, starts):
    length, depth = first_in.shape
    width = weights.shape[2]
    narrow = jax.ShapeDtypeStruct((length, width), jnp.bfloat16)
    outs = [
        narrow,
        narrow,
        narrow,
        narrow,
        jax.ShapeDtypeStruct((width // HEAD_DIM, 1, length), jnp.float32),
    ]
    specs = whole_part(5)
    specs[1] = pl.BlockSpec((3, depth, width), lambda i: (0, 0, 0), pipeline_mode=pl.Buffered(1))
    return pl.pallas_call(
        attention_forward_kernel,
        grid=(1,),
        out_shape=outs,
        in_specs=specs,
        out_specs=whole_part(len(outs)),
        scratch_shapes=[pltpu.VMEM((PAIR, length), jnp.bfloat16)],
        compiler_params=pltpu.CompilerParams(vmem_limit_bytes=60 * 2**20),
        cost_estimate=pl.CostEstimate(
            flops=6 * length * depth * width, bytes_accessed=100 * 2**20, transcendentals=0
        ),
        name="attention_forward",
    )(first_in, weights, cos_tile, sine_tile, starts)


def attention_back_kernel(
    d_attn, out_weight, queries, key_rows, values, attended, log_totals, cos_ref, sine_ref,
    starts_ref, query_raw, key_raw, value_raw,
    d_attended, turned_keys, key_sum, value_sum, held, held_sems
):
    length, width = queries.shape

    def fetch(block):
        return pltpu.make_async_copy(
            d_attn.at[pl.ds(block * QUERIES, QUERIES), :], held.at[block % 2], held_sems.at[block % 2]
        )

    fetch(0).start()
    for block in range(length // QUERIES):
        fetch(block).wait()
        if (block + 1) * QUERIES < length:
            fetch(block + 1).start()
        d_attended[block * QUERIES : (block + 1) * QUERIES, :] = jnp.dot(
            held[block % 2], out_weight[0], preferred_element_type=jnp.float32
        ).astype(jnp.bfloat16)

    @pl.loop(0, width // PAIR)
    def _(pair):
        lanes = pl.ds(pl.multiple_of(pair * PAIR, PAIR), PAIR)
        turned_keys[...] = key_rows[:, lanes].astype(jnp.float32).T.astype(jnp.bfloat16)
        key_sum[...] = jnp.zeros_like(key_sum)
        value_sum[...] = jnp.zeros_like(value_sum)
        for block in range(length // QUERIES):
            at = pl.ds(block * QUERIES, QUERIES)
            reach = (block + 1) * QUERIES
            starts = starts_ref[:, at]
            grads = d_attended[at, lanes]
            shares = (grads.astype(jnp.float32) * attended[at, lanes].astype(jnp.float32)).T
            both = []
            for head in range(2):
                heads = slice(head * HEAD_DIM, (head + 1) * HEAD_DIM)
                query = one_head(queries[at, lanes], head)
                grad = one_head(grads, head)
                share = jnp.sum(shares[heads], axis=0, keepdims=True)
                scores = masked(
                    over_lanes(key_rows[0:reach, lanes], query), starts, block * QUERIES
                )
                probs = jnp.exp(scores - log_totals[2 * pair + head, :, at])
                prob_grad = over_lanes(values[0:reach, lanes], grad)
                score_grad = (probs * (prob_grad - share)).astype(jnp.bfloat16)
                value_sum[0:reach, :] = value_sum[0:reach, :] + jnp.dot(
                    probs.astype(jnp.bfloat16), grad, preferred_element_type=jnp.float32
                )
                key_sum[0:reach, :] = key_sum[0:reach, :] + jnp.dot(
                    score_grad, query, preferred_element_type=jnp.float32
                )
                both.append(
                    jnp.dot(
                        turned_keys[heads, 0:reach], score_grad, preferred_element_type=jnp.float32
                    )
                )
            query_grad = jnp.concatenate(both, axis=0).T * HEAD_DIM ** (-0.5)
            query_raw[at, lanes] = turned(query_grad, cos_ref[at, :], -sine_ref[at, :]).astype(
                jnp.bfloat16
            )
        key_raw[:, lanes] = turned(key_sum[...], cos_ref[...], -sine_ref[...]).astype(jnp.bfloat16)
        value_raw[:, lanes] = value_sum[...].astype(jnp.bfloat16)


def attention_back(
    d_attn, attn_low, queries, key_rows, values, attended, log_totals, cos_tile, sine_tile, starts
):
    length, depth = d_attn.shape
    width = queries.shape[1]
    narrow = jax.ShapeDtypeStruct((length, width), jnp.bfloat16)
    specs = whole_part(10)
    specs[0] = pl.BlockSpec(memory_space=pl.ANY)
    specs[1] = pl.BlockSpec(
        (1, depth, width), lambda i: (3, 0, 0), pipeline_mode=pl.Buffered(1)
    )
    return pl.pallas_call(
        attention_back_kernel,
        grid=(1,),
        out_shape=[narrow, narrow, narrow],
        in_specs=specs,
        out_specs=whole_part(3),
        scratch_shapes=[
            pltpu.VMEM((length, width), jnp.bfloat16),
            pltpu.VMEM((PAIR, length), jnp.bfloat16),
            pltpu.VMEM((length, PAIR), jnp.float32),
            pltpu.VMEM((length, PAIR), jnp.float32),
            pltpu.VMEM((2, QUERIES, depth), jnp.bfloat16),
            pltpu.SemaphoreType.DMA((2,)),
        ],
        compiler_params=pltpu.CompilerParams(vmem_limit_bytes=60 * 2**20),
        cost_estimate=pl.CostEstimate(
            flops=2 * length * depth * width, bytes_accessed=120 * 2**20, transcendentals=0
        ),
        name="attention_back",
    )(
        d_attn, attn_low, queries, key_rows, values, attended, log_totals, cos_tile, sine_tile,
        starts
    )


def turn_into(target, source):
    @pl.loop(0, source.shape[0] // TILE)
    def _(block):
        at = pl.ds(pl.multiple_of(block * TILE, TILE), TILE)
        for k in range(source.shape[1] // TILE):
            columns = slice(k * TILE, (k + 1) * TILE)
            target[columns, at] = source[at, columns].astype(jnp.float32).T.astype(jnp.bfloat16)


def mlp_kernel(second_in, cotangent, weights, hidden, d_gate, d_up, grads, second_turned, cot_turned):
    @pl.when(pl.program_id(0) == 0)
    def _():
        turn_into(second_turned, second_in)
        turn_into(cot_turned, cotangent)

    for block in range(second_in.shape[0] // QUERIES):
        at = slice(block * QUERIES, (block + 1) * QUERIES)
        source = second_in[at, :]
        gate_proj = jnp.dot(source, weights[0], preferred_element_type=jnp.float32)
        up_proj = jnp.dot(source, weights[1], preferred_element_type=jnp.float32)
        d_hidden = jnp.dot(cotangent[at, :], weights[2], preferred_element_type=jnp.float32)
        sigmoid_gate = jax.nn.sigmoid(gate_proj)
        silu = gate_proj * sigmoid_gate
        hidden[at, :] = (silu * up_proj).astype(jnp.bfloat16)
        slope = sigmoid_gate * (1.0 + gate_proj * (1.0 - sigmoid_gate))
        d_gate[at, :] = (d_hidden * up_proj * slope).astype(jnp.bfloat16)
        d_up[at, :] = (d_hidden * silu).astype(jnp.bfloat16)
    for which, (left, right) in enumerate(
        ((second_turned, d_gate), (second_turned, d_up), (cot_turned, hidden))
    ):

        @pl.loop(0, left.shape[0] // 512)
        def _(block):
            at = pl.ds(pl.multiple_of(block * 512, 512), 512)
            grads[which, at, :] = jnp.dot(
                left[at, :], right[...], preferred_element_type=jnp.float32
            ).astype(jnp.bfloat16)


def mlp_middle(second_in, cotangent, weights):
    length, depth = second_in.shape
    units = weights.shape[2]
    tile = 256
    wide = jax.ShapeDtypeStruct((length, units), jnp.bfloat16)
    column = pl.BlockSpec((length, tile), lambda j: (0, j))
    stacked = pl.BlockSpec((3, depth, tile), lambda j: (0, 0, j))
    return pl.pallas_call(
        mlp_kernel,
        grid=(units // tile,),
        out_shape=[wide, wide, wide, jax.ShapeDtypeStruct((3, depth, units), jnp.bfloat16)],
        in_specs=whole_part(2) + [stacked],
        out_specs=[column, column, column, stacked],
        scratch_shapes=[pltpu.VMEM((depth, length), jnp.bfloat16)] * 2,
        compiler_params=pltpu.CompilerParams(vmem_limit_bytes=60 * 2**20),
        cost_estimate=pl.CostEstimate(
            flops=12 * length * depth * units, bytes_accessed=60 * 2**20, transcendentals=0
        ),
        name="mlp_middle",
    )(second_in, cotangent, weights)


def grads_kernel(first_in, query_raw, key_raw, value_raw, d_attn, attended, grads, turned_rows):
    which = pl.program_id(0)
    pl.when(which == 0)(lambda: turn_into(turned_rows, first_in))
    pl.when(which == 3)(lambda: turn_into(turned_rows, d_attn))
    for k, right in enumerate((query_raw, key_raw, value_raw, attended)):

        @pl.when(which == k)
        def _():
            @pl.loop(0, turned_rows.shape[0] // 512)
            def _(block):
                at = pl.ds(pl.multiple_of(block * 512, 512), 512)
                grads[at, :] = jnp.dot(
                    turned_rows[at, :], right[...], preferred_element_type=jnp.float32
                ).astype(jnp.bfloat16)


def attention_grads(first_in, query_raw, key_raw, value_raw, d_attn, attended):
    length, depth = first_in.shape
    width = attended.shape[1]
    return pl.pallas_call(
        grads_kernel,
        grid=(4,),
        out_shape=jax.ShapeDtypeStruct((4, depth, width), jnp.bfloat16),
        in_specs=whole_part(6),
        out_specs=pl.BlockSpec((None, depth, width), lambda j: (j, 0, 0)),
        scratch_shapes=[pltpu.VMEM((depth, length), jnp.bfloat16)],
        compiler_params=pltpu.CompilerParams(vmem_limit_bytes=60 * 2**20),
        cost_estimate=pl.CostEstimate(
            flops=8 * length * depth * width, bytes_accessed=20 * 2**20, transcendentals=0
        ),
        name="attention_grads",
    )(first_in, query_raw, key_raw, value_raw, d_attn, attended)


def attn_rates():
    return jnp.array([1.0, 1.0, 1.0, 8.0**0.5], jnp.float32).reshape(4, 1, 1) * (0.5 * D ** (-0.5))


def adam_update(weight, gradient, moment_one, moment_two, step_rate):
    first_new = BETA_ONE * moment_one + (1.0 - BETA_ONE) * gradient
    second_new = BETA_TWO * moment_two + (1.0 - BETA_TWO) * gradient * gradient
    fix_one = 1.0 - BETA_ONE**STEP
    fix_two = 1.0 - BETA_TWO**STEP
    weight_new = weight - step_rate * (
        first_new / fix_one / (jnp.sqrt(second_new / fix_two) + EPS_ADAM) + WEIGHT_DECAY * weight
    )
    return (first_new, second_new, weight_new)


def local(
    inputs,
    cotangent,
    doc_lengths,
    norm_gains,
    attn_weight,
    mlp_weight,
    gain_first,
    attn_first,
    mlp_first,
    gain_second,
    attn_second,
    mlp_second,
):
    row_count = inputs.shape[0]
    seq_length = row_count * lax.axis_size("tensor")
    segment, position = doc_layout(doc_lengths[0], seq_length)
    cos_tile, sine_tile = rope_tables(position)
    starts = (jnp.arange(seq_length, dtype=jnp.int32) - position)[None, :]
    width = inputs.shape[1]
    rows_f32 = jax.ShapeDtypeStruct((row_count, width), jnp.float32)
    gain_f32 = jax.ShapeDtypeStruct((8, width), jnp.float32)
    exchange = functools.partial(line_exchange, rows=row_count, width=width)
    (first_in,) = exchange(
        "first_norm", 1, [], [inputs, norm_gains], [], finish=first_norm, gathers=True, parts=1
    )
    attn_low = lax.all_gather(attn_weight.astype(jnp.bfloat16), "dp", axis=1, tiled=True)

    grad_out = lax.all_gather(cotangent, "tensor", axis=0, tiled=True)
    queries, key_rows, values, attended, log_totals = attention_forward(
        first_in, attn_low, cos_tile, sine_tile, starts
    )
    middle, second_in = exchange(
        "attention_out",
        2,
        [(attended, attn_low, 3)],
        [inputs, norm_gains],
        [rows_f32],
        finish=second_norm,
        gathers=True,
        parts=2,
    )
    mlp_low = lax.all_gather(mlp_weight.astype(jnp.bfloat16), "dp", axis=1, tiled=True)
    hidden, d_gate, d_up, mlp_sums = mlp_middle(second_in, grad_out, mlp_low)

    mlp_owned = lax.psum_scatter(mlp_sums, "dp", scatter_dimension=1, tiled=True)
    d_middle, gain_two, d_attn, out_sums = exchange(
        "mlp_back",
        3,
        [(d_gate, mlp_low, 0), (d_up, mlp_low, 1)],
        [middle, cotangent, norm_gains],
        [rows_f32, gain_f32],
        finish=second_back,
        gathers=True,
        parts=2,
        side=(hidden, mlp_low),
    )
    out_sums, mlp_owned = lax.optimization_barrier((out_sums, mlp_owned))
    out_rows = lax.psum_scatter(out_sums, "tensor", scatter_dimension=0, tiled=True)
    query_raw, key_raw, value_raw = attention_back(
        d_attn, attn_low, queries, key_rows, values, attended, log_totals, cos_tile, sine_tile,
        starts
    )
    attn_sums, out_rows = lax.optimization_barrier(
        (attention_grads(first_in, query_raw, key_raw, value_raw, d_attn, attended), out_rows)
    )
    attn_owned = lax.psum_scatter(attn_sums, "dp", scatter_dimension=1, tiled=True)
    layer_out = (middle + out_rows.astype(jnp.float32)).astype(jnp.bfloat16)
    mlp_grad, attn_grad = mlp_owned.astype(jnp.float32), attn_owned.astype(jnp.float32)
    grad_in, gain_one = exchange(
        "input_back",
        4,
        [(query_raw, attn_low, 0), (key_raw, attn_low, 1), (value_raw, attn_low, 2)],
        [inputs, d_middle, norm_gains],
        [rows_f32, gain_f32],
        finish=first_back,
        gathers=False,
        parts=1,
    )
    gain_parts = jnp.stack([jnp.sum(gain_one, axis=0), jnp.sum(gain_two, axis=0)])
    gain_grad = sum_everywhere(gain_parts.reshape(8, -1)).reshape(norm_gains.shape)
    gain_first_new, gain_second_new, gain_new = adam_update(
        norm_gains, gain_grad, gain_first, gain_second, GAIN_RATE
    )
    attn_first_new, attn_second_new, attn_new = adam_update(
        attn_weight, attn_grad, attn_first, attn_second, attn_rates()
    )
    mlp_first_new, mlp_second_new, mlp_new = adam_update(
        mlp_weight, mlp_grad, mlp_first, mlp_second, 0.5 * D ** (-0.5)
    )
    return (
        layer_out,
        grad_in,
        gain_grad,
        attn_grad,
        mlp_grad,
        gain_first_new,
        attn_first_new,
        mlp_first_new,
        gain_second_new,
        attn_second_new,
        mlp_second_new,
        gain_new,
        attn_new,
        mlp_new,
    )


def solution(mesh):
    placed = (
        P(("dp", "tensor"), None),
        P(("dp", "tensor"), None),
        P("dp", None),
        P(),
        P(None, "dp", "tensor"),
        P(None, "dp", "tensor"),
        P(),
        P(None, "dp", "tensor"),
        P(None, "dp", "tensor"),
        P(),
        P(None, "dp", "tensor"),
        P(None, "dp", "tensor"),
    )
    return jax.shard_map(
        local,
        mesh=mesh,
        in_specs=placed,
        out_specs=(
            P(("dp", "tensor"), None),
            P(("dp", "tensor"), None),
            P(),
            P(None, "dp", "tensor"),
            P(None, "dp", "tensor"),
            P(),
            P(None, "dp", "tensor"),
            P(None, "dp", "tensor"),
            P(),
            P(None, "dp", "tensor"),
            P(None, "dp", "tensor"),
            P(),
            P(None, "dp", "tensor"),
            P(None, "dp", "tensor"),
        ),
        check_vma=False,
    )
```

```python
import functools

import jax
import jax.numpy as jnp
from jax import lax
from jax.experimental import pallas as pl
from jax.experimental.pallas import tpu as pltpu
from jax.sharding import PartitionSpec as P

D = 2048
HEAD_DIM = 64
STEP = 10


EPS_NORM = 1e-05
ROPE_BASE = 130000.0
BETA_ONE = 0.9
BETA_TWO = 0.95
EPS_ADAM = 1e-08
WEIGHT_DECAY = 0.1
GAIN_RATE = 0.3
MASKED = -1e30


def doc_layout(lengths, seq_length):
    doc_ends = jnp.cumsum(lengths)
    starts = doc_ends - lengths
    places = jnp.arange(seq_length, dtype=jnp.int32)
    segment = jnp.sum((places[:, None] >= doc_ends[None, :]).astype(jnp.int32), axis=1)
    owners = segment[:, None] == jnp.arange(lengths.shape[0], dtype=jnp.int32)[None, :]
    position = places - jnp.sum(jnp.where(owners, starts[None, :], 0), axis=1)
    return (segment, position)


def rope_tables(position):
    half_dim = HEAD_DIM // 2
    frequencies = jnp.power(
        jnp.float32(ROPE_BASE), -2.0 * jnp.arange(half_dim, dtype=jnp.float32) / HEAD_DIM
    )
    angles = position.astype(jnp.float32)[:, None] * frequencies[None, :]
    cosine, sine = jnp.cos(angles), jnp.sin(angles)
    return (
        jnp.concatenate([cosine, cosine] * 2, axis=1),
        jnp.concatenate([-sine, sine] * 2, axis=1),
    )


MESH = pl.DeviceIdType.MESH
BLOCK = 32
TILE = 256


def whole_part(count):
    return [pl.BlockSpec(memory_space=pltpu.VMEM)] * count


def mate_of():
    place = lax.axis_index("dp")
    return place + 1 - 2 * (place % 2)


def greet(n, me, mate=False):
    barrier = pltpu.get_barrier_semaphore()
    if mate:
        pl.semaphore_signal(barrier, inc=1, device_id={"dp": mate_of()}, device_id_type=MESH)
    for there, step in ((me > 0, -1), (me < n - 1, 1)):

        @pl.when(there)
        def _():
            pl.semaphore_signal(barrier, inc=1, device_id={"tensor": me + step}, device_id_type=MESH)

    count = (me > 0).astype(jnp.int32) + (me < n - 1).astype(jnp.int32)
    pl.semaphore_wait(barrier, count + 1 if mate else count)


def blocks_of(count, body):
    @pl.loop(0, count // BLOCK)
    def _(block):
        body(pl.multiple_of(block * BLOCK, BLOCK))


class RowGather:
    def __init__(self, n, me, parts, place, sent, got):
        self.n, self.me, self.parts, self.place = n, me, parts, place
        self.sent, self.got = sent, got
        self.rows = place.shape[0] // n
        self.has_left, self.has_right = me > 0, me < n - 1

    def copy(self, way, part, hop, owner):
        count = self.rows // self.parts
        first = pl.multiple_of(owner * self.rows + part * count, count)
        block = self.place.at[pl.ds(first, count), :]
        slot = part * (self.n - 1) + hop
        return pltpu.make_async_remote_copy(
            src_ref=block,
            dst_ref=block,
            send_sem=self.sent.at[way, slot],
            recv_sem=self.got.at[way, slot],
            device_id={"tensor": self.me + 1 - 2 * way},
            device_id_type=MESH,
        )

    def start(self, part):
        pl.when(self.has_right)(lambda: self.copy(0, part, 0, self.me).start())
        pl.when(self.has_left)(lambda: self.copy(1, part, 0, self.me).start())

    def step(self, part, hop):
        last = hop + 1 == self.n - 1

        @pl.when(hop < self.me)
        def _():
            owner = self.me - 1 - hop
            self.copy(0, part, hop, owner).wait_recv()
            if not last:
                pl.when(self.has_right)(lambda: self.copy(0, part, hop + 1, owner).start())

        @pl.when(hop < self.n - 1 - self.me)
        def _():
            owner = self.me + 1 + hop
            self.copy(1, part, hop, owner).wait_recv()
            if not last:
                pl.when(self.has_left)(lambda: self.copy(1, part, hop + 1, owner).start())

    def drain(self):
        for part in range(self.parts):
            for hop in range(self.n - 1):
                pl.when(self.has_right & (hop <= self.me))(
                    lambda: self.copy(0, part, hop, self.me - hop).wait_send()
                )
                pl.when(self.has_left & (hop <= self.n - 1 - self.me))(
                    lambda: self.copy(1, part, hop, self.me + hop).wait_send()
                )


class SumScatter:
    def __init__(self, n, me, parts, lefts, rights, totals, run, sent, got):
        self.n, self.me, self.parts = n, me, parts
        self.lefts, self.rights, self.totals, self.run = lefts, rights, totals, run
        self.sent, self.got = sent, got
        self.rows = totals.shape[1]
        self.fed = (me > 0, me < n - 1)

    def copy(self, way, part, hop):
        slot = part * (self.n - 1) + hop
        run = self.run.at[self.place(way, part, hop)]
        return pltpu.make_async_remote_copy(
            src_ref=run,
            dst_ref=run,
            send_sem=self.sent.at[way, slot],
            recv_sem=self.got.at[way, slot],
            device_id={"tensor": self.me + 1 - 2 * way},
            device_id_type=MESH,
        )

    def product(self, dest):
        first = pl.multiple_of(dest * self.rows, self.rows)

        @pl.loop(0, self.totals.shape[2] // TILE)
        def _(tile):
            columns = pl.ds(pl.multiple_of(tile * TILE, TILE), TILE)
            value = None
            for left, right in zip(self.lefts, self.rights):
                term = lax.dot_general(
                    left[pl.ds(first, self.rows), :],
                    right[columns, :],
                    (((1,), (1,)), ((), ())),
                    preferred_element_type=jnp.float32,
                )
                value = term if value is None else value + term
            self.totals[dest, :, columns] = value.astype(self.totals.dtype)

    def place(self, way, part, hop):
        return part * (self.n + 1) + (hop, self.n - hop)[way]

    def begin(self):
        for hop in range(self.n - 1):
            for way, dest in ((0, self.n - 1 - hop), (1, hop)):
                needed = (dest > self.me, dest < self.me)[way]
                run = self.run
                if self.lefts:
                    pl.when(needed)(lambda: self.product(dest))

                @pl.when(needed & jnp.logical_not(self.fed[way]))
                def _():
                    for part in range(self.parts):
                        first = part * (self.rows // self.parts)
                        slot = self.place(way, part, hop)

                        def body(at):
                            own = self.totals[dest, pl.ds(first + at, BLOCK), :]
                            run[slot, pl.ds(at, BLOCK), :] = own.astype(jnp.bfloat16)

                        blocks_of(self.rows // self.parts, body)
                        self.copy(way, part, hop).start()

        if self.lefts:
            self.product(self.me)

    def arrivals(self, count):
        for way, behind in ((0, self.me), (1, self.n - 1 - self.me)):
            hop = count - behind
            yield way, hop, (self.n - 1 - hop, hop)[way], self.fed[way] & (hop >= 0)

    def pass_on(self, part, count):
        for way, hop, dest, there in self.arrivals(count):
            run, slot = self.run, self.place(way, part, hop)
            first = part * (self.rows // self.parts)

            @pl.when(there)
            def _():
                self.copy(way, part, hop).wait_recv()

                def body(at):
                    own = self.totals[dest, pl.ds(first + at, BLOCK), :].astype(jnp.float32)
                    came = run[slot, pl.ds(at, BLOCK), :].astype(jnp.float32)
                    run[slot, pl.ds(at, BLOCK), :] = (own + came).astype(jnp.bfloat16)

                blocks_of(self.rows // self.parts, body)
                self.copy(way, part, hop).start()

    def last(self, part):
        first = part * (self.rows // self.parts)
        for way, hop, dest, there in self.arrivals(self.n - 1):
            run, slot = self.run, self.place(way, part, hop)

            @pl.when(there)
            def _():
                self.copy(way, part, hop).wait_recv()

                def body(at):
                    own = pl.ds(first + at, BLOCK)
                    came = run[slot, pl.ds(at, BLOCK), :].astype(jnp.float32)
                    total = self.totals[self.me, own, :].astype(jnp.float32) + came
                    self.totals[self.me, own, :] = total.astype(self.totals.dtype)

                blocks_of(self.rows // self.parts, body)

    def drain(self):
        for part in range(self.parts):
            for hop in range(self.n - 1):
                pl.when(self.n - 1 - hop > self.me)(lambda: self.copy(0, part, hop).wait_send())
                pl.when(hop < self.me)(lambda: self.copy(1, part, hop).wait_send())


def scatter_scratch(n, parts, rows, width):
    slots = parts * (n - 1)
    kept = jnp.float32 if n * rows * width <= 2**21 else jnp.bfloat16
    return [
        pltpu.VMEM((n, rows, width), kept),
        pltpu.VMEM((parts * (n + 1), rows // parts, width), jnp.bfloat16),
        pltpu.SemaphoreType.DMA((2, slots)),
        pltpu.SemaphoreType.DMA((2, slots)),
    ]


def gather_scratch(n, parts):
    return [pltpu.SemaphoreType.DMA((2, parts * (n - 1)))] * 2


class SideProduct:
    def __init__(self, source, columns, target, held, weight, staged, sems):
        self.source, self.columns, self.target = source, columns, target
        self.held, self.weight, self.staged, self.sems = held, weight, staged, sems
        self.count = source.shape[0] // QUERIES
        self.done = 0

    def fetch(self, block):
        return pltpu.make_async_copy(
            self.source.at[pl.ds(block * QUERIES, QUERIES), :],
            self.held.at[block % 2],
            self.sems.at[block % 2],
        )

    def store(self, block):
        return pltpu.make_async_copy(
            self.staged.at[block % 2],
            self.target.at[pl.ds(block * QUERIES, QUERIES), :],
            self.sems.at[2 + block % 2],
        )

    def fetch_weight(self):
        return pltpu.make_async_copy(self.columns.at[2], self.weight, self.sems.at[4])

    def open(self, lefts):
        self.fetch_weight().start()
        self.fetch(0).start()

    def step(self):
        block = self.done
        if block == self.count:
            return
        if block == 0:
            self.fetch_weight().wait()
        self.fetch(block).wait()
        if block + 1 < self.count:
            self.fetch(block + 1).start()
        if block >= 2:
            self.store(block - 2).wait()

        @pl.loop(0, self.weight.shape[0] // TILE)
        def _(tile):
            columns = pl.ds(pl.multiple_of(tile * TILE, TILE), TILE)
            self.staged[block % 2, :, columns] = over_lanes(
                self.held[block % 2], self.weight[columns, :]
            ).astype(jnp.bfloat16)

        self.store(block).start()
        self.done = block + 1

    def close(self):
        while self.done < self.count:
            self.step()
        for block in range(max(0, self.count - 2), self.count):
            self.store(block).wait()


def side_scratch(depth, units):
    return [
        pltpu.VMEM((2, QUERIES, units), jnp.bfloat16),
        pltpu.VMEM((depth, units), jnp.bfloat16),
        pltpu.VMEM((2, QUERIES, depth), jnp.bfloat16),
        pltpu.SemaphoreType.DMA((5,)),
    ]


def line_kernel(n, parts, products, extras, outs, gathers, side, finish, *refs):
    refs = list(refs)
    take = lambda count: [refs.pop(0) for _ in range(count)]
    lefts, rights, more = take(products), take(products), take(extras)
    side_in = take(2) if side else None
    results = take(outs)
    gathered = take(1)[0] if gathers else None
    filler = SideProduct(*side_in, *take(1), *[refs.pop() for _ in range(4)][::-1]) if side else None
    me = lax.axis_index("tensor")
    if products:
        totals = refs[0]
        sums = SumScatter(n, me, parts, lefts, rights, *take(4))
    if gathers:
        gather = RowGather(n, me, parts, gathered, *take(2))
    rows = totals.shape[1] if products else gathered.shape[0] // n
    part_rows = rows // parts

    def finish_part(part):
        def body(block):
            at = pl.multiple_of(part * part_rows + block, BLOCK)
            total = totals[me, pl.ds(at, BLOCK), :].astype(jnp.float32) if products else None
            sent_rows = finish(at, total, more, results)
            if gathers:
                gathered[pl.ds(pl.multiple_of(me * rows + at, BLOCK), BLOCK), :] = sent_rows

        blocks_of(part_rows, body)

    greet(n, me)
    for result in results:
        if result.shape[0] == 8:
            result[...] = jnp.zeros_like(result)
    if products:
        sums.begin()
    if filler:
        filler.open(lefts)
    for part in range(parts):
        for hop in range(n - 1):
            if filler:
                filler.step()
            if products and hop < n - 2:
                sums.pass_on(part, hop + 1)
            if products and hop == n - 2:
                sums.last(part)
            if gathers and part > 0:
                gather.step(part - 1, hop)
        finish_part(part)
        if gathers:
            gather.start(part)
    if gathers:
        for hop in range(n - 1):
            if filler:
                filler.step()
            gather.step(parts - 1, hop)
        gather.drain()
    if filler:
        filler.close()
    if products:
        sums.drain()


def line_exchange(
    name, collective_id, pairs, extras, outs, rows, width, finish, gathers, parts, side=()
):
    n = lax.axis_size("tensor")
    scratch = scatter_scratch(n, parts, rows, width) if pairs else []
    if gathers:
        scratch = scratch + gather_scratch(n, parts)
        outs = outs + [jax.ShapeDtypeStruct((n * rows, width), jnp.bfloat16)]
    operands = [pair[0] for pair in pairs] + [pair[1] for pair in pairs] + list(extras)
    specs = whole_part(len(operands)) + [pl.BlockSpec(memory_space=pl.ANY)] * len(side)
    own_outs = len(outs) - gathers
    out_specs = whole_part(len(outs))
    operands = operands + list(side)
    if side:
        outs = outs + [jax.ShapeDtypeStruct((side[0].shape[0], width), jnp.bfloat16)]
        out_specs = out_specs + [pl.BlockSpec(memory_space=pl.ANY)]
        scratch = scratch + side_scratch(width, side[0].shape[1])
    for k, (left, right, which) in enumerate(pairs):
        specs[len(pairs) + k] = pl.BlockSpec(
            (None, *right.shape[1:]), lambda i, which=which: (which, 0, 0), pipeline_mode=pl.Buffered(1)
        )
    depth = sum(pair[0].shape[1] for pair in pairs)
    return pl.pallas_call(
        functools.partial(
            line_kernel, n, parts, len(pairs), len(extras), own_outs, gathers, len(side) > 0, finish
        ),
        grid=(1,),
        out_shape=outs,
        in_specs=specs,
        out_specs=out_specs,
        scratch_shapes=scratch,
        compiler_params=pltpu.CompilerParams(
            collective_id=collective_id, has_side_effects=True, vmem_limit_bytes=60 * 2**20
        ),
        cost_estimate=pl.CostEstimate(
            flops=2 * n * rows * width * max(depth, 1),
            bytes_accessed=200 * 2**20,
            transcendentals=0,
        ),
        name=name,
    )(*operands)


def everywhere_kernel(sizes, field, result, came, sent, got):
    places = [lax.axis_index(name) for name in sizes]
    partners = []
    for name, place in zip(sizes, places):
        stride = 1
        while stride < sizes[name]:
            other = place + stride - 2 * stride * (place // stride % 2)
            partners.append({name: other})
            stride = 2 * stride
    barrier = pltpu.get_barrier_semaphore()
    for partner in partners:
        pl.semaphore_signal(barrier, inc=1, device_id=partner, device_id_type=MESH)
    pl.semaphore_wait(barrier, len(partners))
    result[...] = field[...]
    for k, partner in enumerate(partners):
        came[2 * k] = result[...]
        copy = pltpu.make_async_remote_copy(
            src_ref=came.at[2 * k],
            dst_ref=came.at[2 * k + 1],
            send_sem=sent.at[k],
            recv_sem=got.at[k],
            device_id=partner,
            device_id_type=MESH,
        )
        copy.start()
        copy.wait()
        result[...] = result[...] + came[2 * k + 1]


def sum_everywhere(field):
    sizes = {name: lax.axis_size(name) for name in ("dp", "tensor")}
    steps = sum(size.bit_length() - 1 for size in sizes.values())
    return pl.pallas_call(
        functools.partial(everywhere_kernel, sizes),
        out_shape=jax.ShapeDtypeStruct(field.shape, jnp.float32),
        in_specs=whole_part(1),
        out_specs=pl.BlockSpec(memory_space=pltpu.VMEM),
        scratch_shapes=[
            pltpu.VMEM((2 * steps, *field.shape), jnp.float32),
            pltpu.SemaphoreType.DMA((steps,)),
            pltpu.SemaphoreType.DMA((steps,)),
        ],
        compiler_params=pltpu.CompilerParams(collective_id=7, has_side_effects=True),
        name="gain_sum",
    )(field)


def inverse_scale(field):
    return lax.rsqrt(jnp.mean(field * field, axis=-1, keepdims=True) + EPS_NORM)


def first_norm(at, total, more, results):
    layer_in, gains = more
    field = layer_in[pl.ds(at, BLOCK), :].astype(jnp.float32)
    return (field * inverse_scale(field) * gains[0:1, :]).astype(jnp.bfloat16)


def norm_back(field, gradient, gain_row, gain_out):
    inv_scale = inverse_scale(field)
    normed = field * inv_scale
    scaled = gradient * gain_row
    back = inv_scale * (scaled - normed * jnp.mean(scaled * normed, axis=-1, keepdims=True))
    product = gradient * normed
    folded = product[0:8]
    for k in range(8, BLOCK, 8):
        folded = folded + product[k : k + 8]
    gain_out[...] = gain_out[...] + folded
    return back


def second_back(at, total, more, results):
    middle, cotangent, gains = more
    rows = pl.ds(at, BLOCK)
    back = norm_back(middle[rows, :], total, gains[1:2, :], results[1])
    back = back + cotangent[rows, :].astype(jnp.float32)
    results[0][rows, :] = back
    return back.astype(jnp.bfloat16)


def first_back(at, total, more, results):
    layer_in, d_middle, gains = more
    rows = pl.ds(at, BLOCK)
    back = norm_back(layer_in[rows, :].astype(jnp.float32), total, gains[0:1, :], results[1])
    results[0][rows, :] = back + d_middle[rows, :]


PAIR = 2 * HEAD_DIM
QUERIES = 256


def turned(field, cos_tile, sine_tile):
    lanes = lax.broadcasted_iota(jnp.int32, field.shape, 1)
    ahead = pltpu.roll(field, PAIR - HEAD_DIM // 2, 1)
    behind = pltpu.roll(field, HEAD_DIM // 2, 1)
    partner = jnp.where(lanes % HEAD_DIM < HEAD_DIM // 2, ahead, behind)
    return field * cos_tile + partner * sine_tile


def one_head(tile, head):
    lanes = lax.broadcasted_iota(jnp.int32, tile.shape, 1)
    return jnp.where(lanes // HEAD_DIM == head, tile, jnp.zeros_like(tile))


def over_lanes(left, right):
    return lax.dot_general(
        left, right, (((1,), (1,)), ((), ())), preferred_element_type=jnp.float32
    )


def masked(scores, starts, first_query):
    keys = lax.broadcasted_iota(jnp.int32, scores.shape, 0)
    queries = first_query + lax.broadcasted_iota(jnp.int32, scores.shape, 1)
    return jnp.where((keys >= starts) & (keys <= queries), scores, MASKED)


def attention_forward_kernel(
    n, parts, first_in, weights, cos_ref, sine_ref, starts_ref, own_rows, layer_in, gains,
    queries, key_rows, values, attended, log_totals, cot_rows, middle, second_in,
    turned_values, held, held_sems, cot_sent, cot_got, rows_sent, rows_got, turn, totals, run,
    sums_sent, sums_got
):
    me = lax.axis_index("tensor")
    second_core = lax.axis_index("dp") % 2 == 1
    rows = own_rows.shape[0]
    part_rows = rows // parts
    length, width = queries.shape

    def fetch(block):
        return pltpu.make_async_copy(
            first_in.at[pl.ds(block * QUERIES, QUERIES), :], held.at[block % 2], held_sems.at[block % 2]
        )

    fetch(0).start()
    greet(n, me, True)
    cot_gather = RowGather(n, me, 1, cot_rows, cot_sent, cot_got)
    gather = RowGather(n, me, parts, second_in, rows_sent, rows_got)
    sums = SumScatter(
        n, me, parts, [attended], [weights.at[3]], totals, run, sums_sent, sums_got
    )

    def place_own(at):
        place = pl.ds(pl.multiple_of(me * rows + at, BLOCK), BLOCK)
        cot_rows[place, :] = own_rows[pl.ds(at, BLOCK), :]

    blocks_of(rows, place_own)
    cot_gather.start(0)

    for block in range(length // QUERIES):
        fetch(block).wait()
        if (block + 1) * QUERIES < length:
            fetch(block + 1).start()
        at = pl.ds(block * QUERIES, QUERIES)
        source = held[block % 2]
        cos_tile, sine_tile = cos_ref[at, :], sine_ref[at, :]
        for which, target in enumerate((queries, key_rows, values)):
            field = jnp.dot(source, weights[which], preferred_element_type=jnp.float32)
            for pair in range(width // PAIR):
                tile = field[:, pair * PAIR : (pair + 1) * PAIR]
                if which < 2:
                    tile = turned(tile, cos_tile, sine_tile)
                if which == 0:
                    tile = tile.astype(jnp.bfloat16) * HEAD_DIM ** (-0.5)
                target[at, pair * PAIR : (pair + 1) * PAIR] = tile.astype(jnp.bfloat16)

    def attend(pair):
        lanes = pl.ds(pl.multiple_of(pair * PAIR, PAIR), PAIR)
        turned_values[...] = values[:, lanes].astype(jnp.float32).T.astype(jnp.bfloat16)
        for block in range(length // QUERIES):
            at = pl.ds(block * QUERIES, QUERIES)
            reach = (block + 1) * QUERIES
            starts = starts_ref[:, at]
            both = []
            for head in range(2):
                query = one_head(queries[at, lanes], head)
                scores = masked(
                    over_lanes(key_rows[0:reach, lanes], query), starts, block * QUERIES
                )
                peak = jnp.max(scores, axis=0, keepdims=True)
                raised = jnp.exp(scores - peak)
                total = jnp.sum(raised, axis=0, keepdims=True)
                result = jnp.dot(
                    turned_values[head * HEAD_DIM : (head + 1) * HEAD_DIM, 0:reach],
                    raised.astype(jnp.bfloat16),
                    preferred_element_type=jnp.float32,
                )
                both.append(result / total)
                log_totals[2 * pair + head, :, at] = peak + jnp.log(total)
            attended[at, lanes] = jnp.concatenate(both, axis=0).T.astype(jnp.bfloat16)

    pairs = width // PAIR
    pl.loop(0, pairs - 1)(attend)
    cot_gather.step(0, 0)
    pl.loop(pairs - 1, pairs)(attend)

    @pl.when(second_core)
    def _():
        for hop in range(1, n - 1):
            cot_gather.step(0, hop)
        pl.semaphore_wait(turn, 1)

    sums.begin()

    def finish_part(part):
        def body(block):
            at = pl.multiple_of(part * part_rows + block, BLOCK)
            here = pl.ds(at, BLOCK)
            total = totals[me, here, :].astype(jnp.float32)
            field = layer_in[here, :].astype(jnp.float32) + total
            middle[here, :] = field
            place = pl.ds(pl.multiple_of(me * rows + at, BLOCK), BLOCK)
            second_in[place, :] = (field * inverse_scale(field) * gains[1:2, :]).astype(jnp.bfloat16)

        blocks_of(part_rows, body)

    for part in range(parts):
        for hop in range(1, n):
            if part == 0 and hop < n - 1:
                pl.when(jnp.logical_not(second_core))(lambda: cot_gather.step(0, hop))
            if hop < n - 1:
                sums.pass_on(part, hop)
            else:
                sums.last(part)
            if part > 0:
                gather.step(part - 1, hop - 1)
        finish_part(part)
        gather.start(part)

    @pl.when(jnp.logical_not(second_core))
    def _():
        pl.semaphore_signal(turn, inc=1, device_id={"dp": mate_of()}, device_id_type=MESH)

    for hop in range(n - 1):
        gather.step(parts - 1, hop)
    cot_gather.drain()
    gather.drain()
    sums.drain()


def attention_forward(first_in, weights, cos_tile, sine_tile, starts, own_rows, layer_in, gains):
    n = lax.axis_size("tensor")
    parts = 2
    length, depth = first_in.shape
    rows, width = own_rows.shape[0], weights.shape[2]
    narrow = jax.ShapeDtypeStruct((length, width), jnp.bfloat16)
    wide = jax.ShapeDtypeStruct((length, depth), jnp.bfloat16)
    outs = [
        narrow,
        narrow,
        narrow,
        narrow,
        jax.ShapeDtypeStruct((width // HEAD_DIM, 1, length), jnp.float32),
        wide,
        jax.ShapeDtypeStruct((rows, depth), jnp.float32),
        wide,
    ]
    specs = whole_part(8)
    specs[0] = pl.BlockSpec(memory_space=pl.ANY)
    return pl.pallas_call(
        functools.partial(attention_forward_kernel, n, parts),
        out_shape=outs,
        in_specs=specs,
        out_specs=whole_part(len(outs)),
        scratch_shapes=[
            pltpu.VMEM((PAIR, length), jnp.bfloat16),
            pltpu.VMEM((2, QUERIES, depth), jnp.bfloat16),
            pltpu.SemaphoreType.DMA((2,)),
        ]
        + gather_scratch(n, 1)
        + gather_scratch(n, parts)
        + [pltpu.SemaphoreType.REGULAR]
        + scatter_scratch(n, parts, rows, depth),
        compiler_params=pltpu.CompilerParams(
            collective_id=5, has_side_effects=True, vmem_limit_bytes=60 * 2**20
        ),
        cost_estimate=pl.CostEstimate(
            flops=8 * length * depth * width, bytes_accessed=400 * 2**20, transcendentals=0
        ),
        name="attention_forward",
    )(first_in, weights, cos_tile, sine_tile, starts, own_rows, layer_in, gains)


def attention_back_kernel(
    n, d_attn, out_weight, queries, key_rows, values, attended, log_totals, cos_ref, sine_ref,
    starts_ref, middle, out_sums, query_raw, key_raw, value_raw, layer_out,
    d_attended, turned_keys, key_sum, value_sum, held, held_sems, totals, run, sent, got
):
    me = lax.axis_index("tensor")
    length, width = queries.shape
    sums = SumScatter(n, me, 1, [], [], totals, run, sent, got)

    def fetch(block):
        return pltpu.make_async_copy(
            d_attn.at[pl.ds(block * QUERIES, QUERIES), :], held.at[block % 2], held_sems.at[block % 2]
        )

    ready = pltpu.make_async_copy(out_sums, totals, held_sems.at[2])
    ready.start()
    fetch(0).start()
    greet(n, me)
    ready.wait()
    sums.begin()
    for block in range(length // QUERIES):
        fetch(block).wait()
        if (block + 1) * QUERIES < length:
            fetch(block + 1).start()
        d_attended[block * QUERIES : (block + 1) * QUERIES, :] = jnp.dot(
            held[block % 2], out_weight[0], preferred_element_type=jnp.float32
        ).astype(jnp.bfloat16)

    def back_pair(pair):
        lanes = pl.ds(pl.multiple_of(pair * PAIR, PAIR), PAIR)
        turned_keys[...] = key_rows[:, lanes].astype(jnp.float32).T.astype(jnp.bfloat16)
        key_sum[...] = jnp.zeros_like(key_sum)
        value_sum[...] = jnp.zeros_like(value_sum)
        for block in range(length // QUERIES):
            at = pl.ds(block * QUERIES, QUERIES)
            reach = (block + 1) * QUERIES
            starts = starts_ref[:, at]
            grads = d_attended[at, lanes]
            shares = (grads.astype(jnp.float32) * attended[at, lanes].astype(jnp.float32)).T
            both = []
            for head in range(2):
                heads = slice(head * HEAD_DIM, (head + 1) * HEAD_DIM)
                query = one_head(queries[at, lanes], head)
                grad = one_head(grads, head)
                share = jnp.sum(shares[heads], axis=0, keepdims=True)
                scores = masked(
                    over_lanes(key_rows[0:reach, lanes], query), starts, block * QUERIES
                )
                probs = jnp.exp(scores - log_totals[2 * pair + head, :, at])
                prob_grad = over_lanes(values[0:reach, lanes], grad)
                score_grad = (probs * (prob_grad - share)).astype(jnp.bfloat16)
                value_sum[0:reach, :] = value_sum[0:reach, :] + jnp.dot(
                    probs.astype(jnp.bfloat16), grad, preferred_element_type=jnp.float32
                )
                key_sum[0:reach, :] = key_sum[0:reach, :] + jnp.dot(
                    score_grad, query, preferred_element_type=jnp.float32
                )
                both.append(
                    jnp.dot(
                        turned_keys[heads, 0:reach], score_grad, preferred_element_type=jnp.float32
                    )
                )
            query_grad = jnp.concatenate(both, axis=0).T * HEAD_DIM ** (-0.5)
            query_raw[at, lanes] = turned(query_grad, cos_ref[at, :], -sine_ref[at, :]).astype(
                jnp.bfloat16
            )
        key_raw[:, lanes] = turned(key_sum[...], cos_ref[...], -sine_ref[...]).astype(jnp.bfloat16)
        value_raw[:, lanes] = value_sum[...].astype(jnp.bfloat16)

    pairs = width // PAIR
    for count in range(1, n):
        pl.loop(pairs * (count - 1) // (n - 1), pairs * count // (n - 1))(back_pair)
        if count < n - 1:
            sums.pass_on(0, count)
    sums.last(0)

    def body(at):
        rows = pl.ds(at, BLOCK)
        total = middle[rows, :] + totals[me, rows, :].astype(jnp.float32)
        layer_out[rows, :] = total.astype(jnp.bfloat16)

    blocks_of(middle.shape[0], body)
    sums.drain()


def attention_back(
    d_attn, attn_low, queries, key_rows, values, attended, log_totals, cos_tile, sine_tile, starts,
    middle, out_sums
):
    n = lax.axis_size("tensor")
    length, depth = d_attn.shape
    width, rows = queries.shape[1], middle.shape[0]
    narrow = jax.ShapeDtypeStruct((length, width), jnp.bfloat16)
    specs = whole_part(12)
    specs[0] = specs[11] = pl.BlockSpec(memory_space=pl.ANY)
    specs[1] = pl.BlockSpec((1, depth, width), lambda i: (3, 0, 0), pipeline_mode=pl.Buffered(1))
    scratch = scatter_scratch(n, 1, rows, depth)
    scratch[0] = pltpu.VMEM((n, rows, depth), jnp.bfloat16)
    return pl.pallas_call(
        functools.partial(attention_back_kernel, n),
        grid=(1,),
        out_shape=[narrow, narrow, narrow, jax.ShapeDtypeStruct((rows, depth), jnp.bfloat16)],
        in_specs=specs,
        out_specs=whole_part(4),
        scratch_shapes=[
            pltpu.VMEM((length, width), jnp.bfloat16),
            pltpu.VMEM((PAIR, length), jnp.bfloat16),
            pltpu.VMEM((length, PAIR), jnp.float32),
            pltpu.VMEM((length, PAIR), jnp.float32),
            pltpu.VMEM((2, QUERIES, depth), jnp.bfloat16),
            pltpu.SemaphoreType.DMA((3,)),
        ]
        + scratch,
        compiler_params=pltpu.CompilerParams(
            collective_id=6, has_side_effects=True, vmem_limit_bytes=60 * 2**20
        ),
        cost_estimate=pl.CostEstimate(
            flops=2 * length * depth * width, bytes_accessed=200 * 2**20, transcendentals=0
        ),
        name="attention_back",
    )(
        d_attn, attn_low, queries, key_rows, values, attended, log_totals, cos_tile, sine_tile,
        starts, middle, out_sums.reshape(n, rows, depth)
    )


def turn_into(target, source):
    @pl.loop(0, source.shape[0] // TILE)
    def _(block):
        at = pl.ds(pl.multiple_of(block * TILE, TILE), TILE)
        for k in range(source.shape[1] // TILE):
            columns = slice(k * TILE, (k + 1) * TILE)
            target[columns, at] = source[at, columns].astype(jnp.float32).T.astype(jnp.bfloat16)


def mlp_kernel(second_in, cotangent, weights, hidden, d_gate, d_up, grads, second_turned, cot_turned):
    @pl.when(pl.program_id(0) == 0)
    def _():
        turn_into(second_turned, second_in)
        turn_into(cot_turned, cotangent)

    for block in range(second_in.shape[0] // QUERIES):
        at = slice(block * QUERIES, (block + 1) * QUERIES)
        source = second_in[at, :]
        gate_proj = jnp.dot(source, weights[0], preferred_element_type=jnp.float32)
        up_proj = jnp.dot(source, weights[1], preferred_element_type=jnp.float32)
        d_hidden = jnp.dot(cotangent[at, :], weights[2], preferred_element_type=jnp.float32)
        sigmoid_gate = jax.nn.sigmoid(gate_proj)
        silu = gate_proj * sigmoid_gate
        hidden[at, :] = (silu * up_proj).astype(jnp.bfloat16)
        slope = sigmoid_gate * (1.0 + gate_proj * (1.0 - sigmoid_gate))
        d_gate[at, :] = (d_hidden * up_proj * slope).astype(jnp.bfloat16)
        d_up[at, :] = (d_hidden * silu).astype(jnp.bfloat16)
    for which, (left, right) in enumerate(
        ((second_turned, d_gate), (second_turned, d_up), (cot_turned, hidden))
    ):

        @pl.loop(0, left.shape[0] // 512)
        def _(block):
            at = pl.ds(pl.multiple_of(block * 512, 512), 512)
            grads[which, at, :] = jnp.dot(
                left[at, :], right[...], preferred_element_type=jnp.float32
            ).astype(jnp.bfloat16)


def mlp_middle(second_in, cotangent, weights):
    length, depth = second_in.shape
    units = weights.shape[2]
    tile = 256
    wide = jax.ShapeDtypeStruct((length, units), jnp.bfloat16)
    column = pl.BlockSpec((length, tile), lambda j: (0, j))
    stacked = pl.BlockSpec((3, depth, tile), lambda j: (0, 0, j))
    return pl.pallas_call(
        mlp_kernel,
        grid=(units // tile,),
        out_shape=[wide, wide, wide, jax.ShapeDtypeStruct((3, depth, units), jnp.bfloat16)],
        in_specs=whole_part(2) + [stacked],
        out_specs=[column, column, column, stacked],
        scratch_shapes=[pltpu.VMEM((depth, length), jnp.bfloat16)] * 2,
        compiler_params=pltpu.CompilerParams(vmem_limit_bytes=60 * 2**20),
        cost_estimate=pl.CostEstimate(
            flops=12 * length * depth * units, bytes_accessed=60 * 2**20, transcendentals=0
        ),
        name="mlp_middle",
    )(second_in, cotangent, weights)


def grads_kernel(first_in, query_raw, key_raw, value_raw, d_attn, attended, grads, turned_rows):
    which = pl.program_id(0)
    pl.when(which == 0)(lambda: turn_into(turned_rows, first_in))
    pl.when(which == 3)(lambda: turn_into(turned_rows, d_attn))
    for k, right in enumerate((query_raw, key_raw, value_raw, attended)):

        @pl.when(which == k)
        def _():
            @pl.loop(0, turned_rows.shape[0] // 512)
            def _(block):
                at = pl.ds(pl.multiple_of(block * 512, 512), 512)
                grads[at, :] = jnp.dot(
                    turned_rows[at, :], right[...], preferred_element_type=jnp.float32
                ).astype(jnp.bfloat16)


def attention_grads(first_in, query_raw, key_raw, value_raw, d_attn, attended):
    length, depth = first_in.shape
    width = attended.shape[1]
    return pl.pallas_call(
        grads_kernel,
        grid=(4,),
        out_shape=jax.ShapeDtypeStruct((4, depth, width), jnp.bfloat16),
        in_specs=whole_part(6),
        out_specs=pl.BlockSpec((None, depth, width), lambda j: (j, 0, 0)),
        scratch_shapes=[pltpu.VMEM((depth, length), jnp.bfloat16)],
        compiler_params=pltpu.CompilerParams(vmem_limit_bytes=60 * 2**20),
        cost_estimate=pl.CostEstimate(
            flops=8 * length * depth * width, bytes_accessed=20 * 2**20, transcendentals=0
        ),
        name="attention_grads",
    )(first_in, query_raw, key_raw, value_raw, d_attn, attended)


def attn_rates():
    return jnp.array([1.0, 1.0, 1.0, 8.0**0.5], jnp.float32).reshape(4, 1, 1) * (0.5 * D ** (-0.5))


def adam_update(weight, gradient, moment_one, moment_two, step_rate):
    first_new = BETA_ONE * moment_one + (1.0 - BETA_ONE) * gradient
    second_new = BETA_TWO * moment_two + (1.0 - BETA_TWO) * gradient * gradient
    fix_one = 1.0 - BETA_ONE**STEP
    fix_two = 1.0 - BETA_TWO**STEP
    weight_new = weight - step_rate * (
        first_new / fix_one / (jnp.sqrt(second_new / fix_two) + EPS_ADAM) + WEIGHT_DECAY * weight
    )
    return (first_new, second_new, weight_new)


def local(
    inputs,
    cotangent,
    doc_lengths,
    norm_gains,
    attn_weight,
    mlp_weight,
    gain_first,
    attn_first,
    mlp_first,
    gain_second,
    attn_second,
    mlp_second,
):
    row_count = inputs.shape[0]
    seq_length = row_count * lax.axis_size("tensor")
    segment, position = doc_layout(doc_lengths[0], seq_length)
    cos_tile, sine_tile = rope_tables(position)
    starts = (jnp.arange(seq_length, dtype=jnp.int32) - position)[None, :]
    width = inputs.shape[1]
    rows_f32 = jax.ShapeDtypeStruct((row_count, width), jnp.float32)
    gain_f32 = jax.ShapeDtypeStruct((8, width), jnp.float32)
    exchange = functools.partial(line_exchange, rows=row_count, width=width)
    (first_in,) = exchange(
        "first_norm", 1, [], [inputs, norm_gains], [], finish=first_norm, gathers=True, parts=1
    )
    attn_low = lax.all_gather(attn_weight.astype(jnp.bfloat16), "dp", axis=1, tiled=True)

    (
        queries, key_rows, values, attended, log_totals, grad_out, middle, second_in
    ) = attention_forward(
        first_in, attn_low, cos_tile, sine_tile, starts, cotangent, inputs, norm_gains
    )
    mlp_low = lax.all_gather(mlp_weight.astype(jnp.bfloat16), "dp", axis=1, tiled=True)
    hidden, d_gate, d_up, mlp_sums = mlp_middle(second_in, grad_out, mlp_low)

    mlp_owned = lax.psum_scatter(mlp_sums, "dp", scatter_dimension=1, tiled=True)
    d_middle, gain_two, d_attn, out_sums = exchange(
        "mlp_back",
        3,
        [(d_gate, mlp_low, 0), (d_up, mlp_low, 1)],
        [middle, cotangent, norm_gains],
        [rows_f32, gain_f32],
        finish=second_back,
        gathers=True,
        parts=2,
        side=(hidden, mlp_low),
    )
    query_raw, key_raw, value_raw, layer_out = attention_back(
        d_attn, attn_low, queries, key_rows, values, attended, log_totals, cos_tile, sine_tile,
        starts, middle, out_sums
    )
    attn_sums, mlp_owned = lax.optimization_barrier(
        (attention_grads(first_in, query_raw, key_raw, value_raw, d_attn, attended), mlp_owned)
    )
    attn_owned = lax.psum_scatter(attn_sums, "dp", scatter_dimension=1, tiled=True)
    mlp_grad, attn_grad = mlp_owned.astype(jnp.float32), attn_owned.astype(jnp.float32)
    grad_in, gain_one = exchange(
        "input_back",
        4,
        [(query_raw, attn_low, 0), (key_raw, attn_low, 1), (value_raw, attn_low, 2)],
        [inputs, d_middle, norm_gains],
        [rows_f32, gain_f32],
        finish=first_back,
        gathers=False,
        parts=1,
    )
    gain_parts = jnp.stack([jnp.sum(gain_one, axis=0), jnp.sum(gain_two, axis=0)])
    gain_grad = sum_everywhere(gain_parts.reshape(8, -1)).reshape(norm_gains.shape)
    gain_first_new, gain_second_new, gain_new = adam_update(
        norm_gains, gain_grad, gain_first, gain_second, GAIN_RATE
    )
    attn_first_new, attn_second_new, attn_new = adam_update(
        attn_weight, attn_grad, attn_first, attn_second, attn_rates()
    )
    mlp_first_new, mlp_second_new, mlp_new = adam_update(
        mlp_weight, mlp_grad, mlp_first, mlp_second, 0.5 * D ** (-0.5)
    )
    return (
        layer_out,
        grad_in,
        gain_grad,
        attn_grad,
        mlp_grad,
        gain_first_new,
        attn_first_new,
        mlp_first_new,
        gain_second_new,
        attn_second_new,
        mlp_second_new,
        gain_new,
        attn_new,
        mlp_new,
    )


def solution(mesh):
    placed = (
        P(("dp", "tensor"), None),
        P(("dp", "tensor"), None),
        P("dp", None),
        P(),
        P(None, "dp", "tensor"),
        P(None, "dp", "tensor"),
        P(),
        P(None, "dp", "tensor"),
        P(None, "dp", "tensor"),
        P(),
        P(None, "dp", "tensor"),
        P(None, "dp", "tensor"),
    )
    return jax.shard_map(
        local,
        mesh=mesh,
        in_specs=placed,
        out_specs=(
            P(("dp", "tensor"), None),
            P(("dp", "tensor"), None),
            P(),
            P(None, "dp", "tensor"),
            P(None, "dp", "tensor"),
            P(),
            P(None, "dp", "tensor"),
            P(None, "dp", "tensor"),
            P(),
            P(None, "dp", "tensor"),
            P(None, "dp", "tensor"),
            P(),
            P(None, "dp", "tensor"),
            P(None, "dp", "tensor"),
        ),
        check_vma=False,
    )
```

```python
import functools

import jax
import jax.numpy as jnp
from jax import lax
from jax.experimental import pallas as pl
from jax.experimental.pallas import tpu as pltpu
from jax.sharding import PartitionSpec as P

D = 2048
HEAD_DIM = 64
STEP = 10


EPS_NORM = 1e-05
ROPE_BASE = 130000.0
BETA_ONE = 0.9
BETA_TWO = 0.95
EPS_ADAM = 1e-08
WEIGHT_DECAY = 0.1
GAIN_RATE = 0.3
MASKED = -1e30


def doc_layout(lengths, seq_length):
    doc_ends = jnp.cumsum(lengths)
    starts = doc_ends - lengths
    places = jnp.arange(seq_length, dtype=jnp.int32)
    segment = jnp.sum((places[:, None] >= doc_ends[None, :]).astype(jnp.int32), axis=1)
    owners = segment[:, None] == jnp.arange(lengths.shape[0], dtype=jnp.int32)[None, :]
    position = places - jnp.sum(jnp.where(owners, starts[None, :], 0), axis=1)
    return (segment, position)


def rope_tables(position):
    half_dim = HEAD_DIM // 2
    frequencies = jnp.power(
        jnp.float32(ROPE_BASE), -2.0 * jnp.arange(half_dim, dtype=jnp.float32) / HEAD_DIM
    )
    angles = position.astype(jnp.float32)[:, None] * frequencies[None, :]
    cosine, sine = jnp.cos(angles), jnp.sin(angles)
    return (
        jnp.concatenate([cosine, cosine] * 2, axis=1),
        jnp.concatenate([-sine, sine] * 2, axis=1),
    )


MESH = pl.DeviceIdType.MESH
BLOCK = 32
TILE = 256


def whole_part(count):
    return [pl.BlockSpec(memory_space=pltpu.VMEM)] * count


def mate_of():
    place = lax.axis_index("dp")
    return place + 1 - 2 * (place % 2)


def greet(n, me, mate=False):
    barrier = pltpu.get_barrier_semaphore()
    if mate:
        pl.semaphore_signal(barrier, inc=1, device_id={"dp": mate_of()}, device_id_type=MESH)
    for there, step in ((me > 0, -1), (me < n - 1, 1)):

        @pl.when(there)
        def _():
            pl.semaphore_signal(barrier, inc=1, device_id={"tensor": me + step}, device_id_type=MESH)

    count = (me > 0).astype(jnp.int32) + (me < n - 1).astype(jnp.int32)
    pl.semaphore_wait(barrier, count + 1 if mate else count)


def blocks_of(count, body):
    @pl.loop(0, count // BLOCK)
    def _(block):
        body(pl.multiple_of(block * BLOCK, BLOCK))


class RowGather:
    def __init__(self, n, me, parts, place, sent, got):
        self.n, self.me, self.parts, self.place = n, me, parts, place
        self.sent, self.got = sent, got
        self.rows = place.shape[0] // n
        self.has_left, self.has_right = me > 0, me < n - 1

    def copy(self, way, part, hop, owner):
        count = self.rows // self.parts
        first = pl.multiple_of(owner * self.rows + part * count, count)
        block = self.place.at[pl.ds(first, count), :]
        slot = part * (self.n - 1) + hop
        return pltpu.make_async_remote_copy(
            src_ref=block,
            dst_ref=block,
            send_sem=self.sent.at[way, slot],
            recv_sem=self.got.at[way, slot],
            device_id={"tensor": self.me + 1 - 2 * way},
            device_id_type=MESH,
        )

    def start(self, part):
        pl.when(self.has_right)(lambda: self.copy(0, part, 0, self.me).start())
        pl.when(self.has_left)(lambda: self.copy(1, part, 0, self.me).start())

    def step(self, part, hop):
        last = hop + 1 == self.n - 1

        @pl.when(hop < self.me)
        def _():
            owner = self.me - 1 - hop
            self.copy(0, part, hop, owner).wait_recv()
            if not last:
                pl.when(self.has_right)(lambda: self.copy(0, part, hop + 1, owner).start())

        @pl.when(hop < self.n - 1 - self.me)
        def _():
            owner = self.me + 1 + hop
            self.copy(1, part, hop, owner).wait_recv()
            if not last:
                pl.when(self.has_left)(lambda: self.copy(1, part, hop + 1, owner).start())

    def drain(self):
        @pl.loop(0, self.parts)
        def _(part):
            for hop in range(self.n - 1):
                pl.when(self.has_right & (hop <= self.me))(
                    lambda: self.copy(0, part, hop, self.me - hop).wait_send()
                )
                pl.when(self.has_left & (hop <= self.n - 1 - self.me))(
                    lambda: self.copy(1, part, hop, self.me + hop).wait_send()
                )


class SumScatter:
    def __init__(self, n, me, parts, lefts, rights, totals, run, sent, got):
        self.n, self.me, self.parts = n, me, parts
        self.lefts, self.rights, self.totals, self.run = lefts, rights, totals, run
        self.sent, self.got = sent, got
        self.rows = totals.shape[1]
        self.fed = (me > 0, me < n - 1)

    def copy(self, way, part, hop):
        slot = part * (self.n - 1) + hop
        run = self.run.at[self.place(way, part, hop)]
        return pltpu.make_async_remote_copy(
            src_ref=run,
            dst_ref=run,
            send_sem=self.sent.at[way, slot],
            recv_sem=self.got.at[way, slot],
            device_id={"tensor": self.me + 1 - 2 * way},
            device_id_type=MESH,
        )

    def product(self, dest):
        first = pl.multiple_of(dest * self.rows, self.rows)

        @pl.loop(0, self.totals.shape[2] // TILE)
        def _(tile):
            columns = pl.ds(pl.multiple_of(tile * TILE, TILE), TILE)
            value = None
            for left, right in zip(self.lefts, self.rights):
                term = lax.dot_general(
                    left[pl.ds(first, self.rows), :],
                    right[columns, :],
                    (((1,), (1,)), ((), ())),
                    preferred_element_type=jnp.float32,
                )
                value = term if value is None else value + term
            self.totals[dest, :, columns] = value.astype(self.totals.dtype)

    def place(self, way, part, hop):
        return part * (self.n + 1) + (hop, self.n - hop)[way]

    def begin(self):
        part_rows = self.rows // self.parts
        for hop in range(self.n - 1):
            for way, dest in ((0, self.n - 1 - hop), (1, hop)):
                needed = (dest > self.me, dest < self.me)[way]
                if self.lefts:
                    pl.when(needed)(lambda: self.product(dest))

                @pl.when(needed & jnp.logical_not(self.fed[way]))
                def _():
                    @pl.loop(0, self.parts)
                    def _(part):
                        slot = self.place(way, part, hop)

                        def body(at):
                            first = pl.multiple_of(part * part_rows + at, BLOCK)
                            own = self.totals[dest, pl.ds(first, BLOCK), :]
                            self.run[slot, pl.ds(at, BLOCK), :] = own.astype(jnp.bfloat16)

                        blocks_of(part_rows, body)
                        self.copy(way, part, hop).start()

        if self.lefts:
            self.product(self.me)

    def arrivals(self, count):
        for way, behind in ((0, self.me), (1, self.n - 1 - self.me)):
            hop = count - behind
            yield way, hop, (self.n - 1 - hop, hop)[way], self.fed[way] & (hop >= 0)

    def pass_on(self, part, count):
        for way, hop, dest, there in self.arrivals(count):
            run, slot = self.run, self.place(way, part, hop)
            first = part * (self.rows // self.parts)

            @pl.when(there)
            def _():
                self.copy(way, part, hop).wait_recv()

                def body(at):
                    here = pl.ds(pl.multiple_of(first + at, BLOCK), BLOCK)
                    own = self.totals[dest, here, :].astype(jnp.float32)
                    came = run[slot, pl.ds(at, BLOCK), :].astype(jnp.float32)
                    run[slot, pl.ds(at, BLOCK), :] = (own + came).astype(jnp.bfloat16)

                blocks_of(self.rows // self.parts, body)
                self.copy(way, part, hop).start()

    def last(self, part):
        first = part * (self.rows // self.parts)
        for way, hop, dest, there in self.arrivals(self.n - 1):
            run, slot = self.run, self.place(way, part, hop)

            @pl.when(there)
            def _():
                self.copy(way, part, hop).wait_recv()

                def body(at):
                    own = pl.ds(pl.multiple_of(first + at, BLOCK), BLOCK)
                    came = run[slot, pl.ds(at, BLOCK), :].astype(jnp.float32)
                    total = self.totals[self.me, own, :].astype(jnp.float32) + came
                    self.totals[self.me, own, :] = total.astype(self.totals.dtype)

                blocks_of(self.rows // self.parts, body)

    def drain(self):
        @pl.loop(0, self.parts)
        def _(part):
            for hop in range(self.n - 1):
                pl.when(self.n - 1 - hop > self.me)(lambda: self.copy(0, part, hop).wait_send())
                pl.when(hop < self.me)(lambda: self.copy(1, part, hop).wait_send())


def scatter_scratch(n, parts, rows, width):
    slots = parts * (n - 1)
    kept = jnp.float32 if n * rows * width <= 2**21 else jnp.bfloat16
    return [
        pltpu.VMEM((n, rows, width), kept),
        pltpu.VMEM((parts * (n + 1), rows // parts, width), jnp.bfloat16),
        pltpu.SemaphoreType.DMA((2, slots)),
        pltpu.SemaphoreType.DMA((2, slots)),
    ]


def gather_scratch(n, parts):
    return [pltpu.SemaphoreType.DMA((2, parts * (n - 1)))] * 2


class SideProduct:
    def __init__(self, source, columns, target, held, weight, staged, sems):
        self.source, self.columns, self.target = source, columns, target
        self.held, self.weight, self.staged, self.sems = held, weight, staged, sems
        self.count = source.shape[0] // QUERIES
        self.done = 0

    def fetch(self, block):
        return pltpu.make_async_copy(
            self.source.at[pl.ds(block * QUERIES, QUERIES), :],
            self.held.at[block % 2],
            self.sems.at[block % 2],
        )

    def store(self, block):
        return pltpu.make_async_copy(
            self.staged.at[block % 2],
            self.target.at[pl.ds(block * QUERIES, QUERIES), :],
            self.sems.at[2 + block % 2],
        )

    def fetch_weight(self):
        return pltpu.make_async_copy(self.columns.at[2], self.weight, self.sems.at[4])

    def open(self, lefts):
        self.fetch_weight().start()
        self.fetch(0).start()

    def step(self):
        block = self.done
        if block == self.count:
            return
        if block == 0:
            self.fetch_weight().wait()
        self.fetch(block).wait()
        if block + 1 < self.count:
            self.fetch(block + 1).start()
        if block >= 2:
            self.store(block - 2).wait()

        @pl.loop(0, self.weight.shape[0] // TILE)
        def _(tile):
            columns = pl.ds(pl.multiple_of(tile * TILE, TILE), TILE)
            self.staged[block % 2, :, columns] = over_lanes(
                self.held[block % 2], self.weight[columns, :]
            ).astype(jnp.bfloat16)

        self.store(block).start()
        self.done = block + 1

    def close(self):
        while self.done < self.count:
            self.step()
        for block in range(max(0, self.count - 2), self.count):
            self.store(block).wait()


def side_scratch(depth, units):
    return [
        pltpu.VMEM((2, QUERIES, units), jnp.bfloat16),
        pltpu.VMEM((depth, units), jnp.bfloat16),
        pltpu.VMEM((2, QUERIES, depth), jnp.bfloat16),
        pltpu.SemaphoreType.DMA((5,)),
    ]


def line_kernel(n, parts, products, extras, outs, gathers, side, finish, *refs):
    refs = list(refs)
    take = lambda count: [refs.pop(0) for _ in range(count)]
    lefts, rights, more = take(products), take(products), take(extras)
    side_in = take(2) if side else None
    results = take(outs)
    gathered = take(1)[0] if gathers else None
    filler = SideProduct(*side_in, *take(1), *[refs.pop() for _ in range(4)][::-1]) if side else None
    me = lax.axis_index("tensor")
    if products:
        totals = refs[0]
        sums = SumScatter(n, me, parts, lefts, rights, *take(4))
    if gathers:
        gather = RowGather(n, me, parts, gathered, *take(2))
    rows = totals.shape[1] if products else gathered.shape[0] // n
    part_rows = rows // parts

    def finish_part(part):
        def body(block):
            at = pl.multiple_of(part * part_rows + block, BLOCK)
            total = totals[me, pl.ds(at, BLOCK), :].astype(jnp.float32) if products else None
            sent_rows = finish(at, total, more, results)
            if gathers:
                gathered[pl.ds(pl.multiple_of(me * rows + at, BLOCK), BLOCK), :] = sent_rows

        blocks_of(part_rows, body)

    greet(n, me)
    for result in results:
        if result.shape[0] == 8:
            result[...] = jnp.zeros_like(result)
    if products:
        sums.begin()
    if filler:
        filler.open(lefts)
    def complete(part):
        if products:
            sums.last(part)
        finish_part(part)
        if gathers:
            gather.start(part)

    if products:
        for count in range(1, n - 1):
            if filler:
                filler.step()
            pl.loop(0, parts)(lambda part: sums.pass_on(part, count))
        if filler:
            filler.step()
    pl.loop(0, parts)(complete)
    if gathers:
        for hop in range(n - 1):
            if filler:
                filler.step()
            pl.loop(0, parts)(lambda part: gather.step(part, hop))
        gather.drain()
    if filler:
        filler.close()
    if products:
        sums.drain()


def line_exchange(
    name, collective_id, pairs, extras, outs, rows, width, finish, gathers, parts, side=()
):
    n = lax.axis_size("tensor")
    scratch = scatter_scratch(n, parts, rows, width) if pairs else []
    if gathers:
        scratch = scratch + gather_scratch(n, parts)
        outs = outs + [jax.ShapeDtypeStruct((n * rows, width), jnp.bfloat16)]
    operands = [pair[0] for pair in pairs] + [pair[1] for pair in pairs] + list(extras)
    specs = whole_part(len(operands)) + [pl.BlockSpec(memory_space=pl.ANY)] * len(side)
    own_outs = len(outs) - gathers
    out_specs = whole_part(len(outs))
    operands = operands + list(side)
    if side:
        outs = outs + [jax.ShapeDtypeStruct((side[0].shape[0], width), jnp.bfloat16)]
        out_specs = out_specs + [pl.BlockSpec(memory_space=pl.ANY)]
        scratch = scratch + side_scratch(width, side[0].shape[1])
    for k, (left, right, which) in enumerate(pairs):
        specs[len(pairs) + k] = pl.BlockSpec(
            (None, *right.shape[1:]), lambda i, which=which: (which, 0, 0), pipeline_mode=pl.Buffered(1)
        )
    depth = sum(pair[0].shape[1] for pair in pairs)
    return pl.pallas_call(
        functools.partial(
            line_kernel, n, parts, len(pairs), len(extras), own_outs, gathers, len(side) > 0, finish
        ),
        grid=(1,),
        out_shape=outs,
        in_specs=specs,
        out_specs=out_specs,
        scratch_shapes=scratch,
        compiler_params=pltpu.CompilerParams(
            collective_id=collective_id, has_side_effects=True, vmem_limit_bytes=60 * 2**20
        ),
        cost_estimate=pl.CostEstimate(
            flops=2 * n * rows * width * max(depth, 1),
            bytes_accessed=200 * 2**20,
            transcendentals=0,
        ),
        name=name,
    )(*operands)


def everywhere_kernel(sizes, field, result, came, sent, got):
    places = [lax.axis_index(name) for name in sizes]
    partners = []
    for name, place in zip(sizes, places):
        stride = 1
        while stride < sizes[name]:
            other = place + stride - 2 * stride * (place // stride % 2)
            partners.append({name: other})
            stride = 2 * stride
    barrier = pltpu.get_barrier_semaphore()
    for partner in partners:
        pl.semaphore_signal(barrier, inc=1, device_id=partner, device_id_type=MESH)
    pl.semaphore_wait(barrier, len(partners))
    result[...] = field[...]
    for k, partner in enumerate(partners):
        came[2 * k] = result[...]
        copy = pltpu.make_async_remote_copy(
            src_ref=came.at[2 * k],
            dst_ref=came.at[2 * k + 1],
            send_sem=sent.at[k],
            recv_sem=got.at[k],
            device_id=partner,
            device_id_type=MESH,
        )
        copy.start()
        copy.wait()
        result[...] = result[...] + came[2 * k + 1]


def sum_everywhere(field):
    sizes = {name: lax.axis_size(name) for name in ("dp", "tensor")}
    steps = sum(size.bit_length() - 1 for size in sizes.values())
    return pl.pallas_call(
        functools.partial(everywhere_kernel, sizes),
        out_shape=jax.ShapeDtypeStruct(field.shape, jnp.float32),
        in_specs=whole_part(1),
        out_specs=pl.BlockSpec(memory_space=pltpu.VMEM),
        scratch_shapes=[
            pltpu.VMEM((2 * steps, *field.shape), jnp.float32),
            pltpu.SemaphoreType.DMA((steps,)),
            pltpu.SemaphoreType.DMA((steps,)),
        ],
        compiler_params=pltpu.CompilerParams(collective_id=7, has_side_effects=True),
        name="gain_sum",
    )(field)


def inverse_scale(field):
    return lax.rsqrt(jnp.mean(field * field, axis=-1, keepdims=True) + EPS_NORM)


def first_norm(at, total, more, results):
    layer_in, gains = more
    field = layer_in[pl.ds(at, BLOCK), :].astype(jnp.float32)
    return (field * inverse_scale(field) * gains[0:1, :]).astype(jnp.bfloat16)


def norm_back(field, gradient, gain_row, gain_out):
    inv_scale = inverse_scale(field)
    normed = field * inv_scale
    scaled = gradient * gain_row
    back = inv_scale * (scaled - normed * jnp.mean(scaled * normed, axis=-1, keepdims=True))
    product = gradient * normed
    folded = product[0:8]
    for k in range(8, BLOCK, 8):
        folded = folded + product[k : k + 8]
    gain_out[...] = gain_out[...] + folded
    return back


def second_back(at, total, more, results):
    middle, cotangent, gains = more
    rows = pl.ds(at, BLOCK)
    back = norm_back(middle[rows, :], total, gains[1:2, :], results[1])
    back = back + cotangent[rows, :].astype(jnp.float32)
    results[0][rows, :] = back
    return back.astype(jnp.bfloat16)


def first_back(at, total, more, results):
    layer_in, d_middle, gains = more
    rows = pl.ds(at, BLOCK)
    back = norm_back(layer_in[rows, :].astype(jnp.float32), total, gains[0:1, :], results[1])
    results[0][rows, :] = back + d_middle[rows, :]


PAIR = 2 * HEAD_DIM
QUERIES = 256


def turned(field, cos_tile, sine_tile):
    lanes = lax.broadcasted_iota(jnp.int32, field.shape, 1)
    ahead = pltpu.roll(field, PAIR - HEAD_DIM // 2, 1)
    behind = pltpu.roll(field, HEAD_DIM // 2, 1)
    partner = jnp.where(lanes % HEAD_DIM < HEAD_DIM // 2, ahead, behind)
    return field * cos_tile + partner * sine_tile


def one_head(tile, head):
    lanes = lax.broadcasted_iota(jnp.int32, tile.shape, 1)
    return jnp.where(lanes // HEAD_DIM == head, tile, jnp.zeros_like(tile))


def over_lanes(left, right):
    return lax.dot_general(
        left, right, (((1,), (1,)), ((), ())), preferred_element_type=jnp.float32
    )


def masked(scores, starts, first_query):
    keys = lax.broadcasted_iota(jnp.int32, scores.shape, 0)
    queries = first_query + lax.broadcasted_iota(jnp.int32, scores.shape, 1)
    return jnp.where((keys >= starts) & (keys <= queries), scores, MASKED)


def attention_forward_kernel(
    n, parts, first_in, weights, cos_ref, sine_ref, starts_ref, own_rows, layer_in, gains,
    queries, key_rows, values, attended, log_totals, cot_rows, middle, second_in,
    turned_values, held, held_sems, cot_sent, cot_got, rows_sent, rows_got, turn, totals, run,
    sums_sent, sums_got
):
    me = lax.axis_index("tensor")
    second_core = lax.axis_index("dp") % 2 == 1
    rows = own_rows.shape[0]
    part_rows = rows // parts
    length, width = queries.shape

    def fetch(block):
        return pltpu.make_async_copy(
            first_in.at[pl.ds(block * QUERIES, QUERIES), :], held.at[block % 2], held_sems.at[block % 2]
        )

    fetch(0).start()
    greet(n, me, True)
    cot_gather = RowGather(n, me, 1, cot_rows, cot_sent, cot_got)
    gather = RowGather(n, me, parts, second_in, rows_sent, rows_got)
    sums = SumScatter(
        n, me, parts, [attended], [weights.at[3]], totals, run, sums_sent, sums_got
    )

    def place_own(at):
        place = pl.ds(pl.multiple_of(me * rows + at, BLOCK), BLOCK)
        cot_rows[place, :] = own_rows[pl.ds(at, BLOCK), :]

    blocks_of(rows, place_own)
    cot_gather.start(0)

    for block in range(length // QUERIES):
        fetch(block).wait()
        if (block + 1) * QUERIES < length:
            fetch(block + 1).start()
        at = pl.ds(block * QUERIES, QUERIES)
        source = held[block % 2]
        cos_tile, sine_tile = cos_ref[at, :], sine_ref[at, :]
        for which, target in enumerate((queries, key_rows, values)):
            field = jnp.dot(source, weights[which], preferred_element_type=jnp.float32)
            for pair in range(width // PAIR):
                tile = field[:, pair * PAIR : (pair + 1) * PAIR]
                if which < 2:
                    tile = turned(tile, cos_tile, sine_tile)
                if which == 0:
                    tile = tile.astype(jnp.bfloat16) * HEAD_DIM ** (-0.5)
                target[at, pair * PAIR : (pair + 1) * PAIR] = tile.astype(jnp.bfloat16)

    def attend(pair):
        lanes = pl.ds(pl.multiple_of(pair * PAIR, PAIR), PAIR)
        turned_values[...] = values[:, lanes].astype(jnp.float32).T.astype(jnp.bfloat16)
        for block in range(length // QUERIES):
            at = pl.ds(block * QUERIES, QUERIES)
            reach = (block + 1) * QUERIES
            starts = starts_ref[:, at]
            both = []
            for head in range(2):
                query = one_head(queries[at, lanes], head)
                scores = masked(
                    over_lanes(key_rows[0:reach, lanes], query), starts, block * QUERIES
                )
                peak = jnp.max(scores, axis=0, keepdims=True)
                raised = jnp.exp(scores - peak)
                total = jnp.sum(raised, axis=0, keepdims=True)
                result = jnp.dot(
                    turned_values[head * HEAD_DIM : (head + 1) * HEAD_DIM, 0:reach],
                    raised.astype(jnp.bfloat16),
                    preferred_element_type=jnp.float32,
                )
                both.append(result / total)
                log_totals[2 * pair + head, :, at] = peak + jnp.log(total)
            attended[at, lanes] = jnp.concatenate(both, axis=0).T.astype(jnp.bfloat16)

    pairs = width // PAIR
    pl.loop(0, pairs - 1)(attend)
    cot_gather.step(0, 0)
    pl.loop(pairs - 1, pairs)(attend)

    @pl.when(second_core)
    def _():
        for hop in range(1, n - 1):
            cot_gather.step(0, hop)
        pl.semaphore_wait(turn, 1)

    sums.begin()

    def finish_part(part):
        def body(block):
            at = pl.multiple_of(part * part_rows + block, BLOCK)
            here = pl.ds(at, BLOCK)
            total = totals[me, here, :].astype(jnp.float32)
            field = layer_in[here, :].astype(jnp.float32) + total
            middle[here, :] = field
            place = pl.ds(pl.multiple_of(me * rows + at, BLOCK), BLOCK)
            second_in[place, :] = (field * inverse_scale(field) * gains[1:2, :]).astype(jnp.bfloat16)

        blocks_of(part_rows, body)

    def complete(part):
        sums.last(part)
        finish_part(part)
        gather.start(part)

    for count in range(1, n - 1):
        pl.loop(0, parts)(lambda part: sums.pass_on(part, count))
        if count < n - 2:
            pl.when(jnp.logical_not(second_core))(lambda: cot_gather.step(0, count))
    pl.loop(0, parts)(complete)

    @pl.when(jnp.logical_not(second_core))
    def _():
        pl.semaphore_signal(turn, inc=1, device_id={"dp": mate_of()}, device_id_type=MESH)
        cot_gather.step(0, n - 2)

    for hop in range(n - 1):
        pl.loop(0, parts)(lambda part: gather.step(part, hop))
    cot_gather.drain()
    gather.drain()
    sums.drain()


def attention_forward(first_in, weights, cos_tile, sine_tile, starts, own_rows, layer_in, gains):
    n = lax.axis_size("tensor")
    parts = 4
    length, depth = first_in.shape
    rows, width = own_rows.shape[0], weights.shape[2]
    narrow = jax.ShapeDtypeStruct((length, width), jnp.bfloat16)
    wide = jax.ShapeDtypeStruct((length, depth), jnp.bfloat16)
    outs = [
        narrow,
        narrow,
        narrow,
        narrow,
        jax.ShapeDtypeStruct((width // HEAD_DIM, 1, length), jnp.float32),
        wide,
        jax.ShapeDtypeStruct((rows, depth), jnp.float32),
        wide,
    ]
    specs = whole_part(8)
    specs[0] = pl.BlockSpec(memory_space=pl.ANY)
    return pl.pallas_call(
        functools.partial(attention_forward_kernel, n, parts),
        out_shape=outs,
        in_specs=specs,
        out_specs=whole_part(len(outs)),
        scratch_shapes=[
            pltpu.VMEM((PAIR, length), jnp.bfloat16),
            pltpu.VMEM((2, QUERIES, depth), jnp.bfloat16),
            pltpu.SemaphoreType.DMA((2,)),
        ]
        + gather_scratch(n, 1)
        + gather_scratch(n, parts)
        + [pltpu.SemaphoreType.REGULAR]
        + scatter_scratch(n, parts, rows, depth),
        compiler_params=pltpu.CompilerParams(
            collective_id=5, has_side_effects=True, vmem_limit_bytes=60 * 2**20
        ),
        cost_estimate=pl.CostEstimate(
            flops=8 * length * depth * width, bytes_accessed=400 * 2**20, transcendentals=0
        ),
        name="attention_forward",
    )(first_in, weights, cos_tile, sine_tile, starts, own_rows, layer_in, gains)


def attention_back_kernel(
    n, d_attn, out_weight, queries, key_rows, values, attended, log_totals, cos_ref, sine_ref,
    starts_ref, middle, out_sums, query_raw, key_raw, value_raw, layer_out,
    d_attended, turned_keys, key_sum, value_sum, held, held_sems, totals, run, sent, got
):
    me = lax.axis_index("tensor")
    length, width = queries.shape
    parts = 4
    sums = SumScatter(n, me, parts, [], [], totals, run, sent, got)

    def fetch(block):
        return pltpu.make_async_copy(
            d_attn.at[pl.ds(block * QUERIES, QUERIES), :], held.at[block % 2], held_sems.at[block % 2]
        )

    ready = pltpu.make_async_copy(out_sums, totals, held_sems.at[2])
    ready.start()
    fetch(0).start()
    greet(n, me)
    ready.wait()
    sums.begin()
    for block in range(length // QUERIES):
        fetch(block).wait()
        if (block + 1) * QUERIES < length:
            fetch(block + 1).start()
        d_attended[block * QUERIES : (block + 1) * QUERIES, :] = jnp.dot(
            held[block % 2], out_weight[0], preferred_element_type=jnp.float32
        ).astype(jnp.bfloat16)

    def back_pair(pair):
        lanes = pl.ds(pl.multiple_of(pair * PAIR, PAIR), PAIR)
        turned_keys[...] = key_rows[:, lanes].astype(jnp.float32).T.astype(jnp.bfloat16)
        key_sum[...] = jnp.zeros_like(key_sum)
        value_sum[...] = jnp.zeros_like(value_sum)
        for block in range(length // QUERIES):
            at = pl.ds(block * QUERIES, QUERIES)
            reach = (block + 1) * QUERIES
            starts = starts_ref[:, at]
            grads = d_attended[at, lanes]
            shares = (grads.astype(jnp.float32) * attended[at, lanes].astype(jnp.float32)).T
            both = []
            for head in range(2):
                heads = slice(head * HEAD_DIM, (head + 1) * HEAD_DIM)
                query = one_head(queries[at, lanes], head)
                grad = one_head(grads, head)
                share = jnp.sum(shares[heads], axis=0, keepdims=True)
                scores = masked(
                    over_lanes(key_rows[0:reach, lanes], query), starts, block * QUERIES
                )
                probs = jnp.exp(scores - log_totals[2 * pair + head, :, at])
                prob_grad = over_lanes(values[0:reach, lanes], grad)
                score_grad = (probs * (prob_grad - share)).astype(jnp.bfloat16)
                value_sum[0:reach, :] = value_sum[0:reach, :] + jnp.dot(
                    probs.astype(jnp.bfloat16), grad, preferred_element_type=jnp.float32
                )
                key_sum[0:reach, :] = key_sum[0:reach, :] + jnp.dot(
                    score_grad, query, preferred_element_type=jnp.float32
                )
                both.append(
                    jnp.dot(
                        turned_keys[heads, 0:reach], score_grad, preferred_element_type=jnp.float32
                    )
                )
            query_grad = jnp.concatenate(both, axis=0).T * HEAD_DIM ** (-0.5)
            query_raw[at, lanes] = turned(query_grad, cos_ref[at, :], -sine_ref[at, :]).astype(
                jnp.bfloat16
            )
        key_raw[:, lanes] = turned(key_sum[...], cos_ref[...], -sine_ref[...]).astype(jnp.bfloat16)
        value_raw[:, lanes] = value_sum[...].astype(jnp.bfloat16)

    pairs = width // PAIR
    for count in range(1, n):
        pl.loop(pairs * (count - 1) // (n - 1), pairs * count // (n - 1))(back_pair)
        if count < n - 1:
            pl.loop(0, parts)(lambda part: sums.pass_on(part, count))
    pl.loop(0, parts)(sums.last)

    def body(at):
        rows = pl.ds(at, BLOCK)
        total = middle[rows, :] + totals[me, rows, :].astype(jnp.float32)
        layer_out[rows, :] = total.astype(jnp.bfloat16)

    blocks_of(middle.shape[0], body)
    sums.drain()


def attention_back(
    d_attn, attn_low, queries, key_rows, values, attended, log_totals, cos_tile, sine_tile, starts,
    middle, out_sums
):
    n = lax.axis_size("tensor")
    length, depth = d_attn.shape
    width, rows = queries.shape[1], middle.shape[0]
    narrow = jax.ShapeDtypeStruct((length, width), jnp.bfloat16)
    specs = whole_part(12)
    specs[0] = specs[11] = pl.BlockSpec(memory_space=pl.ANY)
    specs[1] = pl.BlockSpec((1, depth, width), lambda i: (3, 0, 0), pipeline_mode=pl.Buffered(1))
    scratch = scatter_scratch(n, 4, rows, depth)
    scratch[0] = pltpu.VMEM((n, rows, depth), jnp.bfloat16)
    return pl.pallas_call(
        functools.partial(attention_back_kernel, n),
        grid=(1,),
        out_shape=[narrow, narrow, narrow, jax.ShapeDtypeStruct((rows, depth), jnp.bfloat16)],
        in_specs=specs,
        out_specs=whole_part(4),
        scratch_shapes=[
            pltpu.VMEM((length, width), jnp.bfloat16),
            pltpu.VMEM((PAIR, length), jnp.bfloat16),
            pltpu.VMEM((length, PAIR), jnp.float32),
            pltpu.VMEM((length, PAIR), jnp.float32),
            pltpu.VMEM((2, QUERIES, depth), jnp.bfloat16),
            pltpu.SemaphoreType.DMA((3,)),
        ]
        + scratch,
        compiler_params=pltpu.CompilerParams(
            collective_id=6, has_side_effects=True, vmem_limit_bytes=60 * 2**20
        ),
        cost_estimate=pl.CostEstimate(
            flops=2 * length * depth * width, bytes_accessed=200 * 2**20, transcendentals=0
        ),
        name="attention_back",
    )(
        d_attn, attn_low, queries, key_rows, values, attended, log_totals, cos_tile, sine_tile,
        starts, middle, out_sums.reshape(n, rows, depth)
    )


def turn_into(target, source):
    @pl.loop(0, source.shape[0] // TILE)
    def _(block):
        at = pl.ds(pl.multiple_of(block * TILE, TILE), TILE)
        for k in range(source.shape[1] // TILE):
            columns = slice(k * TILE, (k + 1) * TILE)
            target[columns, at] = source[at, columns].astype(jnp.float32).T.astype(jnp.bfloat16)


def mlp_kernel(second_in, cotangent, weights, hidden, d_gate, d_up, grads, second_turned, cot_turned):
    @pl.when(pl.program_id(0) == 0)
    def _():
        turn_into(second_turned, second_in)
        turn_into(cot_turned, cotangent)

    for block in range(second_in.shape[0] // QUERIES):
        at = slice(block * QUERIES, (block + 1) * QUERIES)
        source = second_in[at, :]
        gate_proj = jnp.dot(source, weights[0], preferred_element_type=jnp.float32)
        up_proj = jnp.dot(source, weights[1], preferred_element_type=jnp.float32)
        d_hidden = jnp.dot(cotangent[at, :], weights[2], preferred_element_type=jnp.float32)
        sigmoid_gate = jax.nn.sigmoid(gate_proj)
        silu = gate_proj * sigmoid_gate
        hidden[at, :] = (silu * up_proj).astype(jnp.bfloat16)
        slope = sigmoid_gate * (1.0 + gate_proj * (1.0 - sigmoid_gate))
        d_gate[at, :] = (d_hidden * up_proj * slope).astype(jnp.bfloat16)
        d_up[at, :] = (d_hidden * silu).astype(jnp.bfloat16)
    for which, (left, right) in enumerate(
        ((second_turned, d_gate), (second_turned, d_up), (cot_turned, hidden))
    ):

        @pl.loop(0, left.shape[0] // 512)
        def _(block):
            at = pl.ds(pl.multiple_of(block * 512, 512), 512)
            grads[which, at, :] = jnp.dot(
                left[at, :], right[...], preferred_element_type=jnp.float32
            ).astype(jnp.bfloat16)


def mlp_middle(second_in, cotangent, weights):
    length, depth = second_in.shape
    units = weights.shape[2]
    tile = 256
    wide = jax.ShapeDtypeStruct((length, units), jnp.bfloat16)
    column = pl.BlockSpec((length, tile), lambda j: (0, j))
    stacked = pl.BlockSpec((3, depth, tile), lambda j: (0, 0, j))
    return pl.pallas_call(
        mlp_kernel,
        grid=(units // tile,),
        out_shape=[wide, wide, wide, jax.ShapeDtypeStruct((3, depth, units), jnp.bfloat16)],
        in_specs=whole_part(2) + [stacked],
        out_specs=[column, column, column, stacked],
        scratch_shapes=[pltpu.VMEM((depth, length), jnp.bfloat16)] * 2,
        compiler_params=pltpu.CompilerParams(vmem_limit_bytes=60 * 2**20),
        cost_estimate=pl.CostEstimate(
            flops=12 * length * depth * units, bytes_accessed=60 * 2**20, transcendentals=0
        ),
        name="mlp_middle",
    )(second_in, cotangent, weights)


def grads_kernel(first_in, query_raw, key_raw, value_raw, d_attn, attended, grads, turned_rows):
    which = pl.program_id(0)
    pl.when(which == 0)(lambda: turn_into(turned_rows, first_in))
    pl.when(which == 3)(lambda: turn_into(turned_rows, d_attn))
    for k, right in enumerate((query_raw, key_raw, value_raw, attended)):

        @pl.when(which == k)
        def _():
            @pl.loop(0, turned_rows.shape[0] // 512)
            def _(block):
                at = pl.ds(pl.multiple_of(block * 512, 512), 512)
                grads[at, :] = jnp.dot(
                    turned_rows[at, :], right[...], preferred_element_type=jnp.float32
                ).astype(jnp.bfloat16)


def attention_grads(first_in, query_raw, key_raw, value_raw, d_attn, attended):
    length, depth = first_in.shape
    width = attended.shape[1]
    return pl.pallas_call(
        grads_kernel,
        grid=(4,),
        out_shape=jax.ShapeDtypeStruct((4, depth, width), jnp.bfloat16),
        in_specs=whole_part(6),
        out_specs=pl.BlockSpec((None, depth, width), lambda j: (j, 0, 0)),
        scratch_shapes=[pltpu.VMEM((depth, length), jnp.bfloat16)],
        compiler_params=pltpu.CompilerParams(vmem_limit_bytes=60 * 2**20),
        cost_estimate=pl.CostEstimate(
            flops=8 * length * depth * width, bytes_accessed=20 * 2**20, transcendentals=0
        ),
        name="attention_grads",
    )(first_in, query_raw, key_raw, value_raw, d_attn, attended)


def attn_rates():
    return jnp.array([1.0, 1.0, 1.0, 8.0**0.5], jnp.float32).reshape(4, 1, 1) * (0.5 * D ** (-0.5))


def adam_update(weight, gradient, moment_one, moment_two, step_rate):
    first_new = BETA_ONE * moment_one + (1.0 - BETA_ONE) * gradient
    second_new = BETA_TWO * moment_two + (1.0 - BETA_TWO) * gradient * gradient
    fix_one = 1.0 - BETA_ONE**STEP
    fix_two = 1.0 - BETA_TWO**STEP
    weight_new = weight - step_rate * (
        first_new / fix_one / (jnp.sqrt(second_new / fix_two) + EPS_ADAM) + WEIGHT_DECAY * weight
    )
    return (first_new, second_new, weight_new)


def local(
    inputs,
    cotangent,
    doc_lengths,
    norm_gains,
    attn_weight,
    mlp_weight,
    gain_first,
    attn_first,
    mlp_first,
    gain_second,
    attn_second,
    mlp_second,
):
    row_count = inputs.shape[0]
    seq_length = row_count * lax.axis_size("tensor")
    segment, position = doc_layout(doc_lengths[0], seq_length)
    cos_tile, sine_tile = rope_tables(position)
    starts = (jnp.arange(seq_length, dtype=jnp.int32) - position)[None, :]
    width = inputs.shape[1]
    rows_f32 = jax.ShapeDtypeStruct((row_count, width), jnp.float32)
    gain_f32 = jax.ShapeDtypeStruct((8, width), jnp.float32)
    exchange = functools.partial(line_exchange, rows=row_count, width=width)
    (first_in,) = exchange(
        "first_norm", 1, [], [inputs, norm_gains], [], finish=first_norm, gathers=True, parts=4
    )
    attn_low = lax.all_gather(attn_weight.astype(jnp.bfloat16), "dp", axis=1, tiled=True)

    (
        queries, key_rows, values, attended, log_totals, grad_out, middle, second_in
    ) = attention_forward(
        first_in, attn_low, cos_tile, sine_tile, starts, cotangent, inputs, norm_gains
    )
    mlp_low = lax.all_gather(mlp_weight.astype(jnp.bfloat16), "dp", axis=1, tiled=True)
    hidden, d_gate, d_up, mlp_sums = mlp_middle(second_in, grad_out, mlp_low)

    mlp_owned = lax.psum_scatter(mlp_sums, "dp", scatter_dimension=1, tiled=True)
    d_middle, gain_two, d_attn, out_sums = exchange(
        "mlp_back",
        3,
        [(d_gate, mlp_low, 0), (d_up, mlp_low, 1)],
        [middle, cotangent, norm_gains],
        [rows_f32, gain_f32],
        finish=second_back,
        gathers=True,
        parts=4,
        side=(hidden, mlp_low),
    )
    query_raw, key_raw, value_raw, layer_out = attention_back(
        d_attn, attn_low, queries, key_rows, values, attended, log_totals, cos_tile, sine_tile,
        starts, middle, out_sums
    )
    attn_sums, mlp_owned = lax.optimization_barrier(
        (attention_grads(first_in, query_raw, key_raw, value_raw, d_attn, attended), mlp_owned)
    )
    attn_owned = lax.psum_scatter(attn_sums, "dp", scatter_dimension=1, tiled=True)
    mlp_grad, attn_grad = mlp_owned.astype(jnp.float32), attn_owned.astype(jnp.float32)
    grad_in, gain_one = exchange(
        "input_back",
        4,
        [(query_raw, attn_low, 0), (key_raw, attn_low, 1), (value_raw, attn_low, 2)],
        [inputs, d_middle, norm_gains],
        [rows_f32, gain_f32],
        finish=first_back,
        gathers=False,
        parts=4,
    )
    gain_parts = jnp.stack([jnp.sum(gain_one, axis=0), jnp.sum(gain_two, axis=0)])
    gain_grad = sum_everywhere(gain_parts.reshape(8, -1)).reshape(norm_gains.shape)
    gain_first_new, gain_second_new, gain_new = adam_update(
        norm_gains, gain_grad, gain_first, gain_second, GAIN_RATE
    )
    attn_first_new, attn_second_new, attn_new = adam_update(
        attn_weight, attn_grad, attn_first, attn_second, attn_rates()
    )
    mlp_first_new, mlp_second_new, mlp_new = adam_update(
        mlp_weight, mlp_grad, mlp_first, mlp_second, 0.5 * D ** (-0.5)
    )
    return (
        layer_out,
        grad_in,
        gain_grad,
        attn_grad,
        mlp_grad,
        gain_first_new,
        attn_first_new,
        mlp_first_new,
        gain_second_new,
        attn_second_new,
        mlp_second_new,
        gain_new,
        attn_new,
        mlp_new,
    )


def solution(mesh):
    placed = (
        P(("dp", "tensor"), None),
        P(("dp", "tensor"), None),
        P("dp", None),
        P(),
        P(None, "dp", "tensor"),
        P(None, "dp", "tensor"),
        P(),
        P(None, "dp", "tensor"),
        P(None, "dp", "tensor"),
        P(),
        P(None, "dp", "tensor"),
        P(None, "dp", "tensor"),
    )
    return jax.shard_map(
        local,
        mesh=mesh,
        in_specs=placed,
        out_specs=(
            P(("dp", "tensor"), None),
            P(("dp", "tensor"), None),
            P(),
            P(None, "dp", "tensor"),
            P(None, "dp", "tensor"),
            P(),
            P(None, "dp", "tensor"),
            P(None, "dp", "tensor"),
            P(),
            P(None, "dp", "tensor"),
            P(None, "dp", "tensor"),
            P(),
            P(None, "dp", "tensor"),
            P(None, "dp", "tensor"),
        ),
        check_vma=False,
    )
```

```python
import functools

import jax
import jax.numpy as jnp
from jax import lax
from jax.experimental import pallas as pl
from jax.experimental.pallas import tpu as pltpu
from jax.sharding import PartitionSpec as P

D = 2048
HEAD_DIM = 64
STEP = 10


EPS_NORM = 1e-05
ROPE_BASE = 130000.0
BETA_ONE = 0.9
BETA_TWO = 0.95
EPS_ADAM = 1e-08
WEIGHT_DECAY = 0.1
GAIN_RATE = 0.3
MASKED = -1e30


def doc_layout(lengths, seq_length):
    doc_ends = jnp.cumsum(lengths)
    starts = doc_ends - lengths
    places = jnp.arange(seq_length, dtype=jnp.int32)
    segment = jnp.sum((places[:, None] >= doc_ends[None, :]).astype(jnp.int32), axis=1)
    owners = segment[:, None] == jnp.arange(lengths.shape[0], dtype=jnp.int32)[None, :]
    position = places - jnp.sum(jnp.where(owners, starts[None, :], 0), axis=1)
    return (segment, position)


def rope_tables(position):
    half_dim = HEAD_DIM // 2
    frequencies = jnp.power(
        jnp.float32(ROPE_BASE), -2.0 * jnp.arange(half_dim, dtype=jnp.float32) / HEAD_DIM
    )
    angles = position.astype(jnp.float32)[:, None] * frequencies[None, :]
    cosine, sine = jnp.cos(angles), jnp.sin(angles)
    return (
        jnp.concatenate([cosine, cosine] * 2, axis=1),
        jnp.concatenate([-sine, sine] * 2, axis=1),
    )


MESH = pl.DeviceIdType.MESH
BLOCK = 32
TILE = 256


def whole_part(count):
    return [pl.BlockSpec(memory_space=pltpu.VMEM)] * count


def mate_of():
    place = lax.axis_index("dp")
    return place + 1 - 2 * (place % 2)


def signal_mate(semaphore):
    pl.semaphore_signal(semaphore, inc=1, device_id={"dp": mate_of()}, device_id_type=MESH)


def greet(n, me, here=None):
    barrier = pltpu.get_barrier_semaphore()
    for there, step in ((me > 0, -1), (me < n - 1, 1)):

        @pl.when(there)
        def _():
            pl.semaphore_signal(barrier, inc=1, device_id={"tensor": me + step}, device_id_type=MESH)

    count = (me > 0).astype(jnp.int32) + (me < n - 1).astype(jnp.int32)
    if here is not None:
        second_core = lax.axis_index("dp") % 2
        pl.when(second_core == 0)(lambda: signal_mate(barrier))
        count = count + second_core
    pl.semaphore_wait(barrier, count)
    if here is not None:
        pl.when(second_core == 1)(lambda: signal_mate(here))


def blocks_of(count, body):
    @pl.loop(0, count // BLOCK)
    def _(block):
        body(pl.multiple_of(block * BLOCK, BLOCK))


class RowGather:
    def __init__(self, n, me, parts, place, sent, got):
        self.n, self.me, self.parts, self.place = n, me, parts, place
        self.sent, self.got = sent, got
        self.rows = place.shape[0] // n
        self.has_left, self.has_right = me > 0, me < n - 1

    def copy(self, way, part, hop, owner):
        count = self.rows // self.parts
        first = pl.multiple_of(owner * self.rows + part * count, count)
        block = self.place.at[pl.ds(first, count), :]
        slot = part * (self.n - 1) + hop
        return pltpu.make_async_remote_copy(
            src_ref=block,
            dst_ref=block,
            send_sem=self.sent.at[way, slot],
            recv_sem=self.got.at[way, slot],
            device_id={"tensor": self.me + 1 - 2 * way},
            device_id_type=MESH,
        )

    def start(self, part):
        pl.when(self.has_right)(lambda: self.copy(0, part, 0, self.me).start())
        pl.when(self.has_left)(lambda: self.copy(1, part, 0, self.me).start())

    def step(self, part, hop):
        last = hop + 1 == self.n - 1

        @pl.when(hop < self.me)
        def _():
            owner = self.me - 1 - hop
            self.copy(0, part, hop, owner).wait_recv()
            if not last:
                pl.when(self.has_right)(lambda: self.copy(0, part, hop + 1, owner).start())

        @pl.when(hop < self.n - 1 - self.me)
        def _():
            owner = self.me + 1 + hop
            self.copy(1, part, hop, owner).wait_recv()
            if not last:
                pl.when(self.has_left)(lambda: self.copy(1, part, hop + 1, owner).start())

    def drain(self):
        @pl.loop(0, self.parts)
        def _(part):
            for hop in range(self.n - 1):
                pl.when(self.has_right & (hop <= self.me))(
                    lambda: self.copy(0, part, hop, self.me - hop).wait_send()
                )
                pl.when(self.has_left & (hop <= self.n - 1 - self.me))(
                    lambda: self.copy(1, part, hop, self.me + hop).wait_send()
                )


class SumScatter:
    def __init__(self, n, me, parts, lefts, rights, totals, run, sent, got):
        self.n, self.me, self.parts = n, me, parts
        self.lefts, self.rights, self.totals, self.run = lefts, rights, totals, run
        self.sent, self.got = sent, got
        self.rows = totals.shape[1]
        self.fed = (me > 0, me < n - 1)

    def copy(self, way, part, hop):
        slot = part * (self.n - 1) + hop
        run = self.run.at[self.place(way, part, hop)]
        return pltpu.make_async_remote_copy(
            src_ref=run,
            dst_ref=run,
            send_sem=self.sent.at[way, slot],
            recv_sem=self.got.at[way, slot],
            device_id={"tensor": self.me + 1 - 2 * way},
            device_id_type=MESH,
        )

    def product(self, dest):
        first = pl.multiple_of(dest * self.rows, self.rows)

        @pl.loop(0, self.totals.shape[2] // TILE)
        def _(tile):
            columns = pl.ds(pl.multiple_of(tile * TILE, TILE), TILE)
            value = None
            for left, right in zip(self.lefts, self.rights):
                term = lax.dot_general(
                    left[pl.ds(first, self.rows), :],
                    right[columns, :],
                    (((1,), (1,)), ((), ())),
                    preferred_element_type=jnp.float32,
                )
                value = term if value is None else value + term
            self.totals[dest, :, columns] = value.astype(self.totals.dtype)

    def place(self, way, part, hop):
        return part * (self.n + 1) + (hop, self.n - hop)[way]

    def begin(self):
        part_rows = self.rows // self.parts
        for hop in range(self.n - 1):
            for way, dest in ((0, self.n - 1 - hop), (1, hop)):
                needed = (dest > self.me, dest < self.me)[way]
                if self.lefts:
                    pl.when(needed)(lambda: self.product(dest))

                @pl.when(needed & jnp.logical_not(self.fed[way]))
                def _():
                    @pl.loop(0, self.parts)
                    def _(part):
                        slot = self.place(way, part, hop)

                        def body(at):
                            first = pl.multiple_of(part * part_rows + at, BLOCK)
                            own = self.totals[dest, pl.ds(first, BLOCK), :]
                            self.run[slot, pl.ds(at, BLOCK), :] = own.astype(jnp.bfloat16)

                        blocks_of(part_rows, body)
                        self.copy(way, part, hop).start()

        if self.lefts:
            self.product(self.me)

    def arrivals(self, count):
        for way, behind in ((0, self.me), (1, self.n - 1 - self.me)):
            hop = count - behind
            yield way, hop, (self.n - 1 - hop, hop)[way], self.fed[way] & (hop >= 0)

    def pass_on(self, part, count):
        for way, hop, dest, there in self.arrivals(count):
            run, slot = self.run, self.place(way, part, hop)
            first = part * (self.rows // self.parts)

            @pl.when(there)
            def _():
                self.copy(way, part, hop).wait_recv()

                def body(at):
                    here = pl.ds(pl.multiple_of(first + at, BLOCK), BLOCK)
                    own = self.totals[dest, here, :].astype(jnp.float32)
                    came = run[slot, pl.ds(at, BLOCK), :].astype(jnp.float32)
                    run[slot, pl.ds(at, BLOCK), :] = (own + came).astype(jnp.bfloat16)

                blocks_of(self.rows // self.parts, body)
                self.copy(way, part, hop).start()

    def last(self, part):
        first = part * (self.rows // self.parts)
        for way, hop, dest, there in self.arrivals(self.n - 1):
            run, slot = self.run, self.place(way, part, hop)

            @pl.when(there)
            def _():
                self.copy(way, part, hop).wait_recv()

                def body(at):
                    own = pl.ds(pl.multiple_of(first + at, BLOCK), BLOCK)
                    came = run[slot, pl.ds(at, BLOCK), :].astype(jnp.float32)
                    total = self.totals[self.me, own, :].astype(jnp.float32) + came
                    self.totals[self.me, own, :] = total.astype(self.totals.dtype)

                blocks_of(self.rows // self.parts, body)

    def drain(self):
        @pl.loop(0, self.parts)
        def _(part):
            for hop in range(self.n - 1):
                pl.when(self.n - 1 - hop > self.me)(lambda: self.copy(0, part, hop).wait_send())
                pl.when(hop < self.me)(lambda: self.copy(1, part, hop).wait_send())


def scatter_scratch(n, parts, rows, width):
    slots = parts * (n - 1)
    kept = jnp.float32 if n * rows * width <= 2**21 else jnp.bfloat16
    return [
        pltpu.VMEM((n, rows, width), kept),
        pltpu.VMEM((parts * (n + 1), rows // parts, width), jnp.bfloat16),
        pltpu.SemaphoreType.DMA((2, slots)),
        pltpu.SemaphoreType.DMA((2, slots)),
    ]


def gather_scratch(n, parts):
    return [pltpu.SemaphoreType.DMA((2, parts * (n - 1)))] * 2


class SideProduct:
    def __init__(self, source, columns, target, held, weight, staged, sems):
        self.source, self.columns, self.target = source, columns, target
        self.held, self.weight, self.staged, self.sems = held, weight, staged, sems
        self.count = source.shape[0] // QUERIES
        self.done = 0

    def fetch(self, block):
        return pltpu.make_async_copy(
            self.source.at[pl.ds(block * QUERIES, QUERIES), :],
            self.held.at[block % 2],
            self.sems.at[block % 2],
        )

    def store(self, block):
        return pltpu.make_async_copy(
            self.staged.at[block % 2],
            self.target.at[pl.ds(block * QUERIES, QUERIES), :],
            self.sems.at[2 + block % 2],
        )

    def fetch_weight(self):
        return pltpu.make_async_copy(self.columns.at[2], self.weight, self.sems.at[4])

    def open(self, lefts):
        self.fetch_weight().start()
        self.fetch(0).start()

    def step(self):
        block = self.done
        if block == self.count:
            return
        if block == 0:
            self.fetch_weight().wait()
        self.fetch(block).wait()
        if block + 1 < self.count:
            self.fetch(block + 1).start()
        if block >= 2:
            self.store(block - 2).wait()

        @pl.loop(0, self.weight.shape[0] // TILE)
        def _(tile):
            columns = pl.ds(pl.multiple_of(tile * TILE, TILE), TILE)
            self.staged[block % 2, :, columns] = over_lanes(
                self.held[block % 2], self.weight[columns, :]
            ).astype(jnp.bfloat16)

        self.store(block).start()
        self.done = block + 1

    def close(self):
        while self.done < self.count:
            self.step()
        for block in range(max(0, self.count - 2), self.count):
            self.store(block).wait()


def side_scratch(depth, units):
    return [
        pltpu.VMEM((2, QUERIES, units), jnp.bfloat16),
        pltpu.VMEM((depth, units), jnp.bfloat16),
        pltpu.VMEM((2, QUERIES, depth), jnp.bfloat16),
        pltpu.SemaphoreType.DMA((5,)),
    ]


def line_kernel(n, parts, products, extras, outs, gathers, side, turn_hop, finish, *refs):
    refs = list(refs)
    take = lambda count: [refs.pop(0) for _ in range(count)]
    lefts, rights, more = take(products), take(products), take(extras)
    side_in = take(2) if side else None
    results = take(outs)
    gathered = take(1)[0] if gathers else None
    filler = SideProduct(*side_in, *take(1), *[refs.pop() for _ in range(4)][::-1]) if side else None
    me = lax.axis_index("tensor")
    if products:
        totals = refs[0]
        sums = SumScatter(n, me, parts, lefts, rights, *take(4))
    if gathers:
        gather = RowGather(n, me, parts, gathered, *take(2))
    rows = totals.shape[1] if products else gathered.shape[0] // n
    part_rows = rows // parts

    def finish_part(part):
        def body(block):
            at = pl.multiple_of(part * part_rows + block, BLOCK)
            total = totals[me, pl.ds(at, BLOCK), :].astype(jnp.float32) if products else None
            sent_rows = finish(at, total, more, results)
            if gathers:
                gathered[pl.ds(pl.multiple_of(me * rows + at, BLOCK), BLOCK), :] = sent_rows

        blocks_of(part_rows, body)

    second_core = lax.axis_index("dp") % 2 == 1
    if turn_hop is None:
        greet(n, me)
    else:
        turns = take(1)[0]
        greet(n, me, turns.at[1])
    for result in results:
        if result.shape[0] == 8:
            result[...] = jnp.zeros_like(result)
    if products:
        sums.begin()
    if filler:
        filler.open(lefts)
    def complete(part):
        if products:
            sums.last(part)
        finish_part(part)
        if gathers:
            gather.start(part)

    if products:
        for count in range(1, n - 1):
            if filler:
                filler.step()
            pl.loop(0, parts)(lambda part: sums.pass_on(part, count))
        if filler:
            filler.step()
    if turn_hop is not None:
        pl.when(second_core)(lambda: pl.semaphore_wait(turns.at[0], 1))
    pl.loop(0, parts)(complete)
    if gathers:
        for hop in range(n - 1):
            if filler:
                filler.step()
            pl.loop(0, parts)(lambda part: gather.step(part, hop))
            if hop == turn_hop:

                @pl.when(jnp.logical_not(second_core))
                def _():
                    pl.semaphore_wait(turns.at[1], 1)
                    signal_mate(turns.at[0])

        gather.drain()
    if filler:
        filler.close()
    if products:
        sums.drain()


def line_exchange(
    name, collective_id, pairs, extras, outs, rows, width, finish, gathers, parts, side=(), turn_hop=None
):
    n = lax.axis_size("tensor")
    scratch = scatter_scratch(n, parts, rows, width) if pairs else []
    if gathers:
        scratch = scratch + gather_scratch(n, parts)
        outs = outs + [jax.ShapeDtypeStruct((n * rows, width), jnp.bfloat16)]
    operands = [pair[0] for pair in pairs] + [pair[1] for pair in pairs] + list(extras)
    specs = whole_part(len(operands)) + [pl.BlockSpec(memory_space=pl.ANY)] * len(side)
    own_outs = len(outs) - gathers
    out_specs = whole_part(len(outs))
    operands = operands + list(side)
    if side:
        outs = outs + [jax.ShapeDtypeStruct((side[0].shape[0], width), jnp.bfloat16)]
        out_specs = out_specs + [pl.BlockSpec(memory_space=pl.ANY)]
        scratch = scratch + side_scratch(width, side[0].shape[1])
    if turn_hop is not None:
        scratch = scratch + [pltpu.SemaphoreType.REGULAR((2,))]
    for k, (left, right, which) in enumerate(pairs):
        specs[len(pairs) + k] = pl.BlockSpec(
            (None, *right.shape[1:]), lambda i, which=which: (which, 0, 0), pipeline_mode=pl.Buffered(1)
        )
    return pl.pallas_call(
        functools.partial(
            line_kernel, n, parts, len(pairs), len(extras), own_outs, gathers, len(side) > 0, turn_hop, finish
        ),
        grid=(1,),
        out_shape=outs,
        in_specs=specs,
        out_specs=out_specs,
        scratch_shapes=scratch,
        compiler_params=pltpu.CompilerParams(
            collective_id=collective_id, has_side_effects=True, vmem_limit_bytes=60 * 2**20
        ),
        cost_estimate=pl.CostEstimate(
            flops=2 * n * rows * width, bytes_accessed=rows * width, transcendentals=0
        ),
        name=name,
    )(*operands)


def everywhere_kernel(sizes, field, result, came, sent, got):
    places = [lax.axis_index(name) for name in sizes]
    partners = []
    for name, place in zip(sizes, places):
        stride = 1
        while stride < sizes[name]:
            other = place + stride - 2 * stride * (place // stride % 2)
            partners.append({name: other})
            stride = 2 * stride
    barrier = pltpu.get_barrier_semaphore()
    for partner in partners:
        pl.semaphore_signal(barrier, inc=1, device_id=partner, device_id_type=MESH)
    pl.semaphore_wait(barrier, len(partners))
    result[...] = field[...]
    for k, partner in enumerate(partners):
        came[2 * k] = result[...]
        copy = pltpu.make_async_remote_copy(
            src_ref=came.at[2 * k],
            dst_ref=came.at[2 * k + 1],
            send_sem=sent.at[k],
            recv_sem=got.at[k],
            device_id=partner,
            device_id_type=MESH,
        )
        copy.start()
        copy.wait()
        result[...] = result[...] + came[2 * k + 1]


def sum_everywhere(field):
    sizes = {name: lax.axis_size(name) for name in ("dp", "tensor")}
    steps = sum(size.bit_length() - 1 for size in sizes.values())
    return pl.pallas_call(
        functools.partial(everywhere_kernel, sizes),
        out_shape=jax.ShapeDtypeStruct(field.shape, jnp.float32),
        in_specs=whole_part(1),
        out_specs=pl.BlockSpec(memory_space=pltpu.VMEM),
        scratch_shapes=[
            pltpu.VMEM((2 * steps, *field.shape), jnp.float32),
            pltpu.SemaphoreType.DMA((steps,)),
            pltpu.SemaphoreType.DMA((steps,)),
        ],
        compiler_params=pltpu.CompilerParams(collective_id=7, has_side_effects=True),
        name="gain_sum",
    )(field)


def inverse_scale(field):
    return lax.rsqrt(jnp.mean(field * field, axis=-1, keepdims=True) + EPS_NORM)


def first_norm(at, total, more, results):
    layer_in, gains = more
    field = layer_in[pl.ds(at, BLOCK), :].astype(jnp.float32)
    return (field * inverse_scale(field) * gains[0:1, :]).astype(jnp.bfloat16)


def norm_back(field, gradient, gain_row, gain_out):
    inv_scale = inverse_scale(field)
    normed = field * inv_scale
    scaled = gradient * gain_row
    back = inv_scale * (scaled - normed * jnp.mean(scaled * normed, axis=-1, keepdims=True))
    product = gradient * normed
    folded = product[0:8]
    for k in range(8, BLOCK, 8):
        folded = folded + product[k : k + 8]
    gain_out[...] = gain_out[...] + folded
    return back


def second_back(at, total, more, results):
    middle, cotangent, gains = more
    rows = pl.ds(at, BLOCK)
    back = norm_back(middle[rows, :], total, gains[1:2, :], results[1])
    back = back + cotangent[rows, :].astype(jnp.float32)
    results[0][rows, :] = back
    return back.astype(jnp.bfloat16)


def first_back(at, total, more, results):
    layer_in, d_middle, gains = more
    rows = pl.ds(at, BLOCK)
    back = norm_back(layer_in[rows, :].astype(jnp.float32), total, gains[0:1, :], results[1])
    results[0][rows, :] = back + d_middle[rows, :]


PAIR = 2 * HEAD_DIM
QUERIES = 256


def turned(field, cos_tile, sine_tile):
    lanes = lax.broadcasted_iota(jnp.int32, field.shape, 1)
    ahead = pltpu.roll(field, PAIR - HEAD_DIM // 2, 1)
    behind = pltpu.roll(field, HEAD_DIM // 2, 1)
    partner = jnp.where(lanes % HEAD_DIM < HEAD_DIM // 2, ahead, behind)
    return field * cos_tile + partner * sine_tile


def one_head(tile, head):
    lanes = lax.broadcasted_iota(jnp.int32, tile.shape, 1)
    return jnp.where(lanes // HEAD_DIM == head, tile, jnp.zeros_like(tile))


def over_lanes(left, right):
    return lax.dot_general(
        left, right, (((1,), (1,)), ((), ())), preferred_element_type=jnp.float32
    )


def masked(scores, starts, first_query):
    keys = lax.broadcasted_iota(jnp.int32, scores.shape, 0)
    queries = first_query + lax.broadcasted_iota(jnp.int32, scores.shape, 1)
    return jnp.where((keys >= starts) & (keys <= queries), scores, MASKED)


def attention_forward_kernel(
    n, parts, first_in, weights, cos_ref, sine_ref, starts_ref, own_rows, layer_in, gains,
    queries, key_rows, values, attended, log_totals, cot_rows, middle, second_in,
    turned_values, held, held_sems, cot_sent, cot_got, rows_sent, rows_got, turns, totals, run,
    sums_sent, sums_got
):
    me = lax.axis_index("tensor")
    second_core = lax.axis_index("dp") % 2 == 1
    rows = own_rows.shape[0]
    part_rows = rows // parts
    length, width = queries.shape

    def fetch(block):
        return pltpu.make_async_copy(
            first_in.at[pl.ds(block * QUERIES, QUERIES), :], held.at[block % 2], held_sems.at[block % 2]
        )

    fetch(0).start()
    greet(n, me, turns.at[1])
    cot_gather = RowGather(n, me, 1, cot_rows, cot_sent, cot_got)
    gather = RowGather(n, me, parts, second_in, rows_sent, rows_got)
    sums = SumScatter(
        n, me, parts, [attended], [weights.at[3]], totals, run, sums_sent, sums_got
    )

    def place_own(at):
        place = pl.ds(pl.multiple_of(me * rows + at, BLOCK), BLOCK)
        cot_rows[place, :] = own_rows[pl.ds(at, BLOCK), :]

    blocks_of(rows, place_own)
    cot_gather.start(0)

    for block in range(length // QUERIES):
        fetch(block).wait()
        if (block + 1) * QUERIES < length:
            fetch(block + 1).start()
        at = pl.ds(block * QUERIES, QUERIES)
        source = held[block % 2]
        cos_tile, sine_tile = cos_ref[at, :], sine_ref[at, :]
        for which, target in enumerate((queries, key_rows, values)):
            field = jnp.dot(source, weights[which], preferred_element_type=jnp.float32)
            for pair in range(width // PAIR):
                tile = field[:, pair * PAIR : (pair + 1) * PAIR]
                if which < 2:
                    tile = turned(tile, cos_tile, sine_tile)
                if which == 0:
                    tile = tile.astype(jnp.bfloat16) * HEAD_DIM ** (-0.5)
                target[at, pair * PAIR : (pair + 1) * PAIR] = tile.astype(jnp.bfloat16)

    def attend(pair):
        lanes = pl.ds(pl.multiple_of(pair * PAIR, PAIR), PAIR)
        turned_values[...] = values[:, lanes].astype(jnp.float32).T.astype(jnp.bfloat16)
        for block in range(length // QUERIES):
            at = pl.ds(block * QUERIES, QUERIES)
            reach = (block + 1) * QUERIES
            starts = starts_ref[:, at]
            both = []
            for head in range(2):
                query = one_head(queries[at, lanes], head)
                scores = masked(
                    over_lanes(key_rows[0:reach, lanes], query), starts, block * QUERIES
                )
                peak = jnp.max(scores, axis=0, keepdims=True)
                raised = jnp.exp(scores - peak)
                total = jnp.sum(raised, axis=0, keepdims=True)
                result = jnp.dot(
                    turned_values[head * HEAD_DIM : (head + 1) * HEAD_DIM, 0:reach],
                    raised.astype(jnp.bfloat16),
                    preferred_element_type=jnp.float32,
                )
                both.append(result / total)
                log_totals[2 * pair + head, :, at] = peak + jnp.log(total)
            attended[at, lanes] = jnp.concatenate(both, axis=0).T.astype(jnp.bfloat16)

    pairs = width // PAIR
    pl.loop(0, pairs - 1)(attend)
    cot_gather.step(0, 0)
    pl.loop(pairs - 1, pairs)(attend)

    @pl.when(second_core)
    def _():
        for hop in range(1, n - 1):
            cot_gather.step(0, hop)
        pl.semaphore_wait(turns.at[0], 1)

    sums.begin()

    def finish_part(part):
        def body(block):
            at = pl.multiple_of(part * part_rows + block, BLOCK)
            here = pl.ds(at, BLOCK)
            total = totals[me, here, :].astype(jnp.float32)
            field = layer_in[here, :].astype(jnp.float32) + total
            middle[here, :] = field
            place = pl.ds(pl.multiple_of(me * rows + at, BLOCK), BLOCK)
            second_in[place, :] = (field * inverse_scale(field) * gains[1:2, :]).astype(jnp.bfloat16)

        blocks_of(part_rows, body)

    def complete(part):
        sums.last(part)
        finish_part(part)
        gather.start(part)

    for count in range(1, n - 1):
        pl.loop(0, parts)(lambda part: sums.pass_on(part, count))
        if count < n - 2:
            pl.when(jnp.logical_not(second_core))(lambda: cot_gather.step(0, count))
    pl.loop(0, parts)(complete)

    @pl.when(jnp.logical_not(second_core))
    def _():
        pl.semaphore_wait(turns.at[1], 1)
        signal_mate(turns.at[0])
        cot_gather.step(0, n - 2)

    for hop in range(n - 1):
        pl.loop(0, parts)(lambda part: gather.step(part, hop))
    cot_gather.drain()
    gather.drain()
    sums.drain()


def attention_forward(first_in, weights, cos_tile, sine_tile, starts, own_rows, layer_in, gains):
    n = lax.axis_size("tensor")
    parts = 4
    length, depth = first_in.shape
    rows, width = own_rows.shape[0], weights.shape[2]
    narrow = jax.ShapeDtypeStruct((length, width), jnp.bfloat16)
    wide = jax.ShapeDtypeStruct((length, depth), jnp.bfloat16)
    outs = [
        narrow,
        narrow,
        narrow,
        narrow,
        jax.ShapeDtypeStruct((width // HEAD_DIM, 1, length), jnp.float32),
        wide,
        jax.ShapeDtypeStruct((rows, depth), jnp.float32),
        wide,
    ]
    specs = whole_part(8)
    specs[0] = pl.BlockSpec(memory_space=pl.ANY)
    return pl.pallas_call(
        functools.partial(attention_forward_kernel, n, parts),
        out_shape=outs,
        in_specs=specs,
        out_specs=whole_part(len(outs)),
        scratch_shapes=[
            pltpu.VMEM((PAIR, length), jnp.bfloat16),
            pltpu.VMEM((2, QUERIES, depth), jnp.bfloat16),
            pltpu.SemaphoreType.DMA((2,)),
        ]
        + gather_scratch(n, 1)
        + gather_scratch(n, parts)
        + [pltpu.SemaphoreType.REGULAR((2,))]
        + scatter_scratch(n, parts, rows, depth),
        compiler_params=pltpu.CompilerParams(
            collective_id=5, has_side_effects=True, vmem_limit_bytes=60 * 2**20
        ),
        cost_estimate=pl.CostEstimate(
            flops=8 * length * depth * width, bytes_accessed=400 * 2**20, transcendentals=0
        ),
        name="attention_forward",
    )(first_in, weights, cos_tile, sine_tile, starts, own_rows, layer_in, gains)


def attention_back_kernel(
    n, d_attn, out_weight, queries, key_rows, values, attended, log_totals, cos_ref, sine_ref,
    starts_ref, middle, out_sums, first_in, query_raw, key_raw, value_raw, layer_out, grads,
    d_attended, turned_keys, key_sum, value_sum, held, held_sems, turned_rows, staged, staged_sems,
    totals, run, sent, got
):
    me = lax.axis_index("tensor")
    length, width = queries.shape
    parts = 4
    sums = SumScatter(n, me, parts, [], [], totals, run, sent, got)

    blocks = length // QUERIES

    def fetch(block):
        source = d_attn if block < blocks else first_in
        return pltpu.make_async_copy(
            source.at[pl.ds(block % blocks * QUERIES, QUERIES), :],
            held.at[block % 2],
            held_sems.at[block % 2],
        )

    def store(which):
        return pltpu.make_async_copy(
            staged.at[which % 2], grads.at[which], staged_sems.at[which % 2]
        )

    def weight_grad(which, right):
        @pl.loop(0, turned_rows.shape[0] // 512)
        def _(block):
            at = pl.ds(pl.multiple_of(block * 512, 512), 512)
            staged[which % 2, at, :] = jnp.dot(
                turned_rows[at, :], right[...], preferred_element_type=jnp.float32
            ).astype(jnp.bfloat16)

        store(which).start()

    ready = pltpu.make_async_copy(out_sums, totals, held_sems.at[2])
    ready.start()
    fetch(0).start()
    greet(n, me)
    ready.wait()
    sums.begin()
    for block in range(2 * blocks):
        fetch(block).wait()
        if block + 1 < 2 * blocks:
            fetch(block + 1).start()
        here = slice(block % blocks * QUERIES, (block % blocks + 1) * QUERIES)
        source = held[block % 2]
        if block < blocks:
            d_attended[here, :] = jnp.dot(
                source, out_weight[0], preferred_element_type=jnp.float32
            ).astype(jnp.bfloat16)
        for k in range(source.shape[1] // TILE):
            columns = slice(k * TILE, (k + 1) * TILE)
            turned_rows[columns, here] = source[:, columns].astype(jnp.float32).T.astype(jnp.bfloat16)
        if block + 1 == blocks:
            weight_grad(3, attended)

    def back_pair(pair):
        lanes = pl.ds(pl.multiple_of(pair * PAIR, PAIR), PAIR)
        turned_keys[...] = key_rows[:, lanes].astype(jnp.float32).T.astype(jnp.bfloat16)
        key_sum[...] = jnp.zeros_like(key_sum)
        value_sum[...] = jnp.zeros_like(value_sum)
        for block in range(length // QUERIES):
            at = pl.ds(block * QUERIES, QUERIES)
            reach = (block + 1) * QUERIES
            starts = starts_ref[:, at]
            grads = d_attended[at, lanes]
            shares = (grads.astype(jnp.float32) * attended[at, lanes].astype(jnp.float32)).T
            both = []
            for head in range(2):
                heads = slice(head * HEAD_DIM, (head + 1) * HEAD_DIM)
                query = one_head(queries[at, lanes], head)
                grad = one_head(grads, head)
                share = jnp.sum(shares[heads], axis=0, keepdims=True)
                scores = masked(
                    over_lanes(key_rows[0:reach, lanes], query), starts, block * QUERIES
                )
                probs = jnp.exp(scores - log_totals[2 * pair + head, :, at])
                prob_grad = over_lanes(values[0:reach, lanes], grad)
                score_grad = (probs * (prob_grad - share)).astype(jnp.bfloat16)
                value_sum[0:reach, :] = value_sum[0:reach, :] + jnp.dot(
                    probs.astype(jnp.bfloat16), grad, preferred_element_type=jnp.float32
                )
                key_sum[0:reach, :] = key_sum[0:reach, :] + jnp.dot(
                    score_grad, query, preferred_element_type=jnp.float32
                )
                both.append(
                    jnp.dot(
                        turned_keys[heads, 0:reach], score_grad, preferred_element_type=jnp.float32
                    )
                )
            query_grad = jnp.concatenate(both, axis=0).T * HEAD_DIM ** (-0.5)
            query_raw[at, lanes] = turned(query_grad, cos_ref[at, :], -sine_ref[at, :]).astype(
                jnp.bfloat16
            )
        key_raw[:, lanes] = turned(key_sum[...], cos_ref[...], -sine_ref[...]).astype(jnp.bfloat16)
        value_raw[:, lanes] = value_sum[...].astype(jnp.bfloat16)

    pairs = width // PAIR
    pl.loop(0, pairs // 2)(back_pair)
    pl.loop(0, parts)(lambda part: sums.pass_on(part, 1))
    pl.loop(pairs // 2, pairs)(back_pair)
    for count in range(2, n - 1):
        pl.loop(0, parts)(lambda part: sums.pass_on(part, count))
    weight_grad(0, query_raw)
    store(3).wait()
    weight_grad(1, key_raw)
    store(0).wait()
    weight_grad(2, value_raw)
    pl.loop(0, parts)(sums.last)

    def body(at):
        rows = pl.ds(at, BLOCK)
        total = middle[rows, :] + totals[me, rows, :].astype(jnp.float32)
        layer_out[rows, :] = total.astype(jnp.bfloat16)

    blocks_of(middle.shape[0], body)
    store(1).wait()
    store(2).wait()
    sums.drain()


def attention_back(
    d_attn, attn_low, queries, key_rows, values, attended, log_totals, cos_tile, sine_tile, starts,
    middle, out_sums, first_in
):
    n = lax.axis_size("tensor")
    length, depth = d_attn.shape
    width, rows = queries.shape[1], middle.shape[0]
    narrow = jax.ShapeDtypeStruct((length, width), jnp.bfloat16)
    specs = whole_part(13)
    specs[0] = specs[11] = specs[12] = pl.BlockSpec(memory_space=pl.ANY)
    specs[1] = pl.BlockSpec((1, depth, width), lambda i: (3, 0, 0), pipeline_mode=pl.Buffered(1))
    scratch = scatter_scratch(n, 4, rows, depth)
    scratch[0] = pltpu.VMEM((n, rows, depth), jnp.bfloat16)
    return pl.pallas_call(
        functools.partial(attention_back_kernel, n),
        grid=(1,),
        out_shape=[
            narrow,
            narrow,
            narrow,
            jax.ShapeDtypeStruct((rows, depth), jnp.bfloat16),
            jax.ShapeDtypeStruct((4, depth, width), jnp.bfloat16),
        ],
        in_specs=specs,
        out_specs=whole_part(4) + [pl.BlockSpec(memory_space=pl.ANY)],
        scratch_shapes=[
            pltpu.VMEM((length, width), jnp.bfloat16),
            pltpu.VMEM((PAIR, length), jnp.bfloat16),
            pltpu.VMEM((length, PAIR), jnp.float32),
            pltpu.VMEM((length, PAIR), jnp.float32),
            pltpu.VMEM((2, QUERIES, depth), jnp.bfloat16),
            pltpu.SemaphoreType.DMA((3,)),
            pltpu.VMEM((depth, length), jnp.bfloat16),
            pltpu.VMEM((2, depth, width), jnp.bfloat16),
            pltpu.SemaphoreType.DMA((2,)),
        ]
        + scratch,
        compiler_params=pltpu.CompilerParams(
            collective_id=6, has_side_effects=True, vmem_limit_bytes=60 * 2**20
        ),
        cost_estimate=pl.CostEstimate(
            flops=2 * length * depth, bytes_accessed=length * depth, transcendentals=0
        ),
        name="attention_back",
    )(
        d_attn, attn_low, queries, key_rows, values, attended, log_totals, cos_tile, sine_tile,
        starts, middle, out_sums.reshape(n, rows, depth), first_in
    )


def turn_into(target, source):
    @pl.loop(0, source.shape[0] // TILE)
    def _(block):
        at = pl.ds(pl.multiple_of(block * TILE, TILE), TILE)
        for k in range(source.shape[1] // TILE):
            columns = slice(k * TILE, (k + 1) * TILE)
            target[columns, at] = source[at, columns].astype(jnp.float32).T.astype(jnp.bfloat16)


def mlp_kernel(second_in, cotangent, weights, hidden, d_gate, d_up, grads, second_turned, cot_turned):
    @pl.when(pl.program_id(0) == 0)
    def _():
        turn_into(second_turned, second_in)
        turn_into(cot_turned, cotangent)

    for block in range(second_in.shape[0] // QUERIES):
        at = slice(block * QUERIES, (block + 1) * QUERIES)
        source = second_in[at, :]
        gate_proj = jnp.dot(source, weights[0], preferred_element_type=jnp.float32)
        up_proj = jnp.dot(source, weights[1], preferred_element_type=jnp.float32)
        d_hidden = jnp.dot(cotangent[at, :], weights[2], preferred_element_type=jnp.float32)
        sigmoid_gate = jax.nn.sigmoid(gate_proj)
        silu = gate_proj * sigmoid_gate
        hidden[at, :] = (silu * up_proj).astype(jnp.bfloat16)
        slope = sigmoid_gate * (1.0 + gate_proj * (1.0 - sigmoid_gate))
        d_gate[at, :] = (d_hidden * up_proj * slope).astype(jnp.bfloat16)
        d_up[at, :] = (d_hidden * silu).astype(jnp.bfloat16)
    for which, (left, right) in enumerate(
        ((second_turned, d_gate), (second_turned, d_up), (cot_turned, hidden))
    ):

        @pl.loop(0, left.shape[0] // 512)
        def _(block):
            at = pl.ds(pl.multiple_of(block * 512, 512), 512)
            grads[which, at, :] = jnp.dot(
                left[at, :], right[...], preferred_element_type=jnp.float32
            ).astype(jnp.bfloat16)


def mlp_middle(second_in, cotangent, weights):
    length, depth = second_in.shape
    units = weights.shape[2]
    tile = 256
    wide = jax.ShapeDtypeStruct((length, units), jnp.bfloat16)
    column = pl.BlockSpec((length, tile), lambda j: (0, j))
    stacked = pl.BlockSpec((3, depth, tile), lambda j: (0, 0, j))
    return pl.pallas_call(
        mlp_kernel,
        grid=(units // tile,),
        out_shape=[wide, wide, wide, jax.ShapeDtypeStruct((3, depth, units), jnp.bfloat16)],
        in_specs=whole_part(2) + [stacked],
        out_specs=[column, column, column, stacked],
        scratch_shapes=[pltpu.VMEM((depth, length), jnp.bfloat16)] * 2,
        compiler_params=pltpu.CompilerParams(vmem_limit_bytes=60 * 2**20),
        cost_estimate=pl.CostEstimate(
            flops=12 * length * depth * units, bytes_accessed=60 * 2**20, transcendentals=0
        ),
        name="mlp_middle",
    )(second_in, cotangent, weights)


def attn_rates():
    return jnp.array([1.0, 1.0, 1.0, 8.0**0.5], jnp.float32).reshape(4, 1, 1) * (0.5 * D ** (-0.5))


def adam_update(weight, gradient, moment_one, moment_two, step_rate):
    first_new = BETA_ONE * moment_one + (1.0 - BETA_ONE) * gradient
    second_new = BETA_TWO * moment_two + (1.0 - BETA_TWO) * gradient * gradient
    fix_one = 1.0 - BETA_ONE**STEP
    fix_two = 1.0 - BETA_TWO**STEP
    weight_new = weight - step_rate * (
        first_new / fix_one / (jnp.sqrt(second_new / fix_two) + EPS_ADAM) + WEIGHT_DECAY * weight
    )
    return (first_new, second_new, weight_new)


def local(
    inputs,
    cotangent,
    doc_lengths,
    norm_gains,
    attn_weight,
    mlp_weight,
    gain_first,
    attn_first,
    mlp_first,
    gain_second,
    attn_second,
    mlp_second,
):
    row_count = inputs.shape[0]
    seq_length = row_count * lax.axis_size("tensor")
    segment, position = doc_layout(doc_lengths[0], seq_length)
    cos_tile, sine_tile = rope_tables(position)
    starts = (jnp.arange(seq_length, dtype=jnp.int32) - position)[None, :]
    width = inputs.shape[1]
    rows_f32 = jax.ShapeDtypeStruct((row_count, width), jnp.float32)
    gain_f32 = jax.ShapeDtypeStruct((8, width), jnp.float32)
    exchange = functools.partial(line_exchange, rows=row_count, width=width)
    (first_in,) = exchange(
        "first_norm", 1, [], [inputs, norm_gains], [], finish=first_norm, gathers=True, parts=4,
        turn_hop=lax.axis_size("tensor") // 2 - 1,
    )
    attn_low = lax.all_gather(attn_weight.astype(jnp.bfloat16), "dp", axis=1, tiled=True)

    (
        queries, key_rows, values, attended, log_totals, grad_out, middle, second_in
    ) = attention_forward(
        first_in, attn_low, cos_tile, sine_tile, starts, cotangent, inputs, norm_gains
    )
    mlp_low = lax.all_gather(mlp_weight.astype(jnp.bfloat16), "dp", axis=1, tiled=True)
    hidden, d_gate, d_up, mlp_sums = mlp_middle(second_in, grad_out, mlp_low)

    mlp_owned = lax.psum_scatter(mlp_sums, "dp", scatter_dimension=1, tiled=True)
    d_middle, gain_two, d_attn, out_sums = exchange(
        "mlp_back",
        3,
        [(d_gate, mlp_low, 0), (d_up, mlp_low, 1)],
        [middle, cotangent, norm_gains],
        [rows_f32, gain_f32],
        finish=second_back,
        gathers=True,
        parts=4,
        side=(hidden, mlp_low),
    )
    query_raw, key_raw, value_raw, layer_out, attn_sums = attention_back(
        d_attn, attn_low, queries, key_rows, values, attended, log_totals, cos_tile, sine_tile,
        starts, middle, out_sums, first_in
    )
    attn_owned = lax.psum_scatter(attn_sums, "dp", scatter_dimension=1, tiled=True)
    mlp_grad = mlp_owned.astype(jnp.float32)
    grad_in, gain_one = exchange(
        "input_back",
        4,
        [(query_raw, attn_low, 0), (key_raw, attn_low, 1), (value_raw, attn_low, 2)],
        [inputs, d_middle, norm_gains],
        [rows_f32, gain_f32],
        finish=first_back,
        gathers=False,
        parts=4,
    )
    gain_parts = jnp.stack([jnp.sum(gain_one, axis=0), jnp.sum(gain_two, axis=0)])
    gain_grad = sum_everywhere(gain_parts.reshape(8, -1)).reshape(norm_gains.shape)
    gain_first_new, gain_second_new, gain_new = adam_update(
        norm_gains, gain_grad, gain_first, gain_second, GAIN_RATE
    )
    mlp_first_new, mlp_second_new, mlp_new = adam_update(
        mlp_weight, mlp_grad, mlp_first, mlp_second, 0.5 * D ** (-0.5)
    )
    attn_owned, mlp_new = lax.optimization_barrier((attn_owned, mlp_new))
    attn_grad = attn_owned.astype(jnp.float32)
    attn_first_new, attn_second_new, attn_new = adam_update(
        attn_weight, attn_grad, attn_first, attn_second, attn_rates()
    )
    return (
        layer_out,
        grad_in,
        gain_grad,
        attn_grad,
        mlp_grad,
        gain_first_new,
        attn_first_new,
        mlp_first_new,
        gain_second_new,
        attn_second_new,
        mlp_second_new,
        gain_new,
        attn_new,
        mlp_new,
    )


def solution(mesh):
    placed = (
        P(("dp", "tensor"), None),
        P(("dp", "tensor"), None),
        P("dp", None),
        P(),
        P(None, "dp", "tensor"),
        P(None, "dp", "tensor"),
        P(),
        P(None, "dp", "tensor"),
        P(None, "dp", "tensor"),
        P(),
        P(None, "dp", "tensor"),
        P(None, "dp", "tensor"),
    )
    return jax.shard_map(
        local,
        mesh=mesh,
        in_specs=placed,
        out_specs=(
            P(("dp", "tensor"), None),
            P(("dp", "tensor"), None),
            P(),
            P(None, "dp", "tensor"),
            P(None, "dp", "tensor"),
            P(),
            P(None, "dp", "tensor"),
            P(None, "dp", "tensor"),
            P(),
            P(None, "dp", "tensor"),
            P(None, "dp", "tensor"),
            P(),
            P(None, "dp", "tensor"),
            P(None, "dp", "tensor"),
        ),
        check_vma=False,
    )
```

```python
import functools

import jax
import jax.numpy as jnp
from jax import lax
from jax.experimental import pallas as pl
from jax.experimental.pallas import tpu as pltpu
from jax.sharding import PartitionSpec as P

D = 2048
HEAD_DIM = 64
STEP = 10


EPS_NORM = 1e-05
ROPE_BASE = 130000.0
BETA_ONE = 0.9
BETA_TWO = 0.95
EPS_ADAM = 1e-08
WEIGHT_DECAY = 0.1
GAIN_RATE = 0.3
MASKED = -1e30


def doc_layout(lengths, seq_length):
    doc_ends = jnp.cumsum(lengths)
    starts = doc_ends - lengths
    places = jnp.arange(seq_length, dtype=jnp.int32)
    segment = jnp.sum((places[:, None] >= doc_ends[None, :]).astype(jnp.int32), axis=1)
    owners = segment[:, None] == jnp.arange(lengths.shape[0], dtype=jnp.int32)[None, :]
    position = places - jnp.sum(jnp.where(owners, starts[None, :], 0), axis=1)
    return (segment, position)


def rope_tables(position):
    half_dim = HEAD_DIM // 2
    frequencies = jnp.power(
        jnp.float32(ROPE_BASE), -2.0 * jnp.arange(half_dim, dtype=jnp.float32) / HEAD_DIM
    )
    angles = position.astype(jnp.float32)[:, None] * frequencies[None, :]
    cosine, sine = jnp.cos(angles), jnp.sin(angles)
    return (
        jnp.concatenate([cosine, cosine] * 2, axis=1),
        jnp.concatenate([-sine, sine] * 2, axis=1),
    )


MESH = pl.DeviceIdType.MESH
BLOCK = 32
TILE = 256


def whole_part(count):
    return [pl.BlockSpec(memory_space=pltpu.VMEM)] * count


def mate_of():
    place = lax.axis_index("dp")
    return place + 1 - 2 * (place % 2)


def signal_mate(semaphore):
    pl.semaphore_signal(semaphore, inc=1, device_id={"dp": mate_of()}, device_id_type=MESH)


def greet(n, me, here=None):
    barrier = pltpu.get_barrier_semaphore()
    for there, step in ((me > 0, -1), (me < n - 1, 1)):

        @pl.when(there)
        def _():
            pl.semaphore_signal(barrier, inc=1, device_id={"tensor": me + step}, device_id_type=MESH)

    count = (me > 0).astype(jnp.int32) + (me < n - 1).astype(jnp.int32)
    if here is not None:
        second_core = lax.axis_index("dp") % 2
        pl.when(second_core == 0)(lambda: signal_mate(barrier))
        count = count + second_core
    pl.semaphore_wait(barrier, count)
    if here is not None:
        pl.when(second_core == 1)(lambda: signal_mate(here))


def blocks_of(count, body):
    @pl.loop(0, count // BLOCK)
    def _(block):
        body(pl.multiple_of(block * BLOCK, BLOCK))


class RowGather:
    def __init__(self, n, me, parts, place, sent, got):
        self.n, self.me, self.parts, self.place = n, me, parts, place
        self.sent, self.got = sent, got
        self.rows = place.shape[0] // n
        self.has_left, self.has_right = me > 0, me < n - 1

    def copy(self, way, part, hop, owner):
        count = self.rows // self.parts
        first = pl.multiple_of(owner * self.rows + part * count, count)
        block = self.place.at[pl.ds(first, count), :]
        slot = part * (self.n - 1) + hop
        return pltpu.make_async_remote_copy(
            src_ref=block,
            dst_ref=block,
            send_sem=self.sent.at[way, slot],
            recv_sem=self.got.at[way, slot],
            device_id={"tensor": self.me + 1 - 2 * way},
            device_id_type=MESH,
        )

    def start(self, part):
        pl.when(self.has_right)(lambda: self.copy(0, part, 0, self.me).start())
        pl.when(self.has_left)(lambda: self.copy(1, part, 0, self.me).start())

    def step(self, part, hop):
        last = hop + 1 == self.n - 1

        @pl.when(hop < self.me)
        def _():
            owner = self.me - 1 - hop
            self.copy(0, part, hop, owner).wait_recv()
            if not last:
                pl.when(self.has_right)(lambda: self.copy(0, part, hop + 1, owner).start())

        @pl.when(hop < self.n - 1 - self.me)
        def _():
            owner = self.me + 1 + hop
            self.copy(1, part, hop, owner).wait_recv()
            if not last:
                pl.when(self.has_left)(lambda: self.copy(1, part, hop + 1, owner).start())

    def drain(self):
        @pl.loop(0, self.parts)
        def _(part):
            for hop in range(self.n - 1):
                pl.when(self.has_right & (hop <= self.me))(
                    lambda: self.copy(0, part, hop, self.me - hop).wait_send()
                )
                pl.when(self.has_left & (hop <= self.n - 1 - self.me))(
                    lambda: self.copy(1, part, hop, self.me + hop).wait_send()
                )


class SumScatter:
    def __init__(self, n, me, parts, lefts, rights, totals, run, sent, got):
        self.n, self.me, self.parts = n, me, parts
        self.lefts, self.rights, self.totals, self.run = lefts, rights, totals, run
        self.sent, self.got = sent, got
        self.rows = totals.shape[1]
        self.fed = (me > 0, me < n - 1)

    def copy(self, way, part, hop):
        slot = part * (self.n - 1) + hop
        run = self.run.at[self.place(way, part, hop)]
        return pltpu.make_async_remote_copy(
            src_ref=run,
            dst_ref=run,
            send_sem=self.sent.at[way, slot],
            recv_sem=self.got.at[way, slot],
            device_id={"tensor": self.me + 1 - 2 * way},
            device_id_type=MESH,
        )

    def product(self, dest):
        first = pl.multiple_of(dest * self.rows, self.rows)

        @pl.loop(0, self.totals.shape[2] // TILE)
        def _(tile):
            columns = pl.ds(pl.multiple_of(tile * TILE, TILE), TILE)
            value = None
            for left, right in zip(self.lefts, self.rights):
                term = lax.dot_general(
                    left[pl.ds(first, self.rows), :],
                    right[columns, :],
                    (((1,), (1,)), ((), ())),
                    preferred_element_type=jnp.float32,
                )
                value = term if value is None else value + term
            self.totals[dest, :, columns] = value.astype(self.totals.dtype)

    def place(self, way, part, hop):
        return part * (self.n + 1) + (hop, self.n - hop)[way]

    def begin(self):
        part_rows = self.rows // self.parts
        for hop in range(self.n - 1):
            for way, dest in ((0, self.n - 1 - hop), (1, hop)):
                needed = (dest > self.me, dest < self.me)[way]

                @pl.when(needed & jnp.logical_not(self.fed[way]))
                def _():
                    if self.lefts:
                        self.product(dest)

                    @pl.loop(0, self.parts)
                    def _(part):
                        slot = self.place(way, part, hop)

                        def body(at):
                            first = pl.multiple_of(part * part_rows + at, BLOCK)
                            own = self.totals[dest, pl.ds(first, BLOCK), :]
                            self.run[slot, pl.ds(at, BLOCK), :] = own.astype(jnp.bfloat16)

                        blocks_of(part_rows, body)
                        self.copy(way, part, hop).start()

    def prepare(self, count):
        if count == self.n - 1:
            self.product(self.me)
        else:
            for way, hop, dest, there in self.arrivals(count):
                pl.when(there)(lambda: self.product(dest))

    def arrivals(self, count):
        for way, behind in ((0, self.me), (1, self.n - 1 - self.me)):
            hop = count - behind
            yield way, hop, (self.n - 1 - hop, hop)[way], self.fed[way] & (hop >= 0)

    def pass_on(self, part, count):
        for way, hop, dest, there in self.arrivals(count):
            run, slot = self.run, self.place(way, part, hop)
            first = part * (self.rows // self.parts)

            @pl.when(there)
            def _():
                self.copy(way, part, hop).wait_recv()

                def body(at):
                    here = pl.ds(pl.multiple_of(first + at, BLOCK), BLOCK)
                    own = self.totals[dest, here, :].astype(jnp.float32)
                    came = run[slot, pl.ds(at, BLOCK), :].astype(jnp.float32)
                    run[slot, pl.ds(at, BLOCK), :] = (own + came).astype(jnp.bfloat16)

                blocks_of(self.rows // self.parts, body)
                self.copy(way, part, hop).start()

    def last(self, part):
        first = part * (self.rows // self.parts)
        for way, hop, dest, there in self.arrivals(self.n - 1):
            run, slot = self.run, self.place(way, part, hop)

            @pl.when(there)
            def _():
                self.copy(way, part, hop).wait_recv()

                def body(at):
                    own = pl.ds(pl.multiple_of(first + at, BLOCK), BLOCK)
                    came = run[slot, pl.ds(at, BLOCK), :].astype(jnp.float32)
                    total = self.totals[self.me, own, :].astype(jnp.float32) + came
                    self.totals[self.me, own, :] = total.astype(self.totals.dtype)

                blocks_of(self.rows // self.parts, body)

    def drain(self):
        @pl.loop(0, self.parts)
        def _(part):
            for hop in range(self.n - 1):
                pl.when(self.n - 1 - hop > self.me)(lambda: self.copy(0, part, hop).wait_send())
                pl.when(hop < self.me)(lambda: self.copy(1, part, hop).wait_send())


def scatter_scratch(n, parts, rows, width):
    slots = parts * (n - 1)
    kept = jnp.float32 if n * rows * width <= 2**21 else jnp.bfloat16
    return [
        pltpu.VMEM((n, rows, width), kept),
        pltpu.VMEM((parts * (n + 1), rows // parts, width), jnp.bfloat16),
        pltpu.SemaphoreType.DMA((2, slots)),
        pltpu.SemaphoreType.DMA((2, slots)),
    ]


def gather_scratch(n, parts):
    return [pltpu.SemaphoreType.DMA((2, parts * (n - 1)))] * 2


class SideProduct:
    def __init__(self, source, columns, target, held, weight, staged, sems):
        self.source, self.columns, self.target = source, columns, target
        self.held, self.weight, self.staged, self.sems = held, weight, staged, sems
        self.count = source.shape[0] // QUERIES
        self.done = 0

    def fetch(self, block):
        return pltpu.make_async_copy(
            self.source.at[pl.ds(block * QUERIES, QUERIES), :],
            self.held.at[block % 2],
            self.sems.at[block % 2],
        )

    def store(self, block):
        return pltpu.make_async_copy(
            self.staged.at[block % 2],
            self.target.at[pl.ds(block * QUERIES, QUERIES), :],
            self.sems.at[2 + block % 2],
        )

    def fetch_weight(self):
        return pltpu.make_async_copy(self.columns.at[2], self.weight, self.sems.at[4])

    def open(self, lefts):
        self.fetch_weight().start()
        self.fetch(0).start()

    def step(self):
        block = self.done
        if block == self.count:
            return
        if block == 0:
            self.fetch_weight().wait()
        self.fetch(block).wait()
        if block + 1 < self.count:
            self.fetch(block + 1).start()
        if block >= 2:
            self.store(block - 2).wait()

        @pl.loop(0, self.weight.shape[0] // TILE)
        def _(tile):
            columns = pl.ds(pl.multiple_of(tile * TILE, TILE), TILE)
            self.staged[block % 2, :, columns] = over_lanes(
                self.held[block % 2], self.weight[columns, :]
            ).astype(jnp.bfloat16)

        self.store(block).start()
        self.done = block + 1

    def close(self):
        while self.done < self.count:
            self.step()
        for block in range(max(0, self.count - 2), self.count):
            self.store(block).wait()


def side_scratch(depth, units):
    return [
        pltpu.VMEM((2, QUERIES, units), jnp.bfloat16),
        pltpu.VMEM((depth, units), jnp.bfloat16),
        pltpu.VMEM((2, QUERIES, depth), jnp.bfloat16),
        pltpu.SemaphoreType.DMA((5,)),
    ]


def line_kernel(n, parts, products, extras, outs, gathers, side, turn_hop, finish, *refs):
    refs = list(refs)
    take = lambda count: [refs.pop(0) for _ in range(count)]
    lefts, rights, more = take(products), take(products), take(extras)
    side_in = take(2) if side else None
    results = take(outs)
    gathered = take(1)[0] if gathers else None
    filler = SideProduct(*side_in, *take(1), *[refs.pop() for _ in range(4)][::-1]) if side else None
    me = lax.axis_index("tensor")
    if products:
        totals = refs[0]
        sums = SumScatter(n, me, parts, lefts, rights, *take(4))
    if gathers:
        gather = RowGather(n, me, parts, gathered, *take(2))
    rows = totals.shape[1] if products else gathered.shape[0] // n
    part_rows = rows // parts

    def finish_part(part):
        def body(block):
            at = pl.multiple_of(part * part_rows + block, BLOCK)
            total = totals[me, pl.ds(at, BLOCK), :].astype(jnp.float32) if products else None
            sent_rows = finish(at, total, more, results)
            if gathers:
                gathered[pl.ds(pl.multiple_of(me * rows + at, BLOCK), BLOCK), :] = sent_rows

        blocks_of(part_rows, body)

    second_core = lax.axis_index("dp") % 2 == 1
    if turn_hop is None:
        greet(n, me)
    else:
        turns = take(1)[0]
        greet(n, me, turns.at[1])
    for result in results:
        if result.shape[0] == 8:
            result[...] = jnp.zeros_like(result)
    if products:
        sums.begin()
    if filler:
        filler.open(lefts)
    def complete(part):
        if products:
            sums.last(part)
        finish_part(part)
        if gathers:
            gather.start(part)

    if products:
        for count in range(1, n - 1):
            sums.prepare(count)
            pl.loop(0, parts)(lambda part: sums.pass_on(part, count))
        sums.prepare(n - 1)
        if filler:
            filler.step()
    if turn_hop is not None:
        pl.when(second_core)(lambda: pl.semaphore_wait(turns.at[0], 1))
    pl.loop(0, parts)(complete)
    if gathers:
        for hop in range(n - 1):
            if filler:
                filler.step()
            pl.loop(0, parts)(lambda part: gather.step(part, hop))
            if hop == turn_hop:

                @pl.when(jnp.logical_not(second_core))
                def _():
                    pl.semaphore_wait(turns.at[1], 1)
                    signal_mate(turns.at[0])

        gather.drain()
    if filler:
        filler.close()
    if products:
        sums.drain()


def line_exchange(
    name, collective_id, pairs, extras, outs, rows, width, finish, gathers, parts, side=(), turn_hop=None
):
    n = lax.axis_size("tensor")
    scratch = scatter_scratch(n, parts, rows, width) if pairs else []
    if gathers:
        scratch = scratch + gather_scratch(n, parts)
        outs = outs + [jax.ShapeDtypeStruct((n * rows, width), jnp.bfloat16)]
    operands = [pair[0] for pair in pairs] + [pair[1] for pair in pairs] + list(extras)
    specs = whole_part(len(operands)) + [pl.BlockSpec(memory_space=pl.ANY)] * len(side)
    own_outs = len(outs) - gathers
    out_specs = whole_part(len(outs))
    operands = operands + list(side)
    if side:
        outs = outs + [jax.ShapeDtypeStruct((side[0].shape[0], width), jnp.bfloat16)]
        out_specs = out_specs + [pl.BlockSpec(memory_space=pl.ANY)]
        scratch = scratch + side_scratch(width, side[0].shape[1])
    if turn_hop is not None:
        scratch = scratch + [pltpu.SemaphoreType.REGULAR((2,))]
    for k, (left, right, which) in enumerate(pairs):
        specs[len(pairs) + k] = pl.BlockSpec(
            (None, *right.shape[1:]), lambda i, which=which: (which, 0, 0), pipeline_mode=pl.Buffered(1)
        )
    return pl.pallas_call(
        functools.partial(
            line_kernel, n, parts, len(pairs), len(extras), own_outs, gathers, len(side) > 0, turn_hop, finish
        ),
        grid=(1,),
        out_shape=outs,
        in_specs=specs,
        out_specs=out_specs,
        scratch_shapes=scratch,
        compiler_params=pltpu.CompilerParams(
            collective_id=collective_id, has_side_effects=True, vmem_limit_bytes=60 * 2**20
        ),
        cost_estimate=pl.CostEstimate(
            flops=2 * n * rows * width, bytes_accessed=rows * width, transcendentals=0
        ),
        name=name,
    )(*operands)


def everywhere_kernel(sizes, field, result, came, sent, got):
    places = [lax.axis_index(name) for name in sizes]
    partners = []
    for name, place in zip(sizes, places):
        stride = 1
        while stride < sizes[name]:
            other = place + stride - 2 * stride * (place // stride % 2)
            partners.append({name: other})
            stride = 2 * stride
    barrier = pltpu.get_barrier_semaphore()
    for partner in partners:
        pl.semaphore_signal(barrier, inc=1, device_id=partner, device_id_type=MESH)
    pl.semaphore_wait(barrier, len(partners))
    result[...] = field[...]
    for k, partner in enumerate(partners):
        came[2 * k] = result[...]
        copy = pltpu.make_async_remote_copy(
            src_ref=came.at[2 * k],
            dst_ref=came.at[2 * k + 1],
            send_sem=sent.at[k],
            recv_sem=got.at[k],
            device_id=partner,
            device_id_type=MESH,
        )
        copy.start()
        copy.wait()
        result[...] = result[...] + came[2 * k + 1]


def sum_everywhere(field):
    sizes = {name: lax.axis_size(name) for name in ("dp", "tensor")}
    steps = sum(size.bit_length() - 1 for size in sizes.values())
    return pl.pallas_call(
        functools.partial(everywhere_kernel, sizes),
        out_shape=jax.ShapeDtypeStruct(field.shape, jnp.float32),
        in_specs=whole_part(1),
        out_specs=pl.BlockSpec(memory_space=pltpu.VMEM),
        scratch_shapes=[
            pltpu.VMEM((2 * steps, *field.shape), jnp.float32),
            pltpu.SemaphoreType.DMA((steps,)),
            pltpu.SemaphoreType.DMA((steps,)),
        ],
        compiler_params=pltpu.CompilerParams(collective_id=7, has_side_effects=True),
        name="gain_sum",
    )(field)


def inverse_scale(field):
    return lax.rsqrt(jnp.mean(field * field, axis=-1, keepdims=True) + EPS_NORM)


def first_norm(at, total, more, results):
    layer_in, gains = more
    field = layer_in[pl.ds(at, BLOCK), :].astype(jnp.float32)
    return (field * inverse_scale(field) * gains[0:1, :]).astype(jnp.bfloat16)


def norm_back(field, gradient, gain_row, gain_out):
    inv_scale = inverse_scale(field)
    normed = field * inv_scale
    scaled = gradient * gain_row
    back = inv_scale * (scaled - normed * jnp.mean(scaled * normed, axis=-1, keepdims=True))
    product = gradient * normed
    folded = product[0:8]
    for k in range(8, BLOCK, 8):
        folded = folded + product[k : k + 8]
    gain_out[...] = gain_out[...] + folded
    return back


def second_back(at, total, more, results):
    middle, cotangent, gains = more
    rows = pl.ds(at, BLOCK)
    back = norm_back(middle[rows, :], total, gains[1:2, :], results[1])
    back = back + cotangent[rows, :].astype(jnp.float32)
    results[0][rows, :] = back
    return back.astype(jnp.bfloat16)


def first_back(at, total, more, results):
    layer_in, d_middle, gains = more
    rows = pl.ds(at, BLOCK)
    back = norm_back(layer_in[rows, :].astype(jnp.float32), total, gains[0:1, :], results[1])
    results[0][rows, :] = back + d_middle[rows, :]


PAIR = 2 * HEAD_DIM
QUERIES = 256


def turned(field, cos_tile, sine_tile):
    lanes = lax.broadcasted_iota(jnp.int32, field.shape, 1)
    ahead = pltpu.roll(field, PAIR - HEAD_DIM // 2, 1)
    behind = pltpu.roll(field, HEAD_DIM // 2, 1)
    partner = jnp.where(lanes % HEAD_DIM < HEAD_DIM // 2, ahead, behind)
    return field * cos_tile + partner * sine_tile


def one_head(tile, head):
    lanes = lax.broadcasted_iota(jnp.int32, tile.shape, 1)
    return jnp.where(lanes // HEAD_DIM == head, tile, jnp.zeros_like(tile))


def over_lanes(left, right):
    return lax.dot_general(
        left, right, (((1,), (1,)), ((), ())), preferred_element_type=jnp.float32
    )


def masked(scores, starts, first_query):
    keys = lax.broadcasted_iota(jnp.int32, scores.shape, 0)
    queries = first_query + lax.broadcasted_iota(jnp.int32, scores.shape, 1)
    return jnp.where((keys >= starts) & (keys <= queries), scores, MASKED)


def attention_forward_kernel(
    n, parts, first_in, weights, cos_ref, sine_ref, starts_ref, own_rows, layer_in, gains,
    queries, key_rows, values, attended, log_totals, cot_rows, middle, second_in,
    turned_values, held, held_sems, cot_sent, cot_got, rows_sent, rows_got, turns, totals, run,
    sums_sent, sums_got
):
    me = lax.axis_index("tensor")
    second_core = lax.axis_index("dp") % 2 == 1
    rows = own_rows.shape[0]
    part_rows = rows // parts
    length, width = queries.shape

    def fetch(block):
        return pltpu.make_async_copy(
            first_in.at[pl.ds(block * QUERIES, QUERIES), :], held.at[block % 2], held_sems.at[block % 2]
        )

    fetch(0).start()
    greet(n, me)
    cot_gather = RowGather(n, me, 1, cot_rows, cot_sent, cot_got)
    gather = RowGather(n, me, parts, second_in, rows_sent, rows_got)
    sums = SumScatter(
        n, me, parts, [attended], [weights.at[3]], totals, run, sums_sent, sums_got
    )

    def place_own(at):
        place = pl.ds(pl.multiple_of(me * rows + at, BLOCK), BLOCK)
        cot_rows[place, :] = own_rows[pl.ds(at, BLOCK), :]

    blocks_of(rows, place_own)
    cot_gather.start(0)

    for block in range(length // QUERIES):
        fetch(block).wait()
        if (block + 1) * QUERIES < length:
            fetch(block + 1).start()
        at = pl.ds(block * QUERIES, QUERIES)
        source = held[block % 2]
        cos_tile, sine_tile = cos_ref[at, :], sine_ref[at, :]
        for which, target in enumerate((queries, key_rows, values)):
            field = jnp.dot(source, weights[which], preferred_element_type=jnp.float32)
            for pair in range(width // PAIR):
                tile = field[:, pair * PAIR : (pair + 1) * PAIR]
                if which < 2:
                    tile = turned(tile, cos_tile, sine_tile)
                if which == 0:
                    tile = tile.astype(jnp.bfloat16) * HEAD_DIM ** (-0.5)
                target[at, pair * PAIR : (pair + 1) * PAIR] = tile.astype(jnp.bfloat16)

    def attend(pair):
        lanes = pl.ds(pl.multiple_of(pair * PAIR, PAIR), PAIR)
        turned_values[...] = values[:, lanes].astype(jnp.float32).T.astype(jnp.bfloat16)
        for block in range(length // QUERIES):
            at = pl.ds(block * QUERIES, QUERIES)
            reach = (block + 1) * QUERIES
            starts = starts_ref[:, at]
            both = []
            for head in range(2):
                query = one_head(queries[at, lanes], head)
                scores = masked(
                    over_lanes(key_rows[0:reach, lanes], query), starts, block * QUERIES
                )
                peak = jnp.max(scores, axis=0, keepdims=True)
                raised = jnp.exp(scores - peak)
                total = jnp.sum(raised, axis=0, keepdims=True)
                result = jnp.dot(
                    turned_values[head * HEAD_DIM : (head + 1) * HEAD_DIM, 0:reach],
                    raised.astype(jnp.bfloat16),
                    preferred_element_type=jnp.float32,
                )
                both.append(result / total)
                log_totals[2 * pair + head, :, at] = peak + jnp.log(total)
            attended[at, lanes] = jnp.concatenate(both, axis=0).T.astype(jnp.bfloat16)

    pairs = width // PAIR
    pl.loop(0, pairs - 1)(attend)
    cot_gather.step(0, 0)
    pl.loop(pairs - 1, pairs)(attend)

    @pl.when(second_core)
    def _():
        for hop in range(1, n - 1):
            cot_gather.step(0, hop)

    sums.begin()

    def finish_part(part):
        def body(block):
            at = pl.multiple_of(part * part_rows + block, BLOCK)
            here = pl.ds(at, BLOCK)
            total = totals[me, here, :].astype(jnp.float32)
            field = layer_in[here, :].astype(jnp.float32) + total
            middle[here, :] = field
            place = pl.ds(pl.multiple_of(me * rows + at, BLOCK), BLOCK)
            second_in[place, :] = (field * inverse_scale(field) * gains[1:2, :]).astype(jnp.bfloat16)

        blocks_of(part_rows, body)

    def complete(part):
        sums.last(part)
        finish_part(part)
        gather.start(part)

    for count in range(1, n - 1):
        sums.prepare(count)
        pl.loop(0, parts)(lambda part: sums.pass_on(part, count))
        if count < n - 2:
            pl.when(jnp.logical_not(second_core))(lambda: cot_gather.step(0, count))
    sums.prepare(n - 1)
    pl.loop(0, parts)(complete)

    pl.when(jnp.logical_not(second_core))(lambda: cot_gather.step(0, n - 2))

    for hop in range(n - 1):
        pl.loop(0, parts)(lambda part: gather.step(part, hop))
    cot_gather.drain()
    gather.drain()
    sums.drain()


def attention_forward(first_in, weights, cos_tile, sine_tile, starts, own_rows, layer_in, gains):
    n = lax.axis_size("tensor")
    parts = 4
    length, depth = first_in.shape
    rows, width = own_rows.shape[0], weights.shape[2]
    narrow = jax.ShapeDtypeStruct((length, width), jnp.bfloat16)
    wide = jax.ShapeDtypeStruct((length, depth), jnp.bfloat16)
    outs = [
        narrow,
        narrow,
        narrow,
        narrow,
        jax.ShapeDtypeStruct((width // HEAD_DIM, 1, length), jnp.float32),
        wide,
        jax.ShapeDtypeStruct((rows, depth), jnp.float32),
        wide,
    ]
    specs = whole_part(8)
    specs[0] = pl.BlockSpec(memory_space=pl.ANY)
    return pl.pallas_call(
        functools.partial(attention_forward_kernel, n, parts),
        out_shape=outs,
        in_specs=specs,
        out_specs=whole_part(len(outs)),
        scratch_shapes=[
            pltpu.VMEM((PAIR, length), jnp.bfloat16),
            pltpu.VMEM((2, QUERIES, depth), jnp.bfloat16),
            pltpu.SemaphoreType.DMA((2,)),
        ]
        + gather_scratch(n, 1)
        + gather_scratch(n, parts)
        + [pltpu.SemaphoreType.REGULAR((2,))]
        + scatter_scratch(n, parts, rows, depth),
        compiler_params=pltpu.CompilerParams(
            collective_id=5, has_side_effects=True, vmem_limit_bytes=60 * 2**20
        ),
        cost_estimate=pl.CostEstimate(
            flops=8 * length * depth * width, bytes_accessed=400 * 2**20, transcendentals=0
        ),
        name="attention_forward",
    )(first_in, weights, cos_tile, sine_tile, starts, own_rows, layer_in, gains)


def attention_back_kernel(
    n, d_attn, out_weight, queries, key_rows, values, attended, log_totals, cos_ref, sine_ref,
    starts_ref, middle, out_sums, first_in, query_raw, key_raw, value_raw, layer_out, grads,
    d_attended, turned_keys, key_sum, value_sum, held, held_sems, turned_rows, staged, staged_sems,
    totals, run, sent, got
):
    me = lax.axis_index("tensor")
    length, width = queries.shape
    parts = 4
    sums = SumScatter(n, me, parts, [], [], totals, run, sent, got)

    blocks = length // QUERIES

    def fetch(block):
        source = d_attn if block < blocks else first_in
        return pltpu.make_async_copy(
            source.at[pl.ds(block % blocks * QUERIES, QUERIES), :],
            held.at[block % 2],
            held_sems.at[block % 2],
        )

    def store(which):
        return pltpu.make_async_copy(
            staged.at[which % 2], grads.at[which], staged_sems.at[which % 2]
        )

    def weight_grad(which, right):
        @pl.loop(0, turned_rows.shape[0] // 512)
        def _(block):
            at = pl.ds(pl.multiple_of(block * 512, 512), 512)
            staged[which % 2, at, :] = jnp.dot(
                turned_rows[at, :], right[...], preferred_element_type=jnp.float32
            ).astype(jnp.bfloat16)

        store(which).start()

    ready = pltpu.make_async_copy(out_sums, totals, held_sems.at[2])
    ready.start()
    fetch(0).start()
    greet(n, me)
    ready.wait()
    sums.begin()
    for block in range(2 * blocks):
        fetch(block).wait()
        if block + 1 < 2 * blocks:
            fetch(block + 1).start()
        here = slice(block % blocks * QUERIES, (block % blocks + 1) * QUERIES)
        source = held[block % 2]
        if block < blocks:
            d_attended[here, :] = jnp.dot(
                source, out_weight[0], preferred_element_type=jnp.float32
            ).astype(jnp.bfloat16)
        for k in range(source.shape[1] // TILE):
            columns = slice(k * TILE, (k + 1) * TILE)
            turned_rows[columns, here] = source[:, columns].astype(jnp.float32).T.astype(jnp.bfloat16)
        if block + 1 == blocks:
            weight_grad(3, attended)

    def back_pair(pair):
        lanes = pl.ds(pl.multiple_of(pair * PAIR, PAIR), PAIR)
        turned_keys[...] = key_rows[:, lanes].astype(jnp.float32).T.astype(jnp.bfloat16)
        key_sum[...] = jnp.zeros_like(key_sum)
        value_sum[...] = jnp.zeros_like(value_sum)
        for block in range(length // QUERIES):
            at = pl.ds(block * QUERIES, QUERIES)
            reach = (block + 1) * QUERIES
            starts = starts_ref[:, at]
            grads = d_attended[at, lanes]
            shares = (grads.astype(jnp.float32) * attended[at, lanes].astype(jnp.float32)).T
            both = []
            for head in range(2):
                heads = slice(head * HEAD_DIM, (head + 1) * HEAD_DIM)
                query = one_head(queries[at, lanes], head)
                grad = one_head(grads, head)
                share = jnp.sum(shares[heads], axis=0, keepdims=True)
                scores = masked(
                    over_lanes(key_rows[0:reach, lanes], query), starts, block * QUERIES
                )
                probs = jnp.exp(scores - log_totals[2 * pair + head, :, at])
                prob_grad = over_lanes(values[0:reach, lanes], grad)
                score_grad = (probs * (prob_grad - share)).astype(jnp.bfloat16)
                value_sum[0:reach, :] = value_sum[0:reach, :] + jnp.dot(
                    probs.astype(jnp.bfloat16), grad, preferred_element_type=jnp.float32
                )
                key_sum[0:reach, :] = key_sum[0:reach, :] + jnp.dot(
                    score_grad, query, preferred_element_type=jnp.float32
                )
                both.append(
                    jnp.dot(
                        turned_keys[heads, 0:reach], score_grad, preferred_element_type=jnp.float32
                    )
                )
            query_grad = jnp.concatenate(both, axis=0).T * HEAD_DIM ** (-0.5)
            query_raw[at, lanes] = turned(query_grad, cos_ref[at, :], -sine_ref[at, :]).astype(
                jnp.bfloat16
            )
        key_raw[:, lanes] = turned(key_sum[...], cos_ref[...], -sine_ref[...]).astype(jnp.bfloat16)
        value_raw[:, lanes] = value_sum[...].astype(jnp.bfloat16)

    pairs = width // PAIR
    pl.loop(0, pairs // 2)(back_pair)
    pl.loop(0, parts)(lambda part: sums.pass_on(part, 1))
    pl.loop(pairs // 2, pairs)(back_pair)
    for count in range(2, n - 1):
        pl.loop(0, parts)(lambda part: sums.pass_on(part, count))
    weight_grad(0, query_raw)
    store(3).wait()
    weight_grad(1, key_raw)
    store(0).wait()
    weight_grad(2, value_raw)
    pl.loop(0, parts)(sums.last)

    def body(at):
        rows = pl.ds(at, BLOCK)
        total = middle[rows, :] + totals[me, rows, :].astype(jnp.float32)
        layer_out[rows, :] = total.astype(jnp.bfloat16)

    blocks_of(middle.shape[0], body)
    store(1).wait()
    store(2).wait()
    sums.drain()


def attention_back(
    d_attn, attn_low, queries, key_rows, values, attended, log_totals, cos_tile, sine_tile, starts,
    middle, out_sums, first_in
):
    n = lax.axis_size("tensor")
    length, depth = d_attn.shape
    width, rows = queries.shape[1], middle.shape[0]
    narrow = jax.ShapeDtypeStruct((length, width), jnp.bfloat16)
    specs = whole_part(13)
    specs[0] = specs[11] = specs[12] = pl.BlockSpec(memory_space=pl.ANY)
    specs[1] = pl.BlockSpec((1, depth, width), lambda i: (3, 0, 0), pipeline_mode=pl.Buffered(1))
    scratch = scatter_scratch(n, 4, rows, depth)
    scratch[0] = pltpu.VMEM((n, rows, depth), jnp.bfloat16)
    return pl.pallas_call(
        functools.partial(attention_back_kernel, n),
        grid=(1,),
        out_shape=[
            narrow,
            narrow,
            narrow,
            jax.ShapeDtypeStruct((rows, depth), jnp.bfloat16),
            jax.ShapeDtypeStruct((4, depth, width), jnp.bfloat16),
        ],
        in_specs=specs,
        out_specs=whole_part(4) + [pl.BlockSpec(memory_space=pl.ANY)],
        scratch_shapes=[
            pltpu.VMEM((length, width), jnp.bfloat16),
            pltpu.VMEM((PAIR, length), jnp.bfloat16),
            pltpu.VMEM((length, PAIR), jnp.float32),
            pltpu.VMEM((length, PAIR), jnp.float32),
            pltpu.VMEM((2, QUERIES, depth), jnp.bfloat16),
            pltpu.SemaphoreType.DMA((3,)),
            pltpu.VMEM((depth, length), jnp.bfloat16),
            pltpu.VMEM((2, depth, width), jnp.bfloat16),
            pltpu.SemaphoreType.DMA((2,)),
        ]
        + scratch,
        compiler_params=pltpu.CompilerParams(
            collective_id=6, has_side_effects=True, vmem_limit_bytes=60 * 2**20
        ),
        cost_estimate=pl.CostEstimate(
            flops=2 * length * depth, bytes_accessed=length * depth, transcendentals=0
        ),
        name="attention_back",
    )(
        d_attn, attn_low, queries, key_rows, values, attended, log_totals, cos_tile, sine_tile,
        starts, middle, out_sums.reshape(n, rows, depth), first_in
    )


def turn_into(target, source):
    @pl.loop(0, source.shape[0] // TILE)
    def _(block):
        at = pl.ds(pl.multiple_of(block * TILE, TILE), TILE)
        for k in range(source.shape[1] // TILE):
            columns = slice(k * TILE, (k + 1) * TILE)
            target[columns, at] = source[at, columns].astype(jnp.float32).T.astype(jnp.bfloat16)


def mlp_kernel(second_in, cotangent, weights, hidden, d_gate, d_up, grads, second_turned, cot_turned):
    @pl.when(pl.program_id(0) == 0)
    def _():
        turn_into(second_turned, second_in)
        turn_into(cot_turned, cotangent)

    for block in range(second_in.shape[0] // QUERIES):
        at = slice(block * QUERIES, (block + 1) * QUERIES)
        source = second_in[at, :]
        gate_proj = jnp.dot(source, weights[0], preferred_element_type=jnp.float32)
        up_proj = jnp.dot(source, weights[1], preferred_element_type=jnp.float32)
        d_hidden = jnp.dot(cotangent[at, :], weights[2], preferred_element_type=jnp.float32)
        sigmoid_gate = jax.nn.sigmoid(gate_proj)
        silu = gate_proj * sigmoid_gate
        hidden[at, :] = (silu * up_proj).astype(jnp.bfloat16)
        slope = sigmoid_gate * (1.0 + gate_proj * (1.0 - sigmoid_gate))
        d_gate[at, :] = (d_hidden * up_proj * slope).astype(jnp.bfloat16)
        d_up[at, :] = (d_hidden * silu).astype(jnp.bfloat16)
    for which, (left, right) in enumerate(
        ((second_turned, d_gate), (second_turned, d_up), (cot_turned, hidden))
    ):

        @pl.loop(0, left.shape[0] // 512)
        def _(block):
            at = pl.ds(pl.multiple_of(block * 512, 512), 512)
            grads[which, at, :] = jnp.dot(
                left[at, :], right[...], preferred_element_type=jnp.float32
            ).astype(jnp.bfloat16)


def mlp_middle(second_in, cotangent, weights):
    length, depth = second_in.shape
    units = weights.shape[2]
    tile = 256
    wide = jax.ShapeDtypeStruct((length, units), jnp.bfloat16)
    column = pl.BlockSpec((length, tile), lambda j: (0, j))
    stacked = pl.BlockSpec((3, depth, tile), lambda j: (0, 0, j))
    return pl.pallas_call(
        mlp_kernel,
        grid=(units // tile,),
        out_shape=[wide, wide, wide, jax.ShapeDtypeStruct((3, depth, units), jnp.bfloat16)],
        in_specs=whole_part(2) + [stacked],
        out_specs=[column, column, column, stacked],
        scratch_shapes=[pltpu.VMEM((depth, length), jnp.bfloat16)] * 2,
        compiler_params=pltpu.CompilerParams(vmem_limit_bytes=60 * 2**20),
        cost_estimate=pl.CostEstimate(
            flops=12 * length * depth * units, bytes_accessed=60 * 2**20, transcendentals=0
        ),
        name="mlp_middle",
    )(second_in, cotangent, weights)


def attn_rates():
    return jnp.array([1.0, 1.0, 1.0, 8.0**0.5], jnp.float32).reshape(4, 1, 1) * (0.5 * D ** (-0.5))


def adam_update(weight, gradient, moment_one, moment_two, step_rate):
    first_new = BETA_ONE * moment_one + (1.0 - BETA_ONE) * gradient
    second_new = BETA_TWO * moment_two + (1.0 - BETA_TWO) * gradient * gradient
    fix_one = 1.0 - BETA_ONE**STEP
    fix_two = 1.0 - BETA_TWO**STEP
    weight_new = weight - step_rate * (
        first_new / fix_one / (jnp.sqrt(second_new / fix_two) + EPS_ADAM) + WEIGHT_DECAY * weight
    )
    return (first_new, second_new, weight_new)


def local(
    inputs,
    cotangent,
    doc_lengths,
    norm_gains,
    attn_weight,
    mlp_weight,
    gain_first,
    attn_first,
    mlp_first,
    gain_second,
    attn_second,
    mlp_second,
):
    row_count = inputs.shape[0]
    seq_length = row_count * lax.axis_size("tensor")
    segment, position = doc_layout(doc_lengths[0], seq_length)
    cos_tile, sine_tile = rope_tables(position)
    starts = (jnp.arange(seq_length, dtype=jnp.int32) - position)[None, :]
    width = inputs.shape[1]
    rows_f32 = jax.ShapeDtypeStruct((row_count, width), jnp.float32)
    gain_f32 = jax.ShapeDtypeStruct((8, width), jnp.float32)
    exchange = functools.partial(line_exchange, rows=row_count, width=width)
    (first_in,) = exchange(
        "first_norm", 1, [], [inputs, norm_gains], [], finish=first_norm, gathers=True, parts=4,
        turn_hop=lax.axis_size("tensor") // 2 - 1,
    )
    attn_low = lax.all_gather(attn_weight.astype(jnp.bfloat16), "dp", axis=1, tiled=True)

    (
        queries, key_rows, values, attended, log_totals, grad_out, middle, second_in
    ) = attention_forward(
        first_in, attn_low, cos_tile, sine_tile, starts, cotangent, inputs, norm_gains
    )
    mlp_low = lax.all_gather(mlp_weight.astype(jnp.bfloat16), "dp", axis=1, tiled=True)
    hidden, d_gate, d_up, mlp_sums = mlp_middle(second_in, grad_out, mlp_low)

    mlp_owned = lax.psum_scatter(mlp_sums, "dp", scatter_dimension=1, tiled=True)
    d_middle, gain_two, d_attn, out_sums = exchange(
        "mlp_back",
        3,
        [(d_gate, mlp_low, 0), (d_up, mlp_low, 1)],
        [middle, cotangent, norm_gains],
        [rows_f32, gain_f32],
        finish=second_back,
        gathers=True,
        parts=4,
        side=(hidden, mlp_low),
    )
    query_raw, key_raw, value_raw, layer_out, attn_sums = attention_back(
        d_attn, attn_low, queries, key_rows, values, attended, log_totals, cos_tile, sine_tile,
        starts, middle, out_sums, first_in
    )
    attn_owned = lax.psum_scatter(attn_sums, "dp", scatter_dimension=1, tiled=True)
    mlp_grad = mlp_owned.astype(jnp.float32)
    grad_in, gain_one = exchange(
        "input_back",
        4,
        [(query_raw, attn_low, 0), (key_raw, attn_low, 1), (value_raw, attn_low, 2)],
        [inputs, d_middle, norm_gains],
        [rows_f32, gain_f32],
        finish=first_back,
        gathers=False,
        parts=4,
    )
    gain_parts = jnp.stack([jnp.sum(gain_one, axis=0), jnp.sum(gain_two, axis=0)])
    gain_grad = sum_everywhere(gain_parts.reshape(8, -1)).reshape(norm_gains.shape)
    gain_first_new, gain_second_new, gain_new = adam_update(
        norm_gains, gain_grad, gain_first, gain_second, GAIN_RATE
    )
    mlp_first_new, mlp_second_new, mlp_new = adam_update(
        mlp_weight, mlp_grad, mlp_first, mlp_second, 0.5 * D ** (-0.5)
    )
    attn_owned, mlp_new = lax.optimization_barrier((attn_owned, mlp_new))
    attn_grad = attn_owned.astype(jnp.float32)
    attn_first_new, attn_second_new, attn_new = adam_update(
        attn_weight, attn_grad, attn_first, attn_second, attn_rates()
    )
    return (
        layer_out,
        grad_in,
        gain_grad,
        attn_grad,
        mlp_grad,
        gain_first_new,
        attn_first_new,
        mlp_first_new,
        gain_second_new,
        attn_second_new,
        mlp_second_new,
        gain_new,
        attn_new,
        mlp_new,
    )


def solution(mesh):
    placed = (
        P(("dp", "tensor"), None),
        P(("dp", "tensor"), None),
        P("dp", None),
        P(),
        P(None, "dp", "tensor"),
        P(None, "dp", "tensor"),
        P(),
        P(None, "dp", "tensor"),
        P(None, "dp", "tensor"),
        P(),
        P(None, "dp", "tensor"),
        P(None, "dp", "tensor"),
    )
    return jax.shard_map(
        local,
        mesh=mesh,
        in_specs=placed,
        out_specs=(
            P(("dp", "tensor"), None),
            P(("dp", "tensor"), None),
            P(),
            P(None, "dp", "tensor"),
            P(None, "dp", "tensor"),
            P(),
            P(None, "dp", "tensor"),
            P(None, "dp", "tensor"),
            P(),
            P(None, "dp", "tensor"),
            P(None, "dp", "tensor"),
            P(),
            P(None, "dp", "tensor"),
            P(None, "dp", "tensor"),
        ),
        check_vma=False,
    )
```

```python
import functools

import jax
import jax.numpy as jnp
from jax import lax
from jax.experimental import pallas as pl
from jax.experimental.pallas import tpu as pltpu
from jax.sharding import PartitionSpec as P

D = 2048
HEAD_DIM = 64
STEP = 10


EPS_NORM = 1e-05
ROPE_BASE = 130000.0
BETA_ONE = 0.9
BETA_TWO = 0.95
EPS_ADAM = 1e-08
WEIGHT_DECAY = 0.1
GAIN_RATE = 0.3
MASKED = -1e30


def doc_layout(lengths, seq_length):
    doc_ends = jnp.cumsum(lengths)
    starts = doc_ends - lengths
    places = jnp.arange(seq_length, dtype=jnp.int32)
    segment = jnp.sum((places[:, None] >= doc_ends[None, :]).astype(jnp.int32), axis=1)
    owners = segment[:, None] == jnp.arange(lengths.shape[0], dtype=jnp.int32)[None, :]
    position = places - jnp.sum(jnp.where(owners, starts[None, :], 0), axis=1)
    return (segment, position)


def rope_tables(position):
    half_dim = HEAD_DIM // 2
    frequencies = jnp.power(
        jnp.float32(ROPE_BASE), -2.0 * jnp.arange(half_dim, dtype=jnp.float32) / HEAD_DIM
    )
    angles = position.astype(jnp.float32)[:, None] * frequencies[None, :]
    cosine, sine = jnp.cos(angles), jnp.sin(angles)
    return (
        jnp.concatenate([cosine, cosine] * 2, axis=1),
        jnp.concatenate([-sine, sine] * 2, axis=1),
    )


MESH = pl.DeviceIdType.MESH
BLOCK = 32
TILE = 256


def whole_part(count):
    return [pl.BlockSpec(memory_space=pltpu.VMEM)] * count


def mate_of():
    place = lax.axis_index("dp")
    return place + 1 - 2 * (place % 2)


def signal_mate(semaphore):
    pl.semaphore_signal(semaphore, inc=1, device_id={"dp": mate_of()}, device_id_type=MESH)


def greet(n, me, here=None):
    barrier = pltpu.get_barrier_semaphore()
    for there, step in ((me > 0, -1), (me < n - 1, 1)):

        @pl.when(there)
        def _():
            pl.semaphore_signal(barrier, inc=1, device_id={"tensor": me + step}, device_id_type=MESH)

    count = (me > 0).astype(jnp.int32) + (me < n - 1).astype(jnp.int32)
    if here is not None:
        second_core = lax.axis_index("dp") % 2
        pl.when(second_core == 0)(lambda: signal_mate(barrier))
        count = count + second_core
    pl.semaphore_wait(barrier, count)
    if here is not None:
        pl.when(second_core == 1)(lambda: signal_mate(here))


def blocks_of(count, body):
    @pl.loop(0, count // BLOCK)
    def _(block):
        body(pl.multiple_of(block * BLOCK, BLOCK))


class RowGather:
    def __init__(self, n, me, parts, place, sent, got):
        self.n, self.me, self.parts, self.place = n, me, parts, place
        self.sent, self.got = sent, got
        self.rows = place.shape[0] // n
        self.has_left, self.has_right = me > 0, me < n - 1

    def copy(self, way, part, hop, owner):
        count = self.rows // self.parts
        first = pl.multiple_of(owner * self.rows + part * count, count)
        block = self.place.at[pl.ds(first, count), :]
        slot = part * (self.n - 1) + hop
        return pltpu.make_async_remote_copy(
            src_ref=block,
            dst_ref=block,
            send_sem=self.sent.at[way, slot],
            recv_sem=self.got.at[way, slot],
            device_id={"tensor": self.me + 1 - 2 * way},
            device_id_type=MESH,
        )

    def start(self, part):
        pl.when(self.has_right)(lambda: self.copy(0, part, 0, self.me).start())
        pl.when(self.has_left)(lambda: self.copy(1, part, 0, self.me).start())

    def step(self, part, hop):
        last = hop + 1 == self.n - 1

        @pl.when(hop < self.me)
        def _():
            owner = self.me - 1 - hop
            self.copy(0, part, hop, owner).wait_recv()
            if not last:
                pl.when(self.has_right)(lambda: self.copy(0, part, hop + 1, owner).start())

        @pl.when(hop < self.n - 1 - self.me)
        def _():
            owner = self.me + 1 + hop
            self.copy(1, part, hop, owner).wait_recv()
            if not last:
                pl.when(self.has_left)(lambda: self.copy(1, part, hop + 1, owner).start())

    def drain(self):
        @pl.loop(0, self.parts)
        def _(part):
            for hop in range(self.n - 1):
                pl.when(self.has_right & (hop <= self.me))(
                    lambda: self.copy(0, part, hop, self.me - hop).wait_send()
                )
                pl.when(self.has_left & (hop <= self.n - 1 - self.me))(
                    lambda: self.copy(1, part, hop, self.me + hop).wait_send()
                )


class SumScatter:
    def __init__(self, n, me, parts, lefts, rights, totals, run, sent, got):
        self.n, self.me, self.parts = n, me, parts
        self.lefts, self.rights, self.totals, self.run = lefts, rights, totals, run
        self.sent, self.got = sent, got
        self.rows = totals.shape[1]
        self.fed = (me > 0, me < n - 1)

    def copy(self, way, part, hop):
        slot = part * (self.n - 1) + hop
        run = self.run.at[self.place(way, part, hop)]
        return pltpu.make_async_remote_copy(
            src_ref=run,
            dst_ref=run,
            send_sem=self.sent.at[way, slot],
            recv_sem=self.got.at[way, slot],
            device_id={"tensor": self.me + 1 - 2 * way},
            device_id_type=MESH,
        )

    def product(self, dest):
        first = pl.multiple_of(dest * self.rows, self.rows)

        @pl.loop(0, self.totals.shape[2] // TILE)
        def _(tile):
            columns = pl.ds(pl.multiple_of(tile * TILE, TILE), TILE)
            value = None
            for left, right in zip(self.lefts, self.rights):
                term = lax.dot_general(
                    left[pl.ds(first, self.rows), :],
                    right[columns, :],
                    (((1,), (1,)), ((), ())),
                    preferred_element_type=jnp.float32,
                )
                value = term if value is None else value + term
            self.totals[dest, :, columns] = value.astype(self.totals.dtype)

    def place(self, way, part, hop):
        return part * (self.n + 1) + (hop, self.n - hop)[way]

    def begin(self):
        part_rows = self.rows // self.parts
        for hop in range(self.n - 1):
            for way, dest in ((0, self.n - 1 - hop), (1, hop)):
                needed = (dest > self.me, dest < self.me)[way]

                @pl.when(needed & jnp.logical_not(self.fed[way]))
                def _():
                    if self.lefts:
                        self.product(dest)

                    @pl.loop(0, self.parts)
                    def _(part):
                        slot = self.place(way, part, hop)

                        def body(at):
                            first = pl.multiple_of(part * part_rows + at, BLOCK)
                            own = self.totals[dest, pl.ds(first, BLOCK), :]
                            self.run[slot, pl.ds(at, BLOCK), :] = own.astype(jnp.bfloat16)

                        blocks_of(part_rows, body)
                        self.copy(way, part, hop).start()

    def prepare(self, count):
        if count == self.n - 1:
            self.product(self.me)
        else:
            for way, hop, dest, there in self.arrivals(count):
                pl.when(there)(lambda: self.product(dest))

    def arrivals(self, count):
        for way, behind in ((0, self.me), (1, self.n - 1 - self.me)):
            hop = count - behind
            yield way, hop, (self.n - 1 - hop, hop)[way], self.fed[way] & (hop >= 0)

    def pass_on(self, part, count):
        for way, hop, dest, there in self.arrivals(count):
            run, slot = self.run, self.place(way, part, hop)
            first = part * (self.rows // self.parts)

            @pl.when(there)
            def _():
                self.copy(way, part, hop).wait_recv()

                def body(at):
                    here = pl.ds(pl.multiple_of(first + at, BLOCK), BLOCK)
                    own = self.totals[dest, here, :].astype(jnp.float32)
                    came = run[slot, pl.ds(at, BLOCK), :].astype(jnp.float32)
                    run[slot, pl.ds(at, BLOCK), :] = (own + came).astype(jnp.bfloat16)

                blocks_of(self.rows // self.parts, body)
                self.copy(way, part, hop).start()

    def last(self, part):
        first = part * (self.rows // self.parts)
        for way, hop, dest, there in self.arrivals(self.n - 1):
            run, slot = self.run, self.place(way, part, hop)

            @pl.when(there)
            def _():
                self.copy(way, part, hop).wait_recv()

                def body(at):
                    own = pl.ds(pl.multiple_of(first + at, BLOCK), BLOCK)
                    came = run[slot, pl.ds(at, BLOCK), :].astype(jnp.float32)
                    total = self.totals[self.me, own, :].astype(jnp.float32) + came
                    self.totals[self.me, own, :] = total.astype(self.totals.dtype)

                blocks_of(self.rows // self.parts, body)

    def drain(self):
        @pl.loop(0, self.parts)
        def _(part):
            for hop in range(self.n - 1):
                pl.when(self.n - 1 - hop > self.me)(lambda: self.copy(0, part, hop).wait_send())
                pl.when(hop < self.me)(lambda: self.copy(1, part, hop).wait_send())


def scatter_scratch(n, parts, rows, width):
    slots = parts * (n - 1)
    kept = jnp.float32 if n * rows * width <= 2**21 else jnp.bfloat16
    return [
        pltpu.VMEM((n, rows, width), kept),
        pltpu.VMEM((parts * (n + 1), rows // parts, width), jnp.bfloat16),
        pltpu.SemaphoreType.DMA((2, slots)),
        pltpu.SemaphoreType.DMA((2, slots)),
    ]


def gather_scratch(n, parts):
    return [pltpu.SemaphoreType.DMA((2, parts * (n - 1)))] * 2


class SideProduct:
    def __init__(self, source, columns, target, held, weight, staged, sems):
        self.source, self.columns, self.target = source, columns, target
        self.held, self.weight, self.staged, self.sems = held, weight, staged, sems
        self.count = source.shape[0] // QUERIES
        self.done = 0

    def fetch(self, block):
        return pltpu.make_async_copy(
            self.source.at[pl.ds(block * QUERIES, QUERIES), :],
            self.held.at[block % 2],
            self.sems.at[block % 2],
        )

    def store(self, block):
        return pltpu.make_async_copy(
            self.staged.at[block % 2],
            self.target.at[pl.ds(block * QUERIES, QUERIES), :],
            self.sems.at[2 + block % 2],
        )

    def fetch_weight(self):
        return pltpu.make_async_copy(self.columns.at[2], self.weight, self.sems.at[4])

    def open(self, lefts):
        self.fetch_weight().start()
        self.fetch(0).start()

    def step(self):
        block = self.done
        if block == self.count:
            return
        if block == 0:
            self.fetch_weight().wait()
        self.fetch(block).wait()
        if block + 1 < self.count:
            self.fetch(block + 1).start()
        if block >= 2:
            self.store(block - 2).wait()

        @pl.loop(0, self.weight.shape[0] // TILE)
        def _(tile):
            columns = pl.ds(pl.multiple_of(tile * TILE, TILE), TILE)
            self.staged[block % 2, :, columns] = over_lanes(
                self.held[block % 2], self.weight[columns, :]
            ).astype(jnp.bfloat16)

        self.store(block).start()
        self.done = block + 1

    def close(self):
        while self.done < self.count:
            self.step()
        for block in range(max(0, self.count - 2), self.count):
            self.store(block).wait()


def side_scratch(depth, units):
    return [
        pltpu.VMEM((2, QUERIES, units), jnp.bfloat16),
        pltpu.VMEM((depth, units), jnp.bfloat16),
        pltpu.VMEM((2, QUERIES, depth), jnp.bfloat16),
        pltpu.SemaphoreType.DMA((5,)),
    ]


def line_kernel(n, parts, products, extras, outs, gathers, side, turn_hop, finish, *refs):
    refs = list(refs)
    take = lambda count: [refs.pop(0) for _ in range(count)]
    lefts, rights, more = take(products), take(products), take(extras)
    side_in = take(2) if side else None
    results = take(outs)
    gathered = take(1)[0] if gathers else None
    filler = SideProduct(*side_in, *take(1), *[refs.pop() for _ in range(4)][::-1]) if side else None
    me = lax.axis_index("tensor")
    if products:
        totals = refs[0]
        sums = SumScatter(n, me, parts, lefts, rights, *take(4))
    if gathers:
        gather = RowGather(n, me, parts, gathered, *take(2))
    rows = totals.shape[1] if products else gathered.shape[0] // n
    part_rows = rows // parts

    def finish_part(part):
        def body(block):
            at = pl.multiple_of(part * part_rows + block, BLOCK)
            total = totals[me, pl.ds(at, BLOCK), :].astype(jnp.float32) if products else None
            sent_rows = finish(at, total, more, results)
            if gathers:
                gathered[pl.ds(pl.multiple_of(me * rows + at, BLOCK), BLOCK), :] = sent_rows

        blocks_of(part_rows, body)

    second_core = lax.axis_index("dp") % 2 == 1
    if turn_hop is None:
        greet(n, me)
    else:
        turns = take(1)[0]
        greet(n, me, turns.at[1])
    for result in results:
        if result.shape[0] == 8:
            result[...] = jnp.zeros_like(result)
    if products:
        sums.begin()
    if filler:
        filler.open(lefts)
    def complete(part):
        if products:
            sums.last(part)
        finish_part(part)
        if gathers:
            gather.start(part)

    if products:
        for count in range(1, n - 1):
            sums.prepare(count)
            pl.loop(0, parts)(lambda part: sums.pass_on(part, count))
        sums.prepare(n - 1)
        if filler:
            filler.step()
    if turn_hop is not None:
        pl.when(second_core)(lambda: pl.semaphore_wait(turns.at[0], 1))
    pl.loop(0, parts)(complete)
    if gathers:
        for hop in range(n - 1):
            if filler:
                filler.step()
            pl.loop(0, parts)(lambda part: gather.step(part, hop))
            if hop == turn_hop:

                @pl.when(jnp.logical_not(second_core))
                def _():
                    pl.semaphore_wait(turns.at[1], 1)
                    signal_mate(turns.at[0])

        gather.drain()
    if filler:
        filler.close()
    if products:
        sums.drain()


def line_exchange(
    name, collective_id, pairs, extras, outs, rows, width, finish, gathers, parts, side=(), turn_hop=None
):
    n = lax.axis_size("tensor")
    scratch = scatter_scratch(n, parts, rows, width) if pairs else []
    if gathers:
        scratch = scratch + gather_scratch(n, parts)
        outs = outs + [jax.ShapeDtypeStruct((n * rows, width), jnp.bfloat16)]
    operands = [pair[0] for pair in pairs] + [pair[1] for pair in pairs] + list(extras)
    specs = whole_part(len(operands)) + [pl.BlockSpec(memory_space=pl.ANY)] * len(side)
    own_outs = len(outs) - gathers
    out_specs = whole_part(len(outs))
    operands = operands + list(side)
    if side:
        outs = outs + [jax.ShapeDtypeStruct((side[0].shape[0], width), jnp.bfloat16)]
        out_specs = out_specs + [pl.BlockSpec(memory_space=pl.ANY)]
        scratch = scratch + side_scratch(width, side[0].shape[1])
    if turn_hop is not None:
        scratch = scratch + [pltpu.SemaphoreType.REGULAR((2,))]
    for k, (left, right, which) in enumerate(pairs):
        specs[len(pairs) + k] = pl.BlockSpec(
            (None, *right.shape[1:]), lambda i, which=which: (which, 0, 0), pipeline_mode=pl.Buffered(1)
        )
    return pl.pallas_call(
        functools.partial(
            line_kernel, n, parts, len(pairs), len(extras), own_outs, gathers, len(side) > 0, turn_hop, finish
        ),
        grid=(1,),
        out_shape=outs,
        in_specs=specs,
        out_specs=out_specs,
        scratch_shapes=scratch,
        compiler_params=pltpu.CompilerParams(
            collective_id=collective_id, has_side_effects=True, vmem_limit_bytes=60 * 2**20
        ),
        cost_estimate=pl.CostEstimate(
            flops=2 * n * rows * width, bytes_accessed=rows * width, transcendentals=0
        ),
        name=name,
    )(*operands)


def everywhere_kernel(sizes, field, result, came, sent, got):
    places = [lax.axis_index(name) for name in sizes]
    partners = []
    for name, place in zip(sizes, places):
        stride = 1
        while stride < sizes[name]:
            other = place + stride - 2 * stride * (place // stride % 2)
            partners.append({name: other})
            stride = 2 * stride
    barrier = pltpu.get_barrier_semaphore()
    for partner in partners:
        pl.semaphore_signal(barrier, inc=1, device_id=partner, device_id_type=MESH)
    pl.semaphore_wait(barrier, len(partners))
    result[...] = field[...]
    for k, partner in enumerate(partners):
        came[2 * k] = result[...]
        copy = pltpu.make_async_remote_copy(
            src_ref=came.at[2 * k],
            dst_ref=came.at[2 * k + 1],
            send_sem=sent.at[k],
            recv_sem=got.at[k],
            device_id=partner,
            device_id_type=MESH,
        )
        copy.start()
        copy.wait()
        result[...] = result[...] + came[2 * k + 1]


def sum_everywhere(field):
    sizes = {name: lax.axis_size(name) for name in ("dp", "tensor")}
    steps = sum(size.bit_length() - 1 for size in sizes.values())
    return pl.pallas_call(
        functools.partial(everywhere_kernel, sizes),
        out_shape=jax.ShapeDtypeStruct(field.shape, jnp.float32),
        in_specs=whole_part(1),
        out_specs=pl.BlockSpec(memory_space=pltpu.VMEM),
        scratch_shapes=[
            pltpu.VMEM((2 * steps, *field.shape), jnp.float32),
            pltpu.SemaphoreType.DMA((steps,)),
            pltpu.SemaphoreType.DMA((steps,)),
        ],
        compiler_params=pltpu.CompilerParams(collective_id=7, has_side_effects=True),
        name="gain_sum",
    )(field)


def inverse_scale(field):
    return lax.rsqrt(jnp.mean(field * field, axis=-1, keepdims=True) + EPS_NORM)


def first_norm(at, total, more, results):
    layer_in, gains = more
    field = layer_in[pl.ds(at, BLOCK), :].astype(jnp.float32)
    return (field * inverse_scale(field) * gains[0:1, :]).astype(jnp.bfloat16)


def norm_back(field, gradient, gain_row, gain_out):
    inv_scale = inverse_scale(field)
    normed = field * inv_scale
    scaled = gradient * gain_row
    back = inv_scale * (scaled - normed * jnp.mean(scaled * normed, axis=-1, keepdims=True))
    product = gradient * normed
    folded = product[0:8]
    for k in range(8, BLOCK, 8):
        folded = folded + product[k : k + 8]
    gain_out[...] = gain_out[...] + folded
    return back


def second_back(at, total, more, results):
    middle, cotangent, gains = more
    rows = pl.ds(at, BLOCK)
    back = norm_back(middle[rows, :], total, gains[1:2, :], results[1])
    back = back + cotangent[rows, :].astype(jnp.float32)
    results[0][rows, :] = back
    return back.astype(jnp.bfloat16)


def first_back(at, total, more, results):
    layer_in, d_middle, gains = more
    rows = pl.ds(at, BLOCK)
    back = norm_back(layer_in[rows, :].astype(jnp.float32), total, gains[0:1, :], results[1])
    results[0][rows, :] = back + d_middle[rows, :]


PAIR = 2 * HEAD_DIM
QUERIES = 256


def turned(field, cos_tile, sine_tile):
    lanes = lax.broadcasted_iota(jnp.int32, field.shape, 1)
    ahead = pltpu.roll(field, PAIR - HEAD_DIM // 2, 1)
    behind = pltpu.roll(field, HEAD_DIM // 2, 1)
    partner = jnp.where(lanes % HEAD_DIM < HEAD_DIM // 2, ahead, behind)
    return field * cos_tile + partner * sine_tile


def one_head(tile, head):
    lanes = lax.broadcasted_iota(jnp.int32, tile.shape, 1)
    return jnp.where(lanes // HEAD_DIM == head, tile, jnp.zeros_like(tile))


def over_lanes(left, right):
    return lax.dot_general(
        left, right, (((1,), (1,)), ((), ())), preferred_element_type=jnp.float32
    )


def masked(scores, starts, first_query):
    keys = lax.broadcasted_iota(jnp.int32, scores.shape, 0)
    queries = first_query + lax.broadcasted_iota(jnp.int32, scores.shape, 1)
    return jnp.where((keys >= starts) & (keys <= queries), scores, MASKED)


def attention_forward_kernel(
    n, parts, first_in, weights, cos_ref, sine_ref, starts_ref, own_rows, layer_in, gains,
    queries, key_rows, values, attended, log_totals, cot_rows, middle, second_in,
    turned_values, held, held_sems, cot_sent, cot_got, rows_sent, rows_got, turns, totals, run,
    sums_sent, sums_got
):
    me = lax.axis_index("tensor")
    second_core = lax.axis_index("dp") % 2 == 1
    rows = own_rows.shape[0]
    part_rows = rows // parts
    length, width = queries.shape

    def fetch(block):
        return pltpu.make_async_copy(
            first_in.at[pl.ds(block * QUERIES, QUERIES), :], held.at[block % 2], held_sems.at[block % 2]
        )

    fetch(0).start()
    greet(n, me)
    cot_gather = RowGather(n, me, 1, cot_rows, cot_sent, cot_got)
    gather = RowGather(n, me, parts, second_in, rows_sent, rows_got)
    sums = SumScatter(
        n, me, parts, [attended], [weights.at[3]], totals, run, sums_sent, sums_got
    )

    def place_own(at):
        place = pl.ds(pl.multiple_of(me * rows + at, BLOCK), BLOCK)
        cot_rows[place, :] = own_rows[pl.ds(at, BLOCK), :]

    blocks_of(rows, place_own)
    cot_gather.start(0)

    for block in range(length // QUERIES):
        fetch(block).wait()
        if (block + 1) * QUERIES < length:
            fetch(block + 1).start()
        at = pl.ds(block * QUERIES, QUERIES)
        source = held[block % 2]
        cos_tile, sine_tile = cos_ref[at, :], sine_ref[at, :]
        for which, target in enumerate((queries, key_rows, values)):
            field = jnp.dot(source, weights[which], preferred_element_type=jnp.float32)
            for pair in range(width // PAIR):
                tile = field[:, pair * PAIR : (pair + 1) * PAIR]
                if which < 2:
                    tile = turned(tile, cos_tile, sine_tile)
                if which == 0:
                    tile = tile.astype(jnp.bfloat16) * HEAD_DIM ** (-0.5)
                target[at, pair * PAIR : (pair + 1) * PAIR] = tile.astype(jnp.bfloat16)

    def attend(pair):
        lanes = pl.ds(pl.multiple_of(pair * PAIR, PAIR), PAIR)
        turned_values[...] = values[:, lanes].astype(jnp.float32).T.astype(jnp.bfloat16)
        for block in range(length // QUERIES):
            at = pl.ds(block * QUERIES, QUERIES)
            reach = (block + 1) * QUERIES
            starts = starts_ref[:, at]
            both = []
            for head in range(2):
                query = one_head(queries[at, lanes], head)
                scores = masked(
                    over_lanes(key_rows[0:reach, lanes], query), starts, block * QUERIES
                )
                peak = jnp.max(scores, axis=0, keepdims=True)
                raised = jnp.exp(scores - peak)
                total = jnp.sum(raised, axis=0, keepdims=True)
                result = jnp.dot(
                    turned_values[head * HEAD_DIM : (head + 1) * HEAD_DIM, 0:reach],
                    raised.astype(jnp.bfloat16),
                    preferred_element_type=jnp.float32,
                )
                both.append(result / total)
                log_totals[2 * pair + head, :, at] = peak + jnp.log(total)
            attended[at, lanes] = jnp.concatenate(both, axis=0).T.astype(jnp.bfloat16)

    pairs = width // PAIR
    pl.loop(0, pairs - 1)(attend)
    cot_gather.step(0, 0)
    pl.loop(pairs - 1, pairs)(attend)

    @pl.when(second_core)
    def _():
        for hop in range(1, n - 1):
            cot_gather.step(0, hop)

    sums.begin()

    def finish_part(part):
        def body(block):
            at = pl.multiple_of(part * part_rows + block, BLOCK)
            here = pl.ds(at, BLOCK)
            total = totals[me, here, :].astype(jnp.float32)
            field = layer_in[here, :].astype(jnp.float32) + total
            middle[here, :] = field
            place = pl.ds(pl.multiple_of(me * rows + at, BLOCK), BLOCK)
            second_in[place, :] = (field * inverse_scale(field) * gains[1:2, :]).astype(jnp.bfloat16)

        blocks_of(part_rows, body)

    def complete(part):
        sums.last(part)
        finish_part(part)
        gather.start(part)

    for count in range(1, n - 1):
        sums.prepare(count)
        pl.loop(0, parts)(lambda part: sums.pass_on(part, count))
        if count < n - 2:
            pl.when(jnp.logical_not(second_core))(lambda: cot_gather.step(0, count))
    sums.prepare(n - 1)
    pl.loop(0, parts)(complete)

    pl.when(jnp.logical_not(second_core))(lambda: cot_gather.step(0, n - 2))

    for hop in range(n - 1):
        pl.loop(0, parts)(lambda part: gather.step(part, hop))
    cot_gather.drain()
    gather.drain()
    sums.drain()


def attention_forward(first_in, weights, cos_tile, sine_tile, starts, own_rows, layer_in, gains):
    n = lax.axis_size("tensor")
    parts = 4
    length, depth = first_in.shape
    rows, width = own_rows.shape[0], weights.shape[2]
    narrow = jax.ShapeDtypeStruct((length, width), jnp.bfloat16)
    wide = jax.ShapeDtypeStruct((length, depth), jnp.bfloat16)
    outs = [
        narrow,
        narrow,
        narrow,
        narrow,
        jax.ShapeDtypeStruct((width // HEAD_DIM, 1, length), jnp.float32),
        wide,
        jax.ShapeDtypeStruct((rows, depth), jnp.float32),
        wide,
    ]
    specs = whole_part(8)
    specs[0] = pl.BlockSpec(memory_space=pl.ANY)
    return pl.pallas_call(
        functools.partial(attention_forward_kernel, n, parts),
        out_shape=outs,
        in_specs=specs,
        out_specs=whole_part(len(outs)),
        scratch_shapes=[
            pltpu.VMEM((PAIR, length), jnp.bfloat16),
            pltpu.VMEM((2, QUERIES, depth), jnp.bfloat16),
            pltpu.SemaphoreType.DMA((2,)),
        ]
        + gather_scratch(n, 1)
        + gather_scratch(n, parts)
        + [pltpu.SemaphoreType.REGULAR((2,))]
        + scatter_scratch(n, parts, rows, depth),
        compiler_params=pltpu.CompilerParams(
            collective_id=5, has_side_effects=True, vmem_limit_bytes=60 * 2**20
        ),
        cost_estimate=pl.CostEstimate(
            flops=8 * length * depth * width, bytes_accessed=400 * 2**20, transcendentals=0
        ),
        name="attention_forward",
    )(first_in, weights, cos_tile, sine_tile, starts, own_rows, layer_in, gains)


def attention_back_kernel(
    n, d_attn, out_weight, queries, key_rows, values, attended, log_totals, cos_ref, sine_ref,
    starts_ref, middle, out_sums, first_in, query_raw, key_raw, value_raw, layer_out, grads,
    d_attended, turned_keys, key_sum, value_sum, held, held_sems, turned_rows, staged, staged_sems,
    totals, run, sent, got
):
    me = lax.axis_index("tensor")
    length, width = queries.shape
    parts = 4
    sums = SumScatter(n, me, parts, [], [], totals, run, sent, got)

    blocks = length // QUERIES

    def fetch(block):
        source = d_attn if block < blocks else first_in
        return pltpu.make_async_copy(
            source.at[pl.ds(block % blocks * QUERIES, QUERIES), :],
            held.at[block % 2],
            held_sems.at[block % 2],
        )

    def store(which):
        return pltpu.make_async_copy(
            staged.at[which % 2], grads.at[which], staged_sems.at[which % 2]
        )

    def weight_grad(which, right):
        @pl.loop(0, turned_rows.shape[0] // 512)
        def _(block):
            at = pl.ds(pl.multiple_of(block * 512, 512), 512)
            staged[which % 2, at, :] = jnp.dot(
                turned_rows[at, :], right[...], preferred_element_type=jnp.float32
            ).astype(jnp.bfloat16)

        store(which).start()

    ready = pltpu.make_async_copy(out_sums, totals, held_sems.at[2])
    ready.start()
    fetch(0).start()
    greet(n, me)
    ready.wait()
    sums.begin()
    for block in range(2 * blocks):
        fetch(block).wait()
        if block + 1 < 2 * blocks:
            fetch(block + 1).start()
        here = slice(block % blocks * QUERIES, (block % blocks + 1) * QUERIES)
        source = held[block % 2]
        if block < blocks:
            d_attended[here, :] = jnp.dot(
                source, out_weight[0], preferred_element_type=jnp.float32
            ).astype(jnp.bfloat16)
        for k in range(source.shape[1] // TILE):
            columns = slice(k * TILE, (k + 1) * TILE)
            turned_rows[columns, here] = source[:, columns].astype(jnp.float32).T.astype(jnp.bfloat16)
        if block + 1 == blocks:
            weight_grad(3, attended)

    def back_pair(pair):
        lanes = pl.ds(pl.multiple_of(pair * PAIR, PAIR), PAIR)
        turned_keys[...] = key_rows[:, lanes].astype(jnp.float32).T.astype(jnp.bfloat16)
        key_sum[...] = jnp.zeros_like(key_sum)
        value_sum[...] = jnp.zeros_like(value_sum)
        for block in range(length // QUERIES):
            at = pl.ds(block * QUERIES, QUERIES)
            reach = (block + 1) * QUERIES
            starts = starts_ref[:, at]
            grads = d_attended[at, lanes]
            shares = (grads.astype(jnp.float32) * attended[at, lanes].astype(jnp.float32)).T
            both = []
            for head in range(2):
                heads = slice(head * HEAD_DIM, (head + 1) * HEAD_DIM)
                query = one_head(queries[at, lanes], head)
                grad = one_head(grads, head)
                share = jnp.sum(shares[heads], axis=0, keepdims=True)
                scores = masked(
                    over_lanes(key_rows[0:reach, lanes], query), starts, block * QUERIES
                )
                probs = jnp.exp(scores - log_totals[2 * pair + head, :, at])
                prob_grad = over_lanes(values[0:reach, lanes], grad)
                score_grad = (probs * (prob_grad - share)).astype(jnp.bfloat16)
                value_sum[0:reach, :] = value_sum[0:reach, :] + jnp.dot(
                    probs.astype(jnp.bfloat16), grad, preferred_element_type=jnp.float32
                )
                key_sum[0:reach, :] = key_sum[0:reach, :] + jnp.dot(
                    score_grad, query, preferred_element_type=jnp.float32
                )
                both.append(
                    jnp.dot(
                        turned_keys[heads, 0:reach], score_grad, preferred_element_type=jnp.float32
                    )
                )
            query_grad = jnp.concatenate(both, axis=0).T * HEAD_DIM ** (-0.5)
            query_raw[at, lanes] = turned(query_grad, cos_ref[at, :], -sine_ref[at, :]).astype(
                jnp.bfloat16
            )
        key_raw[:, lanes] = turned(key_sum[...], cos_ref[...], -sine_ref[...]).astype(jnp.bfloat16)
        value_raw[:, lanes] = value_sum[...].astype(jnp.bfloat16)

    pairs = width // PAIR
    pl.loop(0, pairs // 2)(back_pair)
    pl.loop(0, parts)(lambda part: sums.pass_on(part, 1))
    late = max(pairs // 2 + 1, 3 * pairs // 4)
    pl.loop(pairs // 2, late)(back_pair)
    for count in range(2, n - 1):
        pl.loop(0, parts)(lambda part: sums.pass_on(part, count))
    if late < pairs:
        pl.loop(late, pairs)(back_pair)
    weight_grad(0, query_raw)
    store(3).wait()
    weight_grad(1, key_raw)
    store(0).wait()
    weight_grad(2, value_raw)
    pl.loop(0, parts)(sums.last)

    def body(at):
        rows = pl.ds(at, BLOCK)
        total = middle[rows, :] + totals[me, rows, :].astype(jnp.float32)
        layer_out[rows, :] = total.astype(jnp.bfloat16)

    blocks_of(middle.shape[0], body)
    store(1).wait()
    store(2).wait()
    sums.drain()


def attention_back(
    d_attn, attn_low, queries, key_rows, values, attended, log_totals, cos_tile, sine_tile, starts,
    middle, out_sums, first_in
):
    n = lax.axis_size("tensor")
    length, depth = d_attn.shape
    width, rows = queries.shape[1], middle.shape[0]
    narrow = jax.ShapeDtypeStruct((length, width), jnp.bfloat16)
    specs = whole_part(13)
    specs[0] = specs[11] = specs[12] = pl.BlockSpec(memory_space=pl.ANY)
    specs[1] = pl.BlockSpec((1, depth, width), lambda i: (3, 0, 0), pipeline_mode=pl.Buffered(1))
    scratch = scatter_scratch(n, 4, rows, depth)
    scratch[0] = pltpu.VMEM((n, rows, depth), jnp.bfloat16)
    return pl.pallas_call(
        functools.partial(attention_back_kernel, n),
        grid=(1,),
        out_shape=[
            narrow,
            narrow,
            narrow,
            jax.ShapeDtypeStruct((rows, depth), jnp.bfloat16),
            jax.ShapeDtypeStruct((4, depth, width), jnp.bfloat16),
        ],
        in_specs=specs,
        out_specs=whole_part(4) + [pl.BlockSpec(memory_space=pl.ANY)],
        scratch_shapes=[
            pltpu.VMEM((length, width), jnp.bfloat16),
            pltpu.VMEM((PAIR, length), jnp.bfloat16),
            pltpu.VMEM((length, PAIR), jnp.float32),
            pltpu.VMEM((length, PAIR), jnp.float32),
            pltpu.VMEM((2, QUERIES, depth), jnp.bfloat16),
            pltpu.SemaphoreType.DMA((3,)),
            pltpu.VMEM((depth, length), jnp.bfloat16),
            pltpu.VMEM((2, depth, width), jnp.bfloat16),
            pltpu.SemaphoreType.DMA((2,)),
        ]
        + scratch,
        compiler_params=pltpu.CompilerParams(
            collective_id=6, has_side_effects=True, vmem_limit_bytes=60 * 2**20
        ),
        cost_estimate=pl.CostEstimate(
            flops=2 * length * depth, bytes_accessed=length * depth, transcendentals=0
        ),
        name="attention_back",
    )(
        d_attn, attn_low, queries, key_rows, values, attended, log_totals, cos_tile, sine_tile,
        starts, middle, out_sums.reshape(n, rows, depth), first_in
    )


def turn_into(target, source):
    @pl.loop(0, source.shape[0] // TILE)
    def _(block):
        at = pl.ds(pl.multiple_of(block * TILE, TILE), TILE)
        for k in range(source.shape[1] // TILE):
            columns = slice(k * TILE, (k + 1) * TILE)
            target[columns, at] = source[at, columns].astype(jnp.float32).T.astype(jnp.bfloat16)


def mlp_kernel(second_in, cotangent, weights, hidden, d_gate, d_up, grads, second_turned, cot_turned):
    @pl.when(pl.program_id(0) == 0)
    def _():
        turn_into(second_turned, second_in)
        turn_into(cot_turned, cotangent)

    for block in range(second_in.shape[0] // QUERIES):
        at = slice(block * QUERIES, (block + 1) * QUERIES)
        source = second_in[at, :]
        gate_proj = jnp.dot(source, weights[0], preferred_element_type=jnp.float32)
        up_proj = jnp.dot(source, weights[1], preferred_element_type=jnp.float32)
        d_hidden = jnp.dot(cotangent[at, :], weights[2], preferred_element_type=jnp.float32)
        sigmoid_gate = jax.nn.sigmoid(gate_proj)
        silu = gate_proj * sigmoid_gate
        hidden[at, :] = (silu * up_proj).astype(jnp.bfloat16)
        slope = sigmoid_gate * (1.0 + gate_proj * (1.0 - sigmoid_gate))
        d_gate[at, :] = (d_hidden * up_proj * slope).astype(jnp.bfloat16)
        d_up[at, :] = (d_hidden * silu).astype(jnp.bfloat16)
    for which, (left, right) in enumerate(
        ((second_turned, d_gate), (second_turned, d_up), (cot_turned, hidden))
    ):

        @pl.loop(0, left.shape[0] // 512)
        def _(block):
            at = pl.ds(pl.multiple_of(block * 512, 512), 512)
            grads[which, at, :] = jnp.dot(
                left[at, :], right[...], preferred_element_type=jnp.float32
            ).astype(jnp.bfloat16)


def mlp_middle(second_in, cotangent, weights):
    length, depth = second_in.shape
    units = weights.shape[2]
    tile = 256
    wide = jax.ShapeDtypeStruct((length, units), jnp.bfloat16)
    column = pl.BlockSpec((length, tile), lambda j: (0, j))
    stacked = pl.BlockSpec((3, depth, tile), lambda j: (0, 0, j))
    return pl.pallas_call(
        mlp_kernel,
        grid=(units // tile,),
        out_shape=[wide, wide, wide, jax.ShapeDtypeStruct((3, depth, units), jnp.bfloat16)],
        in_specs=whole_part(2) + [stacked],
        out_specs=[column, column, column, stacked],
        scratch_shapes=[pltpu.VMEM((depth, length), jnp.bfloat16)] * 2,
        compiler_params=pltpu.CompilerParams(vmem_limit_bytes=60 * 2**20),
        cost_estimate=pl.CostEstimate(
            flops=12 * length * depth * units, bytes_accessed=60 * 2**20, transcendentals=0
        ),
        name="mlp_middle",
    )(second_in, cotangent, weights)


def attn_rates():
    return jnp.array([1.0, 1.0, 1.0, 8.0**0.5], jnp.float32).reshape(4, 1, 1) * (0.5 * D ** (-0.5))


def adam_update(weight, gradient, moment_one, moment_two, step_rate):
    first_new = BETA_ONE * moment_one + (1.0 - BETA_ONE) * gradient
    second_new = BETA_TWO * moment_two + (1.0 - BETA_TWO) * gradient * gradient
    fix_one = 1.0 - BETA_ONE**STEP
    fix_two = 1.0 - BETA_TWO**STEP
    weight_new = weight - step_rate * (
        first_new / fix_one / (jnp.sqrt(second_new / fix_two) + EPS_ADAM) + WEIGHT_DECAY * weight
    )
    return (first_new, second_new, weight_new)


def local(
    inputs,
    cotangent,
    doc_lengths,
    norm_gains,
    attn_weight,
    mlp_weight,
    gain_first,
    attn_first,
    mlp_first,
    gain_second,
    attn_second,
    mlp_second,
):
    row_count = inputs.shape[0]
    seq_length = row_count * lax.axis_size("tensor")
    segment, position = doc_layout(doc_lengths[0], seq_length)
    cos_tile, sine_tile = rope_tables(position)
    starts = (jnp.arange(seq_length, dtype=jnp.int32) - position)[None, :]
    width = inputs.shape[1]
    rows_f32 = jax.ShapeDtypeStruct((row_count, width), jnp.float32)
    gain_f32 = jax.ShapeDtypeStruct((8, width), jnp.float32)
    exchange = functools.partial(line_exchange, rows=row_count, width=width)
    (first_in,) = exchange(
        "first_norm", 1, [], [inputs, norm_gains], [], finish=first_norm, gathers=True, parts=4,
        turn_hop=lax.axis_size("tensor") // 2 - 1,
    )
    attn_low = lax.all_gather(attn_weight.astype(jnp.bfloat16), "dp", axis=1, tiled=True)

    (
        queries, key_rows, values, attended, log_totals, grad_out, middle, second_in
    ) = attention_forward(
        first_in, attn_low, cos_tile, sine_tile, starts, cotangent, inputs, norm_gains
    )
    mlp_low = lax.all_gather(mlp_weight.astype(jnp.bfloat16), "dp", axis=1, tiled=True)
    hidden, d_gate, d_up, mlp_sums = mlp_middle(second_in, grad_out, mlp_low)

    mlp_owned = lax.psum_scatter(mlp_sums, "dp", scatter_dimension=1, tiled=True)
    d_middle, gain_two, d_attn, out_sums = exchange(
        "mlp_back",
        3,
        [(d_gate, mlp_low, 0), (d_up, mlp_low, 1)],
        [middle, cotangent, norm_gains],
        [rows_f32, gain_f32],
        finish=second_back,
        gathers=True,
        parts=4,
        side=(hidden, mlp_low),
    )
    query_raw, key_raw, value_raw, layer_out, attn_sums = attention_back(
        d_attn, attn_low, queries, key_rows, values, attended, log_totals, cos_tile, sine_tile,
        starts, middle, out_sums, first_in
    )
    attn_owned = lax.psum_scatter(attn_sums, "dp", scatter_dimension=1, tiled=True)
    mlp_grad = mlp_owned.astype(jnp.float32)
    grad_in, gain_one = exchange(
        "input_back",
        4,
        [(query_raw, attn_low, 0), (key_raw, attn_low, 1), (value_raw, attn_low, 2)],
        [inputs, d_middle, norm_gains],
        [rows_f32, gain_f32],
        finish=first_back,
        gathers=False,
        parts=4,
    )
    gain_parts = jnp.stack([jnp.sum(gain_one, axis=0), jnp.sum(gain_two, axis=0)])
    gain_grad = sum_everywhere(gain_parts.reshape(8, -1)).reshape(norm_gains.shape)
    gain_first_new, gain_second_new, gain_new = adam_update(
        norm_gains, gain_grad, gain_first, gain_second, GAIN_RATE
    )
    mlp_first_new, mlp_second_new, mlp_new = adam_update(
        mlp_weight, mlp_grad, mlp_first, mlp_second, 0.5 * D ** (-0.5)
    )
    attn_owned, mlp_new = lax.optimization_barrier((attn_owned, mlp_new))
    attn_grad = attn_owned.astype(jnp.float32)
    attn_first_new, attn_second_new, attn_new = adam_update(
        attn_weight, attn_grad, attn_first, attn_second, attn_rates()
    )
    return (
        layer_out,
        grad_in,
        gain_grad,
        attn_grad,
        mlp_grad,
        gain_first_new,
        attn_first_new,
        mlp_first_new,
        gain_second_new,
        attn_second_new,
        mlp_second_new,
        gain_new,
        attn_new,
        mlp_new,
    )


def solution(mesh):
    placed = (
        P(("dp", "tensor"), None),
        P(("dp", "tensor"), None),
        P("dp", None),
        P(),
        P(None, "dp", "tensor"),
        P(None, "dp", "tensor"),
        P(),
        P(None, "dp", "tensor"),
        P(None, "dp", "tensor"),
        P(),
        P(None, "dp", "tensor"),
        P(None, "dp", "tensor"),
    )
    return jax.shard_map(
        local,
        mesh=mesh,
        in_specs=placed,
        out_specs=(
            P(("dp", "tensor"), None),
            P(("dp", "tensor"), None),
            P(),
            P(None, "dp", "tensor"),
            P(None, "dp", "tensor"),
            P(),
            P(None, "dp", "tensor"),
            P(None, "dp", "tensor"),
            P(),
            P(None, "dp", "tensor"),
            P(None, "dp", "tensor"),
            P(),
            P(None, "dp", "tensor"),
            P(None, "dp", "tensor"),
        ),
        check_vma=False,
    )
```
